512 devices in a mesh: expert: 8 (over z), tensor: 64 (over y, x, core).
Axes of the slice: x: 4, y: 8, z: 8, core: 2. Of those that a mesh axis runs over, the one named last changes fastest.
Arguments:
- activations: bfloat16 [1024, 3072], P('expert', 'tensor'), may hold values from -6 to 6
- out_grad: bfloat16 [1024, 3072], P('expert', 'tensor'), may hold values from -6 to 6
- token_scale: float32 [1024], P('expert'), may hold values from 0.25 to 4
- route_prob: float32 [1024, 2], P('expert'), may hold values from 0.1 to 0.9
- route_ids: int32 [1024, 2], P('expert'), may hold values from 0 to 7, all different within a row; in each aligned block of 128 rows (0 to 127, 128 to 255, ...) at most 40 rows name the same one
- w_gate: bfloat16 [8, 3072, 16384], P('expert', None, 'tensor'), may hold values from -0.109375 to 0.109375
- w_up: bfloat16 [8, 3072, 16384], P('expert', None, 'tensor'), may hold values from -0.109375 to 0.109375
- w_down: bfloat16 [8, 16384, 3072], P('expert', 'tensor'), may hold values from -0.046875 to 0.046875
Outputs:
- input_grad: bfloat16 [1024, 3072], P('expert', 'tensor')
The draws below stay inside these ranges and needn't reach their ends.
Inputs may be any that keep to these rules, and one draw needn't show every extreme that they name: `route_ids`: each token names 2 different experts; within the tokens of one index of expert (aligned blocks of 128 rows) no expert is named by more than 40 tokens, a bound that some block reaches.
All inputs are finite; a program needn't handle non-finite values.
Results may differ from the reference program's by a relative error of at most 0.0055.
Values may be sent and summed in bfloat16 or wider, within the bound.
No kernel may reach another device: no remote copies, remote signals or barrier semaphores. Data moves between devices by JAX's collectives and lax.ppermute only.
A program may use at most 64 MiB of HBM per device.

```python
import math
import jax
import jax.numpy as jnp
import numpy as np
from jax import lax

D = 3072
FF = 16384
TOPK = 2
TOK_GROUP = 128
EXPERTS = 8
CAP = 40
TOKENS = 1024
N_EXPERT = 8


def block_levels(stream_key, dims, pieces, low, high):
    level, own = 1.0, jax.random.fold_in(stream_key, 6)
    for position, parts in pieces:
        steps = jnp.exp(jax.random.uniform(jax.random.fold_in(own, position), (parts,), jnp.float32, low / len(pieces), high / len(pieces)))
        level = level * jnp.repeat(steps, dims[position] // parts).reshape([-1 if axis == position else 1 for axis in range(len(dims))])
    return level


def assign_block(rng, own, number, rows, count, top, limit, skew):
    order = jax.random.permutation(rng, count)
    packed, common = shares(count, rows * top, limit, skew, True), shares(count, rows * top, limit, skew, False)
    places = jnp.arange(count)

    def named(tallies, offset_by):
        used = int((tallies > 0).sum())
        fixed = max(1, used // 4)
        passed = fixed + (places - fixed + offset_by * (used - fixed)) % max(1, count - fixed)
        return jnp.zeros((count,), jnp.int32).at[order[jnp.where(places < fixed, places, passed)]].set(jnp.asarray(tallies, jnp.int32))

    tallies = jnp.where(number % 4 == 0, named(packed, number // 4), named(common, number - number // 4 - 1))
    mixed = jax.random.permutation(jax.random.fold_in(own, 3), count)
    giver, receiver = mixed[0:count // 2 * 2:2], mixed[1:count // 2 * 2:2]
    slack = jnp.minimum(tallies[giver] - 1, limit - tallies[receiver]) // 2
    slack = jnp.where((giver == order[0]) | (receiver == order[0]) | (tallies[receiver] == 0), 0, jnp.maximum(slack, 0))
    passed = jax.random.randint(jax.random.fold_in(own, 4), (count // 2,), 0, 1 << 20) % (slack + 1)
    tallies = tallies.at[giver].add(-passed).at[receiver].add(passed)
    items = jnp.searchsorted(jnp.cumsum(tallies), jnp.arange(rows * top), side="right").astype(jnp.int32)
    grid = items.reshape(top, rows).T
    grid = grid[jax.random.permutation(jax.random.fold_in(own, 1), rows)]
    offset_by = jax.random.randint(jax.random.fold_in(own, 2), (rows, 1), 0, top)
    return jnp.take_along_axis(grid, (jnp.arange(top)[None, :] + offset_by) % top, axis=1)


def shares(amount, total, bound, lean, full):
    weights = [(1 << 20) // math.isqrt(grade ** lean) + 1 for grade in range(1, amount + 1)]
    largest = bound if full else min(bound, max(-(-total // amount), total * weights[0] // sum(weights)))
    least = 1 if total - largest >= amount - 1 else 0
    counts, spare = [largest] + [least] * (amount - 1), total - largest - least * (amount - 1)
    while spare > 0:
        candidates = [i for i in range(1, amount) if counts[i] < largest] or [i for i in range(1, amount) if counts[i] < bound]
        mass, remaining = sum([weights[i] for i in candidates]), spare
        for i in candidates:
            extra = min(bound - counts[i], max(1, remaining * weights[i] // mass), spare)
            counts[i] = counts[i] + extra
            spare = spare - extra
    return np.array(counts)


def gaussian(stream_key, extent, scale, most, shards=(), kind=jnp.bfloat16):
    array = jax.random.normal(stream_key, extent, jnp.float32) * scale
    if len(shards) > 0:
        array = block_levels(stream_key, extent, shards, -0.22, 0.18) * array
    return jnp.clip(array, min=-most, max=most).astype(kind)


def setup_inputs(seed: int = 0) -> dict:
    keys = jax.random.split(jax.random.key(seed), 9)
    activations = gaussian(keys[0], (TOKENS, D), 1.0, 6.0, ((0, 8), (1, 64)))
    out_grad = gaussian(keys[1], (TOKENS, D), 1.0, 6.0, ((0, 8), (1, 64)))
    token_scale = jnp.clip(jnp.exp(math.log(4.0) - 2.7725887 * jax.random.uniform(keys[2], (TOKENS,), jnp.float32) ** block_levels(keys[2], (TOKENS,), ((0, 8),), -0.2, 0.2)), 0.25, 4.0)
    route_prob = jnp.clip(0.1 + 0.79999997 * jax.random.uniform(keys[3], (TOKENS, TOPK), jnp.float32) ** block_levels(keys[3], (TOKENS, TOPK), ((0, 8),), -0.2, 0.2), 0.1, 0.9)
    route_ids_keys = jax.random.split(jax.random.fold_in(keys[4], 1), TOKENS // TOK_GROUP)
    route_ids_turns = jax.random.permutation(jax.random.fold_in(keys[4], 3), TOKENS // TOK_GROUP)
    route_ids = jax.vmap(lambda own, number: assign_block(jax.random.fold_in(keys[4], 2), own, number, TOK_GROUP, EXPERTS, TOPK, CAP, 2))(route_ids_keys, route_ids_turns).reshape((TOKENS, TOPK))
    w_gate = gaussian(keys[5], (EXPERTS, D, FF), D ** -0.5, 0.109375, ((0, 8), (2, 64)))
    w_up = gaussian(keys[6], (EXPERTS, D, FF), D ** -0.5, 0.109375, ((0, 8), (2, 64)))
    w_down = gaussian(keys[7], (EXPERTS, FF, D), FF ** -0.5, 0.046875, ((0, 8), (1, 64)))
    return dict(activations=activations, out_grad=out_grad, token_scale=token_scale, route_prob=route_prob, route_ids=route_ids, w_gate=w_gate, w_up=w_up, w_down=w_down)


def backward_tail(gate, upper, back):
    sigmoid_g = jax.nn.sigmoid(gate)
    slope = sigmoid_g * (1.0 + gate * (1.0 - sigmoid_g))
    d_gate = (back * upper * slope).astype(jnp.bfloat16)
    d_upper = (back * gate * sigmoid_g).astype(jnp.bfloat16)
    return d_gate, d_upper


def reference(activations, out_grad, token_scale, route_prob, route_ids, w_gate, w_up, w_down):
    labels = jnp.arange(EXPERTS, dtype=jnp.int32)
    onehot = route_ids[:, :, None] == labels[None, None, :]
    hits = jnp.sum(onehot.astype(jnp.int32), axis=1).astype(jnp.int32)
    weights = jnp.sum(route_prob[:, :, None] * onehot.astype(jnp.float32), axis=1) * token_scale[:, None]
    hits_group = hits.reshape(N_EXPERT, TOK_GROUP, EXPERTS)
    slots = (jnp.cumsum(hits_group, axis=1).astype(jnp.int32) - hits_group).astype(jnp.int32)
    places = jnp.arange(CAP, dtype=jnp.int32)
    positions = jnp.arange(TOK_GROUP, dtype=jnp.int32)
    starts = jnp.arange(N_EXPERT, dtype=jnp.int32) * TOK_GROUP
    total = jnp.zeros((TOKENS, D), jnp.float32)
    for expert in range(EXPERTS):
        match = (hits_group[:, :, expert][:, :, None] > 0) & (slots[:, :, expert][:, :, None] == places[None, None, :])
        valid = jnp.any(match, axis=1).reshape(-1)
        token_of = jnp.sum(jnp.where(match, positions[None, :, None], jnp.zeros((), jnp.int32)), axis=1).astype(jnp.int32)
        index = (starts[:, None] + token_of).reshape(-1).astype(jnp.int32)
        keep = valid[:, None]
        rows_x = jnp.where(keep, activations[index], jnp.zeros((), jnp.bfloat16))
        rows_g = jnp.where(keep, out_grad[index], jnp.zeros((), jnp.bfloat16))
        gate = jnp.dot(rows_x, w_gate[expert], preferred_element_type=jnp.float32)
        upper = jnp.dot(rows_x, w_up[expert], preferred_element_type=jnp.float32)
        back = lax.dot_general(rows_g, w_down[expert], (((1,), (1,)), ((), ())), preferred_element_type=jnp.float32)
        d_gate, d_upper = backward_tail(gate, upper, back)
        part = lax.dot_general(d_gate, w_gate[expert], (((1,), (1,)), ((), ())), preferred_element_type=jnp.float32)
        part = part + lax.dot_general(d_upper, w_up[expert], (((1,), (1,)), ((), ())), preferred_element_type=jnp.float32)
        scaled = jnp.where(keep, weights[index, expert][:, None] * part, jnp.zeros((), jnp.float32))
        total = total.at[index].add(scaled)
    return total.astype(jnp.bfloat16)
```

```python
import jax
import jax.numpy as jnp
from jax import lax
from jax.sharding import Mesh, PartitionSpec as P

BF16 = jnp.bfloat16
F32 = jnp.float32
LANES = 128
FINE = 16


def backward_tail(gate, upper, back):
    sigmoid_g = jax.nn.sigmoid(gate)
    slope = sigmoid_g * (1.0 + gate * (1.0 - sigmoid_g))
    d_gate = (back * upper * slope).astype(BF16)
    d_upper = (back * gate * sigmoid_g).astype(BF16)
    return d_gate, d_upper


def shards(activations, out_grad, token_scale, route_prob, route_ids, w_gate, w_up, w_down):
    nz, ny, nx, nc = (lax.axis_size(a) for a in ("z", "y", "x", "c"))
    core = lax.axis_index("c")
    tokens, feats = activations.shape
    capacity = min(tokens, 5 * tokens // (2 * nz))
    parts = feats // FINE
    hidden = w_gate.shape[2]
    rows = nz * capacity
    wide = feats * ny

    labels = jnp.arange(nz, dtype=jnp.int32)
    onehot = route_ids[:, :, None] == labels[None, None, :]
    hits = jnp.sum(onehot.astype(jnp.int32), axis=1)
    below = jnp.tril(jnp.ones((tokens, tokens), BF16), -1)
    slots = jnp.dot(below, hits.astype(BF16), preferred_element_type=F32).astype(jnp.int32)
    lane = jnp.arange(LANES, dtype=jnp.int32)
    lane_part = lane // capacity
    lane_slot = jnp.where(lane_part < parts, lane % capacity, -1)
    place = (slots[:, :, None] == lane_slot) & (hits[:, :, None] > 0)
    place_bf = place.astype(BF16).reshape(tokens, nz * LANES)

    def packed(values):
        spread = lax.dot_general(
            values, place_bf, (((0,), (0,)), ((), ())), preferred_element_type=F32
        ).astype(BF16)
        spread = spread.reshape(parts, FINE, nz, LANES)
        own = jnp.arange(parts)[:, None, None, None] == lane_part
        return jnp.sum(jnp.where(own, spread, 0), axis=0).transpose(1, 0, 2)

    block = jnp.concatenate([packed(activations), packed(out_grad)], axis=1)
    send = jnp.broadcast_to(block[:, None], (nz, ny) + block.shape[1:])
    send = send.reshape((nz * ny,) + block.shape[1:])
    got = lax.all_to_all(send, ("z", "y"), split_axis=0, concat_axis=0, tiled=True)

    def ordered(w):
        w = w.reshape(ny, nx, nc, parts, FINE, hidden).transpose(2, 1, 3, 0, 4, 5)
        return w.reshape(nc, nx * wide, hidden)

    w_in = jnp.concatenate([ordered(w_gate[0]), ordered(w_up[0])], axis=2)
    w_dn = ordered(w_down[0].T)
    in_own, in_other = (lax.dynamic_index_in_dim(w_in, i, 0, False) for i in (core, 1 - core))
    dn_own, dn_other = (lax.dynamic_index_in_dim(w_dn, i, 0, False) for i in (core, 1 - core))

    got = got.reshape(nz, ny, 2, FINE, LANES)[..., : parts * capacity]
    got = got.reshape(nz, ny, 2, FINE, parts, capacity).transpose(2, 0, 5, 4, 1, 3)
    mine = got.reshape(2 * rows, wide)

    copies = jnp.broadcast_to(mine[None], (nx,) + mine.shape)
    own = lax.all_to_all(copies, "x", split_axis=0, concat_axis=0, tiled=True)
    other = lax.ppermute(own, "c", [(0, 1), (1, 0)])

    def forward(block, w_a, w_b):
        total_a, total_b = 0.0, 0.0
        for i in range(nx):
            k = slice(i * wide, (i + 1) * wide)
            total_a += jnp.dot(block[i, :rows], w_a[k], preferred_element_type=F32)
            total_b += jnp.dot(block[i, rows:], w_b[k], preferred_element_type=F32)
        return total_a, total_b

    in_a, back_a = forward(own, in_own, dn_own)
    in_b, back_b = forward(other, in_other, dn_other)
    both = in_a + in_b
    d_gate, d_upper = backward_tail(both[:, :hidden], both[:, hidden:], back_a + back_b)
    d_both = jnp.concatenate([d_gate, d_upper], axis=1)

    def returned(w):
        return lax.dot_general(d_both, w, (((1,), (1,)), ((), ())), preferred_element_type=F32)

    from_other = lax.ppermute(returned(in_other).astype(BF16), "c", [(0, 1), (1, 0)])
    part = (returned(in_own) + from_other.astype(F32)).astype(BF16)
    part = part.reshape(rows, nx, wide).transpose(1, 0, 2)
    part = lax.all_to_all(part, "x", split_axis=0, concat_axis=0, tiled=True)
    part = jnp.sum(part.astype(F32), axis=0).astype(BF16)

    part = part.reshape(nz, capacity, parts, ny, FINE).transpose(0, 3, 4, 2, 1)
    part = part.reshape(nz * ny, FINE, parts * capacity)
    part = jnp.pad(part, ((0, 0), (0, 0), (0, LANES - parts * capacity)))
    part = lax.all_to_all(part, ("z", "y"), split_axis=0, concat_axis=0, tiled=True)
    part = jnp.sum(part.reshape(nz, ny, FINE, LANES).astype(F32), axis=1)

    weights = (
        jnp.sum(route_prob[:, :, None] * onehot.astype(F32), axis=1) * token_scale[:, None]
    )
    combine = jnp.where(place, weights[:, :, None], 0.0).reshape(tokens, nz * LANES)
    own_part = jnp.arange(parts)[:, None, None, None] == lane_part
    spread = jnp.where(own_part, part.transpose(1, 0, 2)[None], 0.0)
    spread = spread.reshape(feats, nz * LANES)
    result = lax.dot_general(
        combine,
        spread,
        (((1,), (1,)), ((), ())),
        precision=lax.Precision.HIGHEST,
        preferred_element_type=F32,
    )
    return result.astype(BF16)


def solution(mesh):
    devices = mesh.devices
    fine = Mesh(devices.reshape(devices.shape[0], 8, 4, 2), ("z", "y", "x", "c"))
    tensor = ("y", "x", "c")
    placed = (
        P("z", tensor),
        P("z", tensor),
        P("z"),
        P("z", None),
        P("z", None),
        P("z", None, tensor),
        P("z", None, tensor),
        P("z", tensor, None),
    )
    return jax.shard_map(
        shards, mesh=fine, in_specs=placed, out_specs=P("z", tensor), check_vma=False
    )
```

```python
import functools
import math

import jax
import jax.numpy as jnp
from jax import lax
from jax.experimental import pallas as pl
from jax.experimental.pallas import tpu as pltpu
from jax.sharding import Mesh, PartitionSpec as P

BF16 = jnp.bfloat16
F32 = jnp.float32
LANES = 128
FINE = 16


def backward_tail(gate, upper, back):
    sigmoid_g = jax.nn.sigmoid(gate)
    slope = sigmoid_g * (1.0 + gate * (1.0 - sigmoid_g))
    d_gate = (back * upper * slope).astype(BF16)
    d_upper = (back * gate * sigmoid_g).astype(BF16)
    return d_gate, d_upper


def lane_layout(shape, capacity, parts):
    lane = lax.broadcasted_iota(jnp.int32, shape, 1)
    expert = lane // LANES
    inner = lane - expert * LANES
    part = inner // capacity
    slot = jnp.where(part < parts, inner - part * capacity, -1)
    return expert, part, slot


def placement(ids_ref, tokens, lanes, capacity, parts):
    expert, _, slot = lane_layout((tokens, lanes), capacity, parts)
    first = ids_ref[:, 0:1] == expert
    second = ids_ref[:, 1:2] == expert
    hit = first | second
    row = lax.broadcasted_iota(jnp.int32, (tokens, tokens), 0)
    col = lax.broadcasted_iota(jnp.int32, (tokens, tokens), 1)
    below = jnp.where(col < row, 1.0, 0.0).astype(BF16)
    hit_bf = jnp.where(hit, 1.0, 0.0).astype(BF16)
    before = jnp.dot(below, hit_bf, preferred_element_type=F32)
    return hit & (before == slot.astype(F32)), first, second


def pack_kernel(capacity, ids_ref, x_ref, g_ref, out_ref):
    nz, ny = out_ref.shape[:2]
    tokens, feats = x_ref.shape
    parts = feats // FINE
    lanes = nz * LANES
    place, _, _ = placement(ids_ref, tokens, lanes, capacity, parts)
    place = jnp.where(place, 1.0, 0.0).astype(BF16)
    _, part, _ = lane_layout((FINE, lanes), capacity, parts)
    for kind, ref in enumerate((x_ref, g_ref)):
        spread = lax.dot_general(
            ref[...], place, (((0,), (0,)), ((), ())), preferred_element_type=F32
        )
        block = jnp.zeros((FINE, lanes), F32)
        for p in range(parts):
            block = jnp.where(part == p, spread[p * FINE : (p + 1) * FINE], block)
        block = block.astype(BF16)
        for z in range(nz):
            for y in range(ny):
                out_ref[z, y, kind * FINE : (kind + 1) * FINE, :] = block[
                    :, z * LANES : (z + 1) * LANES
                ]


def unpack_kernel(capacity, parts, ny, in_ref, out_ref):
    nx, _, wide = out_ref.shape
    nz = in_ref.shape[0] // ny
    span = wide // parts
    rows = nz * capacity
    for kind in range(2):
        for pair in range(0, nz, 2):
            turned = []
            for z in (pair, pair + 1):
                block = in_ref[z * ny : (z + 1) * ny, kind * FINE : (kind + 1) * FINE, :]
                turned.append(block.reshape(span, LANES).astype(F32).T)
            start = kind * rows + pair * capacity
            for p in range(parts):
                piece = jnp.concatenate(
                    [t[p * capacity : (p + 1) * capacity] for t in turned], axis=0
                ).astype(BF16)
                for i in range(nx):
                    out_ref[i, start : start + 2 * capacity, p * span : (p + 1) * span] = piece


def repack_kernel(capacity, parts, ny, in_ref, out_ref):
    nx, rows, wide = in_ref.shape
    span = wide // parts
    for pair in range(0, rows // capacity, 2):
        here = slice(pair * capacity, (pair + 2) * capacity)
        total = in_ref[0, here, :].astype(F32)
        for i in range(1, nx):
            total += in_ref[i, here, :].astype(F32)
        for half in range(2):
            block = total[half * capacity : (half + 1) * capacity]
            pieces = [block[:, p * span : (p + 1) * span] for p in range(parts)]
            pieces.append(jnp.zeros((LANES - parts * capacity, span), F32))
            turned = jnp.concatenate(pieces, axis=0).T.astype(BF16)
            z = pair + half
            out_ref[z * ny : (z + 1) * ny] = turned.reshape(ny, FINE, LANES)


def combine_kernel(capacity, parts, ids_ref, prob_ref, scale_ref, out_ref):
    tokens, lanes = out_ref.shape
    place, first, _ = placement(ids_ref, tokens, lanes, capacity, parts)
    prob = jnp.where(first, prob_ref[:, 0:1], prob_ref[:, 1:2])
    out_ref[...] = jnp.where(place, prob * scale_ref[...], 0.0)


def final_kernel(capacity, parts, ny, combine_ref, in_ref, out_ref):
    lanes = combine_ref.shape[1]
    nz = lanes // LANES
    sums = []
    for z in range(nz):
        total = in_ref[z * ny].astype(F32)
        for y in range(1, ny):
            total += in_ref[z * ny + y].astype(F32)
        sums.append(total)
    sums = jnp.concatenate(sums, axis=1)
    _, part, _ = lane_layout(sums.shape, capacity, parts)
    spread = jnp.concatenate([jnp.where(part == p, sums, 0.0) for p in range(parts)], axis=0)
    out_ref[...] = lax.dot_general(
        combine_ref[...],
        spread,
        (((1,), (1,)), ((), ())),
        precision=lax.Precision.HIGHEST,
        preferred_element_type=F32,
    ).astype(out_ref.dtype)


def call(kernel, shape, dtype, *operands, flops=0):
    moved = sum(o.size * o.dtype.itemsize for o in operands)
    moved += math.prod(shape) * jnp.dtype(dtype).itemsize
    return pl.pallas_call(
        kernel,
        out_shape=jax.ShapeDtypeStruct(shape, dtype),
        in_specs=[pl.BlockSpec(memory_space=pltpu.VMEM)] * len(operands),
        out_specs=pl.BlockSpec(memory_space=pltpu.VMEM),
        compiler_params=pltpu.CompilerParams(vmem_limit_bytes=32 * 1024 * 1024),
        cost_estimate=pl.CostEstimate(flops=flops, bytes_accessed=moved, transcendentals=0),
    )(*operands)


def shards(activations, out_grad, token_scale, route_prob, route_ids, w_gate, w_up, w_down):
    nz, ny, nx, nc = (lax.axis_size(a) for a in ("z", "y", "x", "c"))
    core = lax.axis_index("c")
    tokens, feats = activations.shape
    capacity = min(tokens, 5 * tokens // (2 * nz))
    parts = feats // FINE
    hidden = w_gate.shape[2]
    rows = nz * capacity
    wide = feats * ny

    send = call(
        functools.partial(pack_kernel, capacity),
        (nz, ny, 2 * FINE, LANES),
        BF16,
        route_ids,
        activations,
        out_grad,
    )
    send = send.reshape(nz * ny, 2 * FINE, LANES)
    got = lax.all_to_all(send, ("z", "y"), split_axis=0, concat_axis=0, tiled=True)

    def ordered(w):
        w = w.reshape(ny, nx, nc, parts, FINE, hidden).transpose(2, 1, 3, 0, 4, 5)
        return w.reshape(nc, nx * wide, hidden)

    w_in = jnp.concatenate([ordered(w_gate[0]), ordered(w_up[0])], axis=2)
    w_dn = ordered(w_down[0].T)
    in_own, in_other = (lax.dynamic_index_in_dim(w_in, i, 0, False) for i in (core, 1 - core))
    dn_own, dn_other = (lax.dynamic_index_in_dim(w_dn, i, 0, False) for i in (core, 1 - core))
    got, in_own, in_other, dn_own, dn_other = lax.optimization_barrier(
        (got, in_own, in_other, dn_own, dn_other)
    )

    copies = call(
        functools.partial(unpack_kernel, capacity, parts, ny), (nx, 2 * rows, wide), BF16, got
    )
    own = lax.all_to_all(copies, "x", split_axis=0, concat_axis=0, tiled=True)
    other = lax.ppermute(own, "c", [(0, 1), (1, 0)])

    def forward(block, w_a, w_b):
        total_a, total_b = 0.0, 0.0
        for i in range(nx):
            k = slice(i * wide, (i + 1) * wide)
            total_a += jnp.dot(block[i, :rows], w_a[k], preferred_element_type=F32)
            total_b += jnp.dot(block[i, rows:], w_b[k], preferred_element_type=F32)
        return total_a, total_b

    in_a, back_a = forward(own, in_own, dn_own)
    in_b, back_b = forward(other, in_other, dn_other)
    both = in_a + in_b
    d_gate, d_upper = backward_tail(both[:, :hidden], both[:, hidden:], back_a + back_b)
    d_both = jnp.concatenate([d_gate, d_upper], axis=1)

    def returned(w):
        return lax.dot_general(d_both, w, (((1,), (1,)), ((), ())), preferred_element_type=F32)

    from_other = lax.ppermute(returned(in_other).astype(BF16), "c", [(0, 1), (1, 0)])
    part = (returned(in_own) + from_other.astype(F32)).astype(BF16)
    part = part.reshape(rows, nx, wide).transpose(1, 0, 2)
    part = lax.all_to_all(part, "x", split_axis=0, concat_axis=0, tiled=True)

    part = call(
        functools.partial(repack_kernel, capacity, parts, ny), (nz * ny, FINE, LANES), BF16, part
    )
    part = lax.all_to_all(part, ("z", "y"), split_axis=0, concat_axis=0, tiled=True)
    combine = call(
        functools.partial(combine_kernel, capacity, parts),
        (tokens, nz * LANES),
        F32,
        route_ids,
        route_prob,
        token_scale.reshape(tokens, 1),
    )
    return call(
        functools.partial(final_kernel, capacity, parts, ny), (tokens, feats), BF16, combine, part
    )


def solution(mesh):
    devices = mesh.devices
    fine = Mesh(devices.reshape(devices.shape[0], 8, 4, 2), ("z", "y", "x", "c"))
    tensor = ("y", "x", "c")
    placed = (
        P("z", tensor),
        P("z", tensor),
        P("z"),
        P("z", None),
        P("z", None),
        P("z", None, tensor),
        P("z", None, tensor),
        P("z", tensor, None),
    )
    return jax.shard_map(
        shards, mesh=fine, in_specs=placed, out_specs=P("z", tensor), check_vma=False
    )
```

```python
import functools
import math

import jax
import jax.numpy as jnp
from jax import lax
from jax.experimental import pallas as pl
from jax.experimental.pallas import tpu as pltpu
from jax.sharding import Mesh, PartitionSpec as P

BF16 = jnp.bfloat16
F32 = jnp.float32
LANES = 128
FINE = 16
AXES = ("z", "y", "x", "c")


def backward_tail(gate, upper, back):
    sigmoid_g = jax.nn.sigmoid(gate)
    slope = sigmoid_g * (1.0 + gate * (1.0 - sigmoid_g))
    d_gate = (back * upper * slope).astype(BF16)
    d_upper = (back * gate * sigmoid_g).astype(BF16)
    return d_gate, d_upper


def lane_layout(shape, axis, capacity, parts):
    lane = lax.broadcasted_iota(jnp.int32, shape, axis)
    expert = lane // LANES
    inner = lane - expert * LANES
    part = inner // capacity
    slot = jnp.where(part < parts, inner - part * capacity, -1)
    return expert, part, slot


def placement(ids_ref, lanes, capacity, parts):
    tokens = ids_ref.shape[1]
    expert, _, slot = lane_layout((lanes, tokens), 0, capacity, parts)
    first = ids_ref[0:1, :] == expert
    second = ids_ref[1:2, :] == expert
    hit = first | second
    row = lax.broadcasted_iota(jnp.int32, (tokens, tokens), 0)
    col = lax.broadcasted_iota(jnp.int32, (tokens, tokens), 1)
    earlier = jnp.where(row < col, 1.0, 0.0).astype(BF16)
    hit_bf = jnp.where(hit, 1.0, 0.0).astype(BF16)
    before = jnp.dot(hit_bf, earlier, preferred_element_type=F32)
    return hit & (before == slot.astype(F32)), first


def pack_kernel(capacity, ids_ref, x_ref, g_ref, out_ref):
    nz, ny = out_ref.shape[:2]
    feats = x_ref.shape[0]
    parts = feats // FINE
    lanes = nz * LANES
    place, _ = placement(ids_ref, lanes, capacity, parts)
    place = jnp.where(place, 1.0, 0.0).astype(BF16)
    _, part, _ = lane_layout((FINE, lanes), 1, capacity, parts)
    for kind, ref in enumerate((x_ref, g_ref)):
        spread = lax.dot_general(
            ref[...], place, (((1,), (1,)), ((), ())), preferred_element_type=F32
        )
        block = jnp.zeros((FINE, lanes), F32)
        for p in range(parts):
            block = jnp.where(part == p, spread[p * FINE : (p + 1) * FINE], block)
        block = block.astype(BF16)
        for z in range(nz):
            for y in range(ny):
                out_ref[z, y, kind * FINE : (kind + 1) * FINE, :] = block[
                    :, z * LANES : (z + 1) * LANES
                ]


def unpack_kernel(capacity, parts, ny, in_ref, out_ref):
    nx, _, wide = out_ref.shape
    nz = in_ref.shape[0] // ny
    span = wide // parts
    rows = nz * capacity
    for kind in range(2):
        for pair in range(0, nz, 2):
            turned = []
            for z in (pair, pair + 1):
                block = in_ref[z * ny : (z + 1) * ny, kind * FINE : (kind + 1) * FINE, :]
                turned.append(block.reshape(span, LANES).astype(F32).T)
            start = kind * rows + pair * capacity
            for p in range(parts):
                piece = jnp.concatenate(
                    [t[p * capacity : (p + 1) * capacity] for t in turned], axis=0
                ).astype(BF16)
                for i in range(nx):
                    out_ref[i, start : start + 2 * capacity, p * span : (p + 1) * span] = piece


def repack_kernel(capacity, parts, ny, in_ref, out_ref):
    nx, rows, wide = in_ref.shape
    span = wide // parts
    for pair in range(0, rows // capacity, 2):
        here = slice(pair * capacity, (pair + 2) * capacity)
        total = in_ref[0, here, :].astype(F32)
        for i in range(1, nx):
            total += in_ref[i, here, :].astype(F32)
        for half in range(2):
            block = total[half * capacity : (half + 1) * capacity]
            pieces = [block[:, p * span : (p + 1) * span] for p in range(parts)]
            pieces.append(jnp.zeros((LANES - parts * capacity, span), F32))
            turned = jnp.concatenate(pieces, axis=0).T.astype(BF16)
            z = pair + half
            out_ref[z * ny : (z + 1) * ny] = turned.reshape(ny, FINE, LANES)


def combine_kernel(capacity, parts, ids_ref, prob_ref, scale_ref, out_ref):
    lanes = out_ref.shape[0]
    place, first = placement(ids_ref, lanes, capacity, parts)
    prob = jnp.where(first, prob_ref[0:1, :], prob_ref[1:2, :])
    out_ref[...] = jnp.where(place, prob * scale_ref[...], 0.0)


def final_kernel(capacity, parts, ny, combine_ref, in_ref, out_ref):
    lanes = combine_ref.shape[0]
    nz = lanes // LANES
    sums = []
    for z in range(nz):
        total = in_ref[z * ny].astype(F32)
        for y in range(1, ny):
            total += in_ref[z * ny + y].astype(F32)
        sums.append(total)
    sums = jnp.concatenate(sums, axis=1)
    _, part, _ = lane_layout(sums.shape, 1, capacity, parts)
    spread = jnp.concatenate([jnp.where(part == p, sums, 0.0) for p in range(parts)], axis=0)
    out_ref[...] = lax.dot_general(
        spread,
        combine_ref[...],
        (((1,), (0,)), ((), ())),
        precision=lax.Precision.HIGHEST,
        preferred_element_type=F32,
    ).astype(out_ref.dtype)


def call(kernel, shape, dtype, *operands, flops=0):
    moved = sum(o.size * o.dtype.itemsize for o in operands)
    moved += math.prod(shape) * jnp.dtype(dtype).itemsize
    return pl.pallas_call(
        kernel,
        out_shape=jax.ShapeDtypeStruct(shape, dtype),
        in_specs=[pl.BlockSpec(memory_space=pltpu.VMEM)] * len(operands),
        out_specs=pl.BlockSpec(memory_space=pltpu.VMEM),
        compiler_params=pltpu.CompilerParams(vmem_limit_bytes=32 * 1024 * 1024),
        cost_estimate=pl.CostEstimate(flops=flops, bytes_accessed=moved, transcendentals=0),
    )(*operands)


def exchange_groups(nz, ny, nx, nc):
    def index(z, y, x, c):
        return ((z * ny + y % ny) * nx + x % nx) * nc + c

    halves = [(yb, xb) for yb in range(2) for xb in range(2)]
    places = [(2 * ya, 2 * xa) for ya in range(ny // 2) for xa in range(nx // 2)]
    far = [
        [index(z, y + yb, x + xb, c) for z in range(nz) for y, x in places]
        for c in range(nc)
        for yb, xb in halves
    ]
    near = [
        [index(z, y + c + (yb + c) % 2, x + c + (xb + c) % 2, c) for yb, xb in halves]
        for z in range(nz)
        for c in range(nc)
        for y, x in places
    ]
    return far, near


def swap(blocks, groups):
    return lax.all_to_all(
        blocks, AXES, split_axis=0, concat_axis=0, axis_index_groups=groups, tiled=True
    )


def shards(activations, out_grad, token_scale, route_prob, route_ids, w_gate, w_up, w_down):
    nz, ny, nx, nc = (lax.axis_size(a) for a in AXES)
    far, near = exchange_groups(nz, ny, nx, nc)
    spread = ny * nx // 4
    members = 4
    core = lax.axis_index("c")
    tokens, feats = activations.shape
    capacity = min(tokens, 5 * tokens // (2 * nz))
    parts = feats // FINE
    hidden = w_gate.shape[2]
    rows = nz * capacity
    wide = feats * spread

    send = call(
        functools.partial(pack_kernel, capacity),
        (nz, spread, 2 * FINE, LANES),
        BF16,
        route_ids.T,
        activations.T,
        out_grad.T,
    )
    got = swap(send.reshape(nz * spread, 2 * FINE, LANES), far)

    def ordered(w):
        w = w.reshape(ny // 2, 2, nx // 2, 2, nc, parts, FINE, hidden)
        return w.transpose(4, 1, 3, 5, 0, 2, 6, 7).reshape(nc, members * wide, hidden)

    w_in = jnp.concatenate([ordered(w_gate[0]), ordered(w_up[0])], axis=2)
    w_dn = ordered(w_down[0].T)
    in_own, in_other = (lax.dynamic_index_in_dim(w_in, i, 0, False) for i in (core, 1 - core))
    dn_own, dn_other = (lax.dynamic_index_in_dim(w_dn, i, 0, False) for i in (core, 1 - core))
    got, in_own, in_other, dn_own, dn_other = lax.optimization_barrier(
        (got, in_own, in_other, dn_own, dn_other)
    )

    copies = call(
        functools.partial(unpack_kernel, capacity, parts, spread),
        (members, 2 * rows, wide),
        BF16,
        got,
    )
    own = swap(copies, near)
    other = lax.ppermute(own, "c", [(0, 1), (1, 0)])

    def forward(block, w_a, w_b):
        total_a, total_b = 0.0, 0.0
        for i in range(members):
            k = slice(i * wide, (i + 1) * wide)
            total_a += jnp.dot(block[i, :rows], w_a[k], preferred_element_type=F32)
            total_b += jnp.dot(block[i, rows:], w_b[k], preferred_element_type=F32)
        return total_a, total_b

    in_a, back_a = forward(own, in_own, dn_own)
    in_b, back_b = forward(other, in_other, dn_other)
    both = in_a + in_b
    d_gate, d_upper = backward_tail(both[:, :hidden], both[:, hidden:], back_a + back_b)
    d_both = jnp.concatenate([d_gate, d_upper], axis=1)

    def returned(w):
        return lax.dot_general(d_both, w, (((1,), (1,)), ((), ())), preferred_element_type=F32)

    from_other = lax.ppermute(returned(in_other).astype(BF16), "c", [(0, 1), (1, 0)])
    part = (returned(in_own) + from_other.astype(F32)).astype(BF16)
    part = swap(part.reshape(rows, members, wide).transpose(1, 0, 2), near)
    part = call(
        functools.partial(repack_kernel, capacity, parts, spread),
        (nz * spread, FINE, LANES),
        BF16,
        part,
    )
    part = swap(part, far)
    combine = call(
        functools.partial(combine_kernel, capacity, parts),
        (nz * LANES, tokens),
        F32,
        route_ids.T,
        route_prob.T,
        token_scale.reshape(1, tokens),
    )
    return call(
        functools.partial(final_kernel, capacity, parts, spread),
        (feats, tokens),
        BF16,
        combine,
        part,
    ).T


def solution(mesh):
    devices = mesh.devices
    fine = Mesh(devices.reshape(devices.shape[0], 8, 4, 2), AXES)
    tensor = ("y", "x", "c")
    placed = (
        P("z", tensor),
        P("z", tensor),
        P("z"),
        P("z", None),
        P("z", None),
        P("z", None, tensor),
        P("z", None, tensor),
        P("z", tensor, None),
    )
    return jax.shard_map(
        shards, mesh=fine, in_specs=placed, out_specs=P("z", tensor), check_vma=False
    )
```

```python
import functools
import math

import jax
import jax.numpy as jnp
from jax import lax
from jax.experimental import pallas as pl
from jax.experimental.pallas import tpu as pltpu
from jax.sharding import Mesh, PartitionSpec as P

BF16 = jnp.bfloat16
F32 = jnp.float32
LANES = 128
FINE = 16
AXES = ("z", "y", "x", "c")


def backward_tail(gate, upper, back):
    sigmoid_g = jax.nn.sigmoid(gate)
    slope = sigmoid_g * (1.0 + gate * (1.0 - sigmoid_g))
    d_gate = (back * upper * slope).astype(BF16)
    d_upper = (back * gate * sigmoid_g).astype(BF16)
    return d_gate, d_upper


def lane_parts(shape, axis, capacity):
    inner = lax.broadcasted_iota(jnp.int32, shape, axis) % LANES
    return inner // capacity


def lane_slots(tokens, capacity, parts):
    inner = lax.broadcasted_iota(jnp.int32, (LANES, tokens), 0)
    part = inner // capacity
    return jnp.where(part < parts, inner - part * capacity, -1).astype(F32)


def token_slots(ids, experts):
    tokens = ids.shape[1]
    expert = lax.broadcasted_iota(jnp.int32, (experts, tokens), 0)
    first = ids[0:1, :] == expert
    hit = first | (ids[1:2, :] == expert)
    row = lax.broadcasted_iota(jnp.int32, (tokens, tokens), 0)
    col = lax.broadcasted_iota(jnp.int32, (tokens, tokens), 1)
    earlier = jnp.where(row < col, 1.0, 0.0).astype(BF16)
    hit_bf = jnp.where(hit, 1.0, 0.0).astype(BF16)
    before = jnp.dot(hit_bf, earlier, preferred_element_type=F32)
    return jnp.where(hit, before, -2.0), first


def pack_kernel(capacity, ids_hbm, x_hbm, g_hbm, out_ref, ids_ref, x_ref, g_ref, sems):
    copies = [
        pltpu.make_async_copy(src, dst, sems.at[i])
        for i, (src, dst) in enumerate(((ids_hbm, ids_ref), (x_hbm, x_ref), (g_hbm, g_ref)))
    ]
    for copy in copies:
        copy.start()
    nz, members = out_ref.shape[:2]
    feats, tokens = x_ref.shape
    parts = feats // FINE
    lanes = nz * LANES
    part = lane_parts((FINE, lanes), 1, capacity)
    slot_of_lane = lane_slots(tokens, capacity, parts)
    copies[0].wait()
    slots, _ = token_slots(ids_ref[...], nz)
    place = jnp.concatenate(
        [jnp.where(slots[z : z + 1] == slot_of_lane, 1.0, 0.0).astype(BF16) for z in range(nz)],
        axis=0,
    )
    for kind, ref in enumerate((x_ref, g_ref)):
        copies[1 + kind].wait()
        spread = lax.dot_general(
            ref[...], place, (((1,), (1,)), ((), ())), preferred_element_type=F32
        )
        block = jnp.zeros((FINE, lanes), F32)
        for p in range(parts):
            block = jnp.where(part == p, spread[p * FINE : (p + 1) * FINE], block)
        block = block.astype(BF16)
        for z in range(nz):
            for m in range(members):
                out_ref[z, m, kind * FINE : (kind + 1) * FINE, :] = block[
                    :, z * LANES : (z + 1) * LANES
                ]


def unpack_kernel(capacity, parts, ny, in_ref, out_ref):
    nx, _, wide = out_ref.shape
    nz = in_ref.shape[0] // ny
    span = wide // parts
    rows = nz * capacity
    for kind in range(2):
        for pair in range(0, nz, 2):
            turned = []
            for z in (pair, pair + 1):
                block = in_ref[z * ny : (z + 1) * ny, kind * FINE : (kind + 1) * FINE, :]
                turned.append(block.reshape(span, LANES).astype(F32).T)
            start = kind * rows + pair * capacity
            for p in range(parts):
                piece = jnp.concatenate(
                    [t[p * capacity : (p + 1) * capacity] for t in turned], axis=0
                ).astype(BF16)
                for i in range(nx):
                    out_ref[i, start : start + 2 * capacity, p * span : (p + 1) * span] = piece


def repack_kernel(capacity, parts, ny, in_ref, out_ref):
    nx, rows, wide = in_ref.shape
    span = wide // parts
    for pair in range(0, rows // capacity, 2):
        here = slice(pair * capacity, (pair + 2) * capacity)
        total = in_ref[0, here, :].astype(F32)
        for i in range(1, nx):
            total += in_ref[i, here, :].astype(F32)
        for half in range(2):
            block = total[half * capacity : (half + 1) * capacity]
            pieces = [block[:, p * span : (p + 1) * span] for p in range(parts)]
            pieces.append(jnp.zeros((LANES - parts * capacity, span), F32))
            turned = jnp.concatenate(pieces, axis=0).T.astype(BF16)
            z = pair + half
            out_ref[z * ny : (z + 1) * ny] = turned.reshape(ny, FINE, LANES)


def order_kernel(gate_hbm, up_hbm, down_hbm, own_ref, sent_ref, sems):
    core = lax.axis_index("c")
    hidden = gate_hbm.shape[-1]
    copies = []
    for out_ref, c in ((own_ref, core), (sent_ref, 1 - core)):
        for k, src in enumerate((gate_hbm, up_hbm, down_hbm)):
            lanes = pl.ds(k * hidden, hidden)
            for yb in range(2):
                for xb in range(2):
                    for p in range(src.shape[5]):
                        copies.append(
                            pltpu.make_async_copy(
                                src.at[:, yb, :, xb, c, p],
                                out_ref.at[2 * yb + xb, p, :, :, :, lanes],
                                sems.at[len(copies)],
                            )
                        )
    for copy in copies:
        copy.start()
    for copy in copies:
        copy.wait()


def project_kernel(in_ref, w_ref, out_ref):
    members = in_ref.shape[0]
    rows, wide = out_ref.shape
    split = wide // 3 * 2
    x = jnp.concatenate([in_ref[i, :rows, :] for i in range(members)], axis=1)
    out_ref[:, :split] = jnp.dot(x, w_ref[:, :split], preferred_element_type=F32)
    g = jnp.concatenate([in_ref[i, rows:, :] for i in range(members)], axis=1)
    out_ref[:, split:] = jnp.dot(g, w_ref[:, split:], preferred_element_type=F32)


def tail_kernel(a_ref, b_ref, out_ref):
    hidden = a_ref.shape[1] // 3
    gate, upper, back = (
        a_ref[:, k * hidden : (k + 1) * hidden] + b_ref[:, k * hidden : (k + 1) * hidden]
        for k in range(3)
    )
    d_gate, d_upper = backward_tail(gate, upper, back)
    out_ref[:, :hidden] = d_gate
    out_ref[:, hidden:] = d_upper


def return_kernel(d_ref, w_ref, out_ref):
    out_ref[...] = lax.dot_general(
        d_ref[...],
        w_ref[:, : d_ref.shape[1]],
        (((1,), (1,)), ((), ())),
        preferred_element_type=F32,
    )


def return_add_kernel(d_ref, w_ref, sum_ref, out_ref):
    members, _, wide = out_ref.shape
    for i in range(members):
        here = slice(i * wide, (i + 1) * wide)
        total = lax.dot_general(
            d_ref[...],
            w_ref[here, : d_ref.shape[1]],
            (((1,), (1,)), ((), ())),
            preferred_element_type=F32,
        )
        out_ref[i] = (total + sum_ref[:, here]).astype(out_ref.dtype)


def combine_kernel(capacity, parts, ids_ref, prob_ref, scale_ref, out_ref):
    lanes, tokens = out_ref.shape
    experts = lanes // LANES
    slots, first = token_slots(ids_ref[...], experts)
    weights = jnp.where(first, prob_ref[0:1, :], prob_ref[1:2, :]) * scale_ref[...]
    slot_of_lane = lane_slots(tokens, capacity, parts)
    for z in range(experts):
        out_ref[z * LANES : (z + 1) * LANES, :] = jnp.where(
            slots[z : z + 1] == slot_of_lane, weights[z : z + 1], 0.0
        )


def final_kernel(capacity, parts, ny, combine_ref, in_ref, out_ref):
    lanes = combine_ref.shape[0]
    nz = lanes // LANES
    sums = []
    for z in range(nz):
        total = in_ref[z * ny].astype(F32)
        for y in range(1, ny):
            total += in_ref[z * ny + y].astype(F32)
        sums.append(total)
    sums = jnp.concatenate(sums, axis=1)
    part = lane_parts(sums.shape, 1, capacity)
    spread = jnp.concatenate([jnp.where(part == p, sums, 0.0) for p in range(parts)], axis=0)
    out_ref[...] = lax.dot_general(
        spread,
        combine_ref[...],
        (((1,), (0,)), ((), ())),
        precision=lax.Precision.HIGHEST,
        preferred_element_type=F32,
    ).astype(out_ref.dtype)


def call(kernel, shape, dtype, *operands, flops=0, spaces=pltpu.VMEM, scratch=()):
    moved = sum(o.size * o.dtype.itemsize for o in operands)
    moved += math.prod(shape) * jnp.dtype(dtype).itemsize
    return pl.pallas_call(
        kernel,
        out_shape=jax.ShapeDtypeStruct(shape, dtype),
        in_specs=[pl.BlockSpec(memory_space=spaces)] * len(operands),
        out_specs=pl.BlockSpec(memory_space=pltpu.VMEM),
        scratch_shapes=scratch,
        compiler_params=pltpu.CompilerParams(vmem_limit_bytes=32 * 1024 * 1024),
        cost_estimate=pl.CostEstimate(flops=flops, bytes_accessed=moved, transcendentals=0),
    )(*operands)


def exchange_groups(nz, ny, nx, nc):
    def index(z, y, x, c):
        return ((z * ny + y % ny) * nx + x % nx) * nc + c

    halves = [(yb, xb) for yb in range(2) for xb in range(2)]
    places = [(2 * ya, 2 * xa) for ya in range(ny // 2) for xa in range(nx // 2)]
    far = [
        [index(z, y + yb, x + xb, c) for z in range(nz) for y, x in places]
        for c in range(nc)
        for yb, xb in halves
    ]
    near = [
        [index(z, y + c + (yb + c) % 2, x + c + (xb + c) % 2, c) for yb, xb in halves]
        for z in range(nz)
        for c in range(nc)
        for y, x in places
    ]
    return far, near


def swap(blocks, groups):
    return lax.all_to_all(
        blocks, AXES, split_axis=0, concat_axis=0, axis_index_groups=groups, tiled=True
    )


def other_core(values):
    return lax.ppermute(values, "c", [(0, 1), (1, 0)])


def shards(activations, out_grad, token_scale, route_prob, route_ids, w_gate, w_up, w_down):
    nz, ny, nx, nc = (lax.axis_size(a) for a in AXES)
    far, near = exchange_groups(nz, ny, nx, nc)
    spread = ny * nx // 4
    members = 4
    core = lax.axis_index("c")
    tokens, feats = activations.shape
    capacity = min(tokens, 5 * tokens // (2 * nz))
    parts = feats // FINE
    hidden = w_gate.shape[2]
    rows = nz * capacity
    wide = feats * spread

    send = call(
        functools.partial(pack_kernel, capacity),
        (nz, spread, 2 * FINE, LANES),
        BF16,
        route_ids.T,
        activations.T,
        out_grad.T,
        spaces=pl.ANY,
        scratch=(
            pltpu.VMEM(route_ids.T.shape, route_ids.dtype),
            pltpu.VMEM((feats, tokens), BF16),
            pltpu.VMEM((feats, tokens), BF16),
            pltpu.SemaphoreType.DMA((3,)),
        ),
    )
    got = swap(send.reshape(nz * spread, 2 * FINE, LANES), far)

    views = (ny // 2, 2, nx // 2, 2, nc, parts, FINE, hidden)
    ordered = (members, parts, ny // 2, nx // 2, FINE, 3 * hidden)
    own, sent = pl.pallas_call(
        order_kernel,
        out_shape=[jax.ShapeDtypeStruct(ordered, BF16)] * 2,
        in_specs=[pl.BlockSpec(memory_space=pl.ANY)] * 3,
        out_specs=[pl.BlockSpec(memory_space=pltpu.VMEM)] * 2,
        scratch_shapes=[pltpu.SemaphoreType.DMA((2 * 3 * members * parts,))],
        compiler_params=pltpu.CompilerParams(vmem_limit_bytes=32 * 1024 * 1024),
        cost_estimate=pl.CostEstimate(flops=0, bytes_accessed=12 * 1024 * 1024, transcendentals=0),
    )(w_gate.reshape(views), w_up.reshape(views), w_down[0].T.reshape(views))
    own, sent = (w.reshape(members * wide, 3 * hidden) for w in (own, sent))
    got, own = lax.optimization_barrier((got, own))

    copies = call(
        functools.partial(unpack_kernel, capacity, parts, spread),
        (members, 2 * rows, wide),
        BF16,
        got,
    )
    block = swap(copies, near)

    other = other_core(sent)
    flops = 2 * rows * members * wide * 3 * hidden

    def project(w):
        return call(project_kernel, (rows, 3 * hidden), F32, block, w, flops=flops)

    theirs = other_core(project(other))
    d_own = call(tail_kernel, (rows, 2 * hidden), BF16, project(own), theirs)
    d_other = other_core(d_own)
    flops = flops // 3 * 2
    part = call(return_kernel, (rows, members * wide), F32, d_own, own, flops=flops)
    part = call(return_add_kernel, (members, rows, wide), BF16, d_other, other, part, flops=flops)
    part = swap(part, near)
    part = call(
        functools.partial(repack_kernel, capacity, parts, spread),
        (nz * spread, FINE, LANES),
        BF16,
        part,
    )
    part = swap(part, far)
    combine = call(
        functools.partial(combine_kernel, capacity, parts),
        (nz * LANES, tokens),
        F32,
        route_ids.T,
        route_prob.T,
        token_scale.reshape(1, tokens),
    )
    return call(
        functools.partial(final_kernel, capacity, parts, spread),
        (feats, tokens),
        BF16,
        combine,
        part,
    ).T


def solution(mesh):
    devices = mesh.devices
    fine = Mesh(devices.reshape(devices.shape[0], 8, 4, 2), AXES)
    tensor = ("y", "x", "c")
    placed = (
        P("z", tensor),
        P("z", tensor),
        P("z"),
        P("z", None),
        P("z", None),
        P("z", None, tensor),
        P("z", None, tensor),
        P("z", tensor, None),
    )
    return jax.shard_map(
        shards, mesh=fine, in_specs=placed, out_specs=P("z", tensor), check_vma=False
    )
```

```python
import functools
import math

import jax
import jax.numpy as jnp
from jax import lax
from jax.experimental import pallas as pl
from jax.experimental.pallas import tpu as pltpu
from jax.sharding import Mesh, PartitionSpec as P

BF16 = jnp.bfloat16
F32 = jnp.float32
LANES = 128
FINE = 16
AXES = ("z", "y", "x", "c")


def backward_tail(gate, upper, back):
    sigmoid_g = jax.nn.sigmoid(gate)
    slope = sigmoid_g * (1.0 + gate * (1.0 - sigmoid_g))
    d_gate = (back * upper * slope).astype(BF16)
    d_upper = (back * gate * sigmoid_g).astype(BF16)
    return d_gate, d_upper


def lane_parts(shape, axis, capacity):
    inner = lax.broadcasted_iota(jnp.int32, shape, axis) % LANES
    return inner // capacity


def lane_slots(tokens, capacity, parts):
    inner = lax.broadcasted_iota(jnp.int32, (LANES, tokens), 0)
    part = inner // capacity
    return jnp.where(part < parts, inner - part * capacity, -1).astype(F32)


def token_slots(ids, experts):
    tokens = ids.shape[1]
    expert = lax.broadcasted_iota(jnp.int32, (experts, tokens), 0).astype(F32)
    first = ids[0:1, :] == expert
    hit = first | (ids[1:2, :] == expert)
    row = lax.broadcasted_iota(jnp.int32, (tokens, tokens), 0)
    col = lax.broadcasted_iota(jnp.int32, (tokens, tokens), 1)
    earlier = jnp.where(row < col, 1.0, 0.0).astype(BF16)
    hit_bf = jnp.where(hit, 1.0, 0.0).astype(BF16)
    before = jnp.dot(hit_bf, earlier, preferred_element_type=F32)
    return jnp.where(hit, before, -2.0), first


def pack_kernel(capacity, feats, head_ref, out_ref):
    nz, members = out_ref.shape[:2]
    tokens = head_ref.shape[1]
    parts = feats // FINE
    lanes = nz * LANES
    part = lane_parts((FINE, lanes), 1, capacity)
    slot_of_lane = lane_slots(tokens, capacity, parts)
    slots, _ = token_slots(head_ref[2 * feats :, :].astype(F32), nz)
    place = jnp.concatenate(
        [jnp.where(slots[z : z + 1] == slot_of_lane, 1.0, 0.0).astype(BF16) for z in range(nz)],
        axis=0,
    )
    for kind in range(2):
        spread = lax.dot_general(
            head_ref[kind * feats : (kind + 1) * feats, :],
            place,
            (((1,), (1,)), ((), ())),
            preferred_element_type=F32,
        )
        block = jnp.zeros((FINE, lanes), F32)
        for p in range(parts):
            block = jnp.where(part == p, spread[p * FINE : (p + 1) * FINE], block)
        block = block.astype(BF16)
        for z in range(nz):
            for m in range(members):
                out_ref[z, m, kind * FINE : (kind + 1) * FINE, :] = block[
                    :, z * LANES : (z + 1) * LANES
                ]


def unpack_kernel(capacity, parts, ny, in_ref, out_ref):
    nx, _, wide = out_ref.shape
    nz = in_ref.shape[0] // ny
    span = wide // parts
    rows = nz * capacity
    for kind in range(2):
        for pair in range(0, nz, 2):
            turned = []
            for z in (pair, pair + 1):
                block = in_ref[z * ny : (z + 1) * ny, kind * FINE : (kind + 1) * FINE, :]
                turned.append(block.reshape(span, LANES).astype(F32).T)
            start = kind * rows + pair * capacity
            for p in range(parts):
                piece = jnp.concatenate(
                    [t[p * capacity : (p + 1) * capacity] for t in turned], axis=0
                ).astype(BF16)
                for i in range(nx):
                    out_ref[i, start : start + 2 * capacity, p * span : (p + 1) * span] = piece


def repack_kernel(capacity, parts, ny, in_ref, out_ref):
    nx, rows, wide = in_ref.shape
    span = wide // parts
    for pair in range(0, rows // capacity, 2):
        here = slice(pair * capacity, (pair + 2) * capacity)
        total = in_ref[0, here, :].astype(F32)
        for i in range(1, nx):
            total += in_ref[i, here, :].astype(F32)
        for half in range(2):
            block = total[half * capacity : (half + 1) * capacity]
            pieces = [block[:, p * span : (p + 1) * span] for p in range(parts)]
            pieces.append(jnp.zeros((LANES - parts * capacity, span), F32))
            turned = jnp.concatenate(pieces, axis=0).T.astype(BF16)
            z = pair + half
            out_ref[z * ny : (z + 1) * ny] = turned.reshape(ny, FINE, LANES)


def order_kernel(*refs):
    core = lax.axis_index("c")
    srcs, own, sent, sems = refs[:3], refs[3:6], refs[6:9], refs[9]
    copies = []
    for outs, c in ((own, core), (sent, 1 - core)):
        for src, out_ref in zip(srcs, outs):
            for yb in range(2):
                for xb in range(2):
                    for p in range(src.shape[5]):
                        copies.append(
                            pltpu.make_async_copy(
                                src.at[:, yb, :, xb, c, p],
                                out_ref.at[2 * yb + xb, p],
                                sems.at[len(copies)],
                            )
                        )
    for copy in copies:
        copy.start()
    for copy in copies:
        copy.wait()


def project_kernel(in_ref, gate_ref, up_ref, down_ref, out_ref):
    members = in_ref.shape[0]
    rows = out_ref.shape[0]
    hidden = gate_ref.shape[1]
    x = jnp.concatenate([in_ref[i, :rows, :] for i in range(members)], axis=1)
    out_ref[:, :hidden] = jnp.dot(x, gate_ref[...], preferred_element_type=F32)
    out_ref[:, hidden : 2 * hidden] = jnp.dot(x, up_ref[...], preferred_element_type=F32)
    g = jnp.concatenate([in_ref[i, rows:, :] for i in range(members)], axis=1)
    out_ref[:, 2 * hidden :] = jnp.dot(g, down_ref[...], preferred_element_type=F32)


def tail_kernel(a_ref, b_ref, out_ref):
    hidden = a_ref.shape[1] // 3
    gate, upper, back = (
        a_ref[:, k * hidden : (k + 1) * hidden] + b_ref[:, k * hidden : (k + 1) * hidden]
        for k in range(3)
    )
    d_gate, d_upper = backward_tail(gate, upper, back)
    out_ref[:, :hidden] = d_gate
    out_ref[:, hidden:] = d_upper


def return_part(d_ref, gate_ref, up_ref, here):
    hidden = gate_ref.shape[1]
    across = (((1,), (1,)), ((), ()))
    part = lax.dot_general(
        d_ref[:, :hidden], gate_ref[here, :], across, preferred_element_type=F32
    )
    return part + lax.dot_general(
        d_ref[:, hidden:], up_ref[here, :], across, preferred_element_type=F32
    )


def return_kernel(d_ref, gate_ref, up_ref, out_ref):
    out_ref[...] = return_part(d_ref, gate_ref, up_ref, slice(None))


def return_add_kernel(d_ref, gate_ref, up_ref, sum_ref, out_ref):
    members, _, wide = out_ref.shape
    for i in range(members):
        here = slice(i * wide, (i + 1) * wide)
        part = return_part(d_ref, gate_ref, up_ref, here)
        out_ref[i] = (part + sum_ref[:, here]).astype(out_ref.dtype)


def combine_kernel(capacity, parts, ids_ref, prob_ref, scale_ref, out_ref):
    lanes, tokens = out_ref.shape
    experts = lanes // LANES
    slots, first = token_slots(ids_ref[...].astype(F32), experts)
    weights = jnp.where(first, prob_ref[0:1, :], prob_ref[1:2, :]) * scale_ref[...]
    slot_of_lane = lane_slots(tokens, capacity, parts)
    for z in range(experts):
        out_ref[z * LANES : (z + 1) * LANES, :] = jnp.where(
            slots[z : z + 1] == slot_of_lane, weights[z : z + 1], 0.0
        )


def final_kernel(capacity, parts, ny, combine_ref, in_ref, out_ref):
    lanes = combine_ref.shape[0]
    nz = lanes // LANES
    sums = []
    for z in range(nz):
        total = in_ref[z * ny].astype(F32)
        for y in range(1, ny):
            total += in_ref[z * ny + y].astype(F32)
        sums.append(total)
    sums = jnp.concatenate(sums, axis=1)
    part = lane_parts(sums.shape, 1, capacity)
    spread = jnp.concatenate([jnp.where(part == p, sums, 0.0) for p in range(parts)], axis=0)
    out_ref[...] = lax.dot_general(
        spread,
        combine_ref[...],
        (((1,), (0,)), ((), ())),
        precision=lax.Precision.HIGHEST,
        preferred_element_type=F32,
    ).astype(out_ref.dtype)


def call(kernel, shape, dtype, *operands, flops=0):
    moved = sum(o.size * o.dtype.itemsize for o in operands)
    moved += math.prod(shape) * jnp.dtype(dtype).itemsize
    return pl.pallas_call(
        kernel,
        out_shape=jax.ShapeDtypeStruct(shape, dtype),
        in_specs=[pl.BlockSpec(memory_space=pltpu.VMEM)] * len(operands),
        out_specs=pl.BlockSpec(memory_space=pltpu.VMEM),
        compiler_params=pltpu.CompilerParams(vmem_limit_bytes=32 * 1024 * 1024),
        cost_estimate=pl.CostEstimate(flops=flops, bytes_accessed=moved, transcendentals=0),
    )(*operands)


def exchange_groups(nz, ny, nx, nc):
    def index(z, y, x, c):
        return ((z * ny + y % ny) * nx + x % nx) * nc + c

    halves = [(yb, xb) for yb in range(2) for xb in range(2)]
    places = [(2 * ya, 2 * xa) for ya in range(ny // 2) for xa in range(nx // 2)]
    far = [
        [index(z, y + yb, x + xb, c) for z in range(nz) for y, x in places]
        for c in range(nc)
        for yb, xb in halves
    ]
    near = [
        [index(z, y + c + (yb + c) % 2, x + c + (xb + c) % 2, c) for yb, xb in halves]
        for z in range(nz)
        for c in range(nc)
        for y, x in places
    ]
    return far, near


def swap(blocks, groups):
    return lax.all_to_all(
        blocks, AXES, split_axis=0, concat_axis=0, axis_index_groups=groups, tiled=True
    )


def other_core(values):
    return lax.ppermute(values, "c", [(0, 1), (1, 0)])


def shards(activations, out_grad, token_scale, route_prob, route_ids, w_gate, w_up, w_down):
    nz, ny, nx, nc = (lax.axis_size(a) for a in AXES)
    far, near = exchange_groups(nz, ny, nx, nc)
    spread = ny * nx // 4
    members = 4
    core = lax.axis_index("c")
    tokens, feats = activations.shape
    capacity = min(tokens, 5 * tokens // (2 * nz))
    parts = feats // FINE
    hidden = w_gate.shape[2]
    rows = nz * capacity
    wide = feats * spread

    ids = jnp.pad(route_ids.T.astype(BF16), ((0, FINE - route_ids.shape[1]), (0, 0)))
    head = jnp.concatenate([activations.T, out_grad.T, ids], axis=0)
    send = call(
        functools.partial(pack_kernel, capacity, feats),
        (nz, spread, 2 * FINE, LANES),
        BF16,
        head,
    )
    got = swap(send.reshape(nz * spread, 2 * FINE, LANES), far)

    views = (ny // 2, 2, nx // 2, 2, nc, parts, FINE, hidden)
    ordered = (members, parts, ny // 2, nx // 2, FINE, hidden)
    weights = pl.pallas_call(
        order_kernel,
        out_shape=[jax.ShapeDtypeStruct(ordered, BF16)] * 6,
        in_specs=[pl.BlockSpec(memory_space=pltpu.HBM)] * 3,
        out_specs=[pl.BlockSpec(memory_space=pltpu.VMEM)] * 6,
        scratch_shapes=[pltpu.SemaphoreType.DMA((2 * 3 * members * parts,))],
        compiler_params=pltpu.CompilerParams(vmem_limit_bytes=32 * 1024 * 1024),
        cost_estimate=pl.CostEstimate(flops=0, bytes_accessed=12 * 1024 * 1024, transcendentals=0),
    )(w_gate.reshape(views), w_up.reshape(views), w_down[0].T.reshape(views))
    weights = [w.reshape(members * wide, hidden) for w in weights]
    own, other = weights[:3], [other_core(w) for w in weights[3:]]
    got, own, other = lax.optimization_barrier((got, own, other))

    copies = call(
        functools.partial(unpack_kernel, capacity, parts, spread),
        (members, 2 * rows, wide),
        BF16,
        got,
    )
    block = swap(copies, near)

    flops = 2 * rows * members * wide * 3 * hidden

    def project(w):
        return call(project_kernel, (rows, 3 * hidden), F32, block, *w, flops=flops)

    def tail(a, b):
        return call(tail_kernel, (rows, 2 * hidden), BF16, a, b)

    part_other = project(other)
    rest_own = other_core(part_other)
    part_own = project(own)
    rest_other = other_core(part_own)
    d_own = tail(part_own, rest_own)
    flops = flops // 3 * 2
    part = call(return_kernel, (rows, members * wide), F32, d_own, *own[:2], flops=flops)
    d_other = tail(part_other, rest_other)
    part = call(
        return_add_kernel, (members, rows, wide), BF16, d_other, *other[:2], part, flops=flops
    )
    part = swap(part, near)
    part = call(
        functools.partial(repack_kernel, capacity, parts, spread),
        (nz * spread, FINE, LANES),
        BF16,
        part,
    )
    part = swap(part, far)
    combine = call(
        functools.partial(combine_kernel, capacity, parts),
        (nz * LANES, tokens),
        F32,
        route_ids.T,
        route_prob.T,
        token_scale.reshape(1, tokens),
    )
    return call(
        functools.partial(final_kernel, capacity, parts, spread),
        (feats, tokens),
        BF16,
        combine,
        part,
    ).T


def solution(mesh):
    devices = mesh.devices
    fine = Mesh(devices.reshape(devices.shape[0], 8, 4, 2), AXES)
    tensor = ("y", "x", "c")
    placed = (
        P("z", tensor),
        P("z", tensor),
        P("z"),
        P("z", None),
        P("z", None),
        P("z", None, tensor),
        P("z", None, tensor),
        P("z", tensor, None),
    )
    return jax.shard_map(
        shards, mesh=fine, in_specs=placed, out_specs=P("z", tensor), check_vma=False
    )
```

```python
import functools
import math

import jax
import jax.numpy as jnp
from jax import lax
from jax.experimental import pallas as pl
from jax.experimental.pallas import tpu as pltpu
from jax.sharding import Mesh, PartitionSpec as P

BF16 = jnp.bfloat16
F32 = jnp.float32
LANES = 128
FINE = 16
VMEM_LIMIT = 16 * 1024 * 1024
AXES = ("z", "y", "x", "c")


def backward_tail(gate, upper, back):
    sigmoid_g = jax.nn.sigmoid(gate)
    slope = sigmoid_g * (1.0 + gate * (1.0 - sigmoid_g))
    d_gate = (back * upper * slope).astype(BF16)
    d_upper = (back * gate * sigmoid_g).astype(BF16)
    return d_gate, d_upper


def lane_parts(shape, axis, capacity):
    inner = lax.broadcasted_iota(jnp.int32, shape, axis) % LANES
    return inner // capacity


def lane_slots(tokens, capacity, parts):
    inner = lax.broadcasted_iota(jnp.int32, (LANES, tokens), 0)
    part = inner // capacity
    return jnp.where(part < parts, inner - part * capacity, -1).astype(F32)


def token_slots(ids, experts):
    tokens = ids.shape[1]
    expert = lax.broadcasted_iota(jnp.int32, (experts, tokens), 0).astype(F32)
    first = ids[0:1, :] == expert
    hit = first | (ids[1:2, :] == expert)
    row = lax.broadcasted_iota(jnp.int32, (tokens, tokens), 0)
    col = lax.broadcasted_iota(jnp.int32, (tokens, tokens), 1)
    earlier = jnp.where(row < col, 1.0, 0.0).astype(BF16)
    hit_bf = jnp.where(hit, 1.0, 0.0).astype(BF16)
    before = jnp.dot(hit_bf, earlier, preferred_element_type=F32)
    return jnp.where(hit, before, -2.0), first


def pack_kernel(capacity, feats, head_ref, out_ref):
    nz, members = out_ref.shape[:2]
    tokens = head_ref.shape[1]
    parts = feats // FINE
    lanes = nz * LANES
    part = lane_parts((FINE, lanes), 1, capacity)
    slot_of_lane = lane_slots(tokens, capacity, parts)
    slots, _ = token_slots(head_ref[2 * feats :, :].astype(F32), nz)
    place = jnp.concatenate(
        [jnp.where(slots[z : z + 1] == slot_of_lane, 1.0, 0.0).astype(BF16) for z in range(nz)],
        axis=0,
    )
    for kind in range(2):
        spread = lax.dot_general(
            head_ref[kind * feats : (kind + 1) * feats, :],
            place,
            (((1,), (1,)), ((), ())),
            preferred_element_type=F32,
        )
        block = jnp.zeros((FINE, lanes), F32)
        for p in range(parts):
            block = jnp.where(part == p, spread[p * FINE : (p + 1) * FINE], block)
        block = block.astype(BF16)
        for z in range(nz):
            for m in range(members):
                out_ref[z, m, kind * FINE : (kind + 1) * FINE, :] = block[
                    :, z * LANES : (z + 1) * LANES
                ]


def unpack_kernel(capacity, parts, ny, in_ref, out_ref):
    nx, _, wide = out_ref.shape
    nz = in_ref.shape[0] // ny
    span = wide // parts
    rows = nz * capacity
    for kind in range(2):
        for pair in range(0, nz, 2):
            turned = []
            for z in (pair, pair + 1):
                block = in_ref[z * ny : (z + 1) * ny, kind * FINE : (kind + 1) * FINE, :]
                turned.append(block.reshape(span, LANES).astype(F32).T)
            start = kind * rows + pair * capacity
            for p in range(parts):
                piece = jnp.concatenate(
                    [t[p * capacity : (p + 1) * capacity] for t in turned], axis=0
                ).astype(BF16)
                for i in range(nx):
                    out_ref[i, start : start + 2 * capacity, p * span : (p + 1) * span] = piece


def repack_kernel(capacity, parts, ny, in_ref, out_ref):
    nx, rows, wide = in_ref.shape
    span = wide // parts
    for pair in range(0, rows // capacity, 2):
        here = slice(pair * capacity, (pair + 2) * capacity)
        total = in_ref[0, here, :].astype(F32)
        for i in range(1, nx):
            total += in_ref[i, here, :].astype(F32)
        for half in range(2):
            block = total[half * capacity : (half + 1) * capacity]
            pieces = [block[:, p * span : (p + 1) * span] for p in range(parts)]
            pieces.append(jnp.zeros((LANES - parts * capacity, span), F32))
            turned = jnp.concatenate(pieces, axis=0).T.astype(BF16)
            z = pair + half
            out_ref[z * ny : (z + 1) * ny] = turned.reshape(ny, FINE, LANES)


def order_kernel(*refs):
    core = lax.axis_index("c")
    srcs, own, sent, sems = refs[:3], refs[3:6], refs[6:9], refs[9]
    copies = []
    for outs, c in ((own, core), (sent, 1 - core)):
        for src, out_ref in zip(srcs, outs):
            for yb in range(2):
                for xb in range(2):
                    for p in range(src.shape[5]):
                        copies.append(
                            pltpu.make_async_copy(
                                src.at[:, yb, :, xb, c, p],
                                out_ref.at[2 * yb + xb, p],
                                sems.at[len(copies)],
                            )
                        )
    for copy in copies:
        copy.start()
    for copy in copies:
        copy.wait()


def project_kernel(in_ref, gate_ref, up_ref, down_ref, out_ref):
    members = in_ref.shape[0]
    rows = out_ref.shape[0]
    hidden = gate_ref.shape[1]
    x = jnp.concatenate([in_ref[i, :rows, :] for i in range(members)], axis=1)
    out_ref[:, :hidden] = jnp.dot(x, gate_ref[...], preferred_element_type=F32)
    out_ref[:, hidden : 2 * hidden] = jnp.dot(x, up_ref[...], preferred_element_type=F32)
    g = jnp.concatenate([in_ref[i, rows:, :] for i in range(members)], axis=1)
    out_ref[:, 2 * hidden :] = jnp.dot(g, down_ref[...], preferred_element_type=F32)


def tail_kernel(a_ref, b_ref, out_ref):
    hidden = a_ref.shape[1] // 3
    gate, upper, back = (
        a_ref[:, k * hidden : (k + 1) * hidden] + b_ref[:, k * hidden : (k + 1) * hidden]
        for k in range(3)
    )
    d_gate, d_upper = backward_tail(gate, upper, back)
    out_ref[:, :hidden] = d_gate
    out_ref[:, hidden:] = d_upper


def return_part(d_ref, gate_ref, up_ref, here):
    hidden = gate_ref.shape[1]
    across = (((1,), (1,)), ((), ()))
    part = lax.dot_general(
        d_ref[:, :hidden], gate_ref[here, :], across, preferred_element_type=F32
    )
    return part + lax.dot_general(
        d_ref[:, hidden:], up_ref[here, :], across, preferred_element_type=F32
    )


def return_kernel(d_ref, gate_ref, up_ref, out_ref):
    out_ref[...] = return_part(d_ref, gate_ref, up_ref, slice(None))


def return_add_kernel(d_ref, gate_ref, up_ref, sum_ref, out_ref):
    members, _, wide = out_ref.shape
    for i in range(members):
        here = slice(i * wide, (i + 1) * wide)
        part = return_part(d_ref, gate_ref, up_ref, here)
        out_ref[i] = (part + sum_ref[:, here]).astype(out_ref.dtype)


def combine_kernel(capacity, parts, ids_ref, prob_ref, scale_ref, out_ref):
    lanes, tokens = out_ref.shape
    experts = lanes // LANES
    slots, first = token_slots(ids_ref[...].astype(F32), experts)
    weights = jnp.where(first, prob_ref[0:1, :], prob_ref[1:2, :]) * scale_ref[...]
    slot_of_lane = lane_slots(tokens, capacity, parts)
    for z in range(experts):
        out_ref[z * LANES : (z + 1) * LANES, :] = jnp.where(
            slots[z : z + 1] == slot_of_lane, weights[z : z + 1], 0.0
        )


def final_kernel(capacity, parts, ny, combine_ref, in_ref, out_ref):
    lanes = combine_ref.shape[0]
    nz = lanes // LANES
    sums = []
    for z in range(nz):
        total = in_ref[z * ny].astype(F32)
        for y in range(1, ny):
            total += in_ref[z * ny + y].astype(F32)
        sums.append(total)
    sums = jnp.concatenate(sums, axis=1)
    part = lane_parts(sums.shape, 1, capacity)
    spread = jnp.concatenate([jnp.where(part == p, sums, 0.0) for p in range(parts)], axis=0)
    out_ref[...] = lax.dot_general(
        spread,
        combine_ref[...],
        (((1,), (0,)), ((), ())),
        precision=lax.Precision.HIGHEST,
        preferred_element_type=F32,
    ).astype(out_ref.dtype)


def call(kernel, shape, dtype, *operands, flops=0):
    moved = sum(o.size * o.dtype.itemsize for o in operands)
    moved += math.prod(shape) * jnp.dtype(dtype).itemsize
    return pl.pallas_call(
        kernel,
        out_shape=jax.ShapeDtypeStruct(shape, dtype),
        in_specs=[pl.BlockSpec(memory_space=pltpu.VMEM)] * len(operands),
        out_specs=pl.BlockSpec(memory_space=pltpu.VMEM),
        compiler_params=pltpu.CompilerParams(vmem_limit_bytes=VMEM_LIMIT),
        cost_estimate=pl.CostEstimate(flops=flops, bytes_accessed=moved, transcendentals=0),
    )(*operands)


def exchange_groups(nz, ny, nx, nc):
    def index(z, y, x, c):
        return ((z * ny + y % ny) * nx + x % nx) * nc + c

    halves = [(yb, xb) for yb in range(2) for xb in range(2)]
    places = [(2 * ya, 2 * xa) for ya in range(ny // 2) for xa in range(nx // 2)]
    far = [
        [index(z, y + yb, x + xb, c) for z in range(nz) for y, x in places]
        for c in range(nc)
        for yb, xb in halves
    ]
    near = [
        [index(z, y + c + (yb + c) % 2, x + c + (xb + c) % 2, c) for yb, xb in halves]
        for z in range(nz)
        for c in range(nc)
        for y, x in places
    ]
    return far, near


def swap(blocks, groups):
    return lax.all_to_all(
        blocks, AXES, split_axis=0, concat_axis=0, axis_index_groups=groups, tiled=True
    )


def other_core(values):
    return lax.ppermute(values, "c", [(0, 1), (1, 0)])


def shards(activations, out_grad, token_scale, route_prob, route_ids, w_gate, w_up, w_down):
    nz, ny, nx, nc = (lax.axis_size(a) for a in AXES)
    far, near = exchange_groups(nz, ny, nx, nc)
    spread = ny * nx // 4
    members = 4
    core = lax.axis_index("c")
    tokens, feats = activations.shape
    capacity = min(tokens, 5 * tokens // (2 * nz))
    parts = feats // FINE
    hidden = w_gate.shape[2]
    rows = nz * capacity
    wide = feats * spread

    ids = jnp.pad(route_ids.T.astype(BF16), ((0, FINE - route_ids.shape[1]), (0, 0)))
    head = jnp.concatenate([activations.T, out_grad.T, ids], axis=0)
    send = call(
        functools.partial(pack_kernel, capacity, feats),
        (nz, spread, 2 * FINE, LANES),
        BF16,
        head,
    )
    got = swap(send.reshape(nz * spread, 2 * FINE, LANES), far)

    views = (ny // 2, 2, nx // 2, 2, nc, parts, FINE, hidden)
    ordered = (members, parts, ny // 2, nx // 2, FINE, hidden)
    weights = pl.pallas_call(
        order_kernel,
        out_shape=[jax.ShapeDtypeStruct(ordered, BF16)] * 6,
        in_specs=[pl.BlockSpec(memory_space=pl.ANY)] * 3,
        out_specs=[pl.BlockSpec(memory_space=pltpu.VMEM)] * 6,
        scratch_shapes=[pltpu.SemaphoreType.DMA((2 * 3 * members * parts,))],
        compiler_params=pltpu.CompilerParams(vmem_limit_bytes=VMEM_LIMIT),
        cost_estimate=pl.CostEstimate(flops=0, bytes_accessed=12 * 1024 * 1024, transcendentals=0),
    )(
        pltpu.with_memory_space_constraint(w_gate.reshape(views), pltpu.HBM),
        pltpu.with_memory_space_constraint(w_up.reshape(views), pltpu.HBM),
        w_down[0].T.reshape(views),
    )
    weights = [w.reshape(members * wide, hidden) for w in weights]
    own, other = weights[:3], [other_core(w) for w in weights[3:]]
    got, own, other = lax.optimization_barrier((got, own, other))

    copies = call(
        functools.partial(unpack_kernel, capacity, parts, spread),
        (members, 2 * rows, wide),
        BF16,
        got,
    )
    block = swap(copies, near)

    flops = 2 * rows * members * wide * 3 * hidden

    def project(w):
        return call(project_kernel, (rows, 3 * hidden), F32, block, *w, flops=flops)

    def tail(a, b):
        return call(tail_kernel, (rows, 2 * hidden), BF16, a, b)

    part_other = project(other)
    rest_own = other_core(part_other)
    part_own = project(own)
    rest_other = other_core(part_own)
    d_own = tail(part_own, rest_own)
    flops = flops // 3 * 2
    part = call(return_kernel, (rows, members * wide), F32, d_own, *own[:2], flops=flops)
    combine = call(
        functools.partial(combine_kernel, capacity, parts),
        (nz * LANES, tokens),
        F32,
        route_ids.T,
        route_prob.T,
        token_scale.reshape(1, tokens),
    )
    part, combine = lax.optimization_barrier((part, combine))
    d_other = tail(part_other, rest_other)
    part = call(
        return_add_kernel, (members, rows, wide), BF16, d_other, *other[:2], part, flops=flops
    )
    part = swap(part, near)
    part = call(
        functools.partial(repack_kernel, capacity, parts, spread),
        (nz * spread, FINE, LANES),
        BF16,
        part,
    )
    part = swap(part, far)
    return call(
        functools.partial(final_kernel, capacity, parts, spread),
        (feats, tokens),
        BF16,
        combine,
        part,
    ).T


def solution(mesh):
    devices = mesh.devices
    fine = Mesh(devices.reshape(devices.shape[0], 8, 4, 2), AXES)
    tensor = ("y", "x", "c")
    placed = (
        P("z", tensor),
        P("z", tensor),
        P("z"),
        P("z", None),
        P("z", None),
        P("z", None, tensor),
        P("z", None, tensor),
        P("z", tensor, None),
    )
    return jax.shard_map(
        shards, mesh=fine, in_specs=placed, out_specs=P("z", tensor), check_vma=False
    )
```

```python
import functools
import math

import jax
import jax.numpy as jnp
from jax import lax
from jax.experimental import pallas as pl
from jax.experimental.pallas import tpu as pltpu
from jax.sharding import Mesh, PartitionSpec as P

BF16 = jnp.bfloat16
F32 = jnp.float32
LANES = 128
FINE = 16
VMEM_LIMIT = 16 * 1024 * 1024
AXES = ("z", "y", "x", "c")


def backward_tail(gate, upper, back):
    sigmoid_g = jax.nn.sigmoid(gate)
    slope = sigmoid_g * (1.0 + gate * (1.0 - sigmoid_g))
    d_gate = (back * upper * slope).astype(BF16)
    d_upper = (back * gate * sigmoid_g).astype(BF16)
    return d_gate, d_upper


def lane_parts(shape, axis, capacity):
    inner = lax.broadcasted_iota(jnp.int32, shape, axis) % LANES
    return inner // capacity


def lane_slots(tokens, capacity, parts):
    inner = lax.broadcasted_iota(jnp.int32, (LANES, tokens), 0)
    part = inner // capacity
    return jnp.where(part < parts, inner - part * capacity, -1).astype(F32)


def token_slots(ids, experts):
    tokens = ids.shape[1]
    expert = lax.broadcasted_iota(jnp.int32, (experts, tokens), 0).astype(F32)
    first = ids[0:1, :] == expert
    hit = first | (ids[1:2, :] == expert)
    row = lax.broadcasted_iota(jnp.int32, (tokens, tokens), 0)
    col = lax.broadcasted_iota(jnp.int32, (tokens, tokens), 1)
    earlier = jnp.where(row < col, 1.0, 0.0).astype(BF16)
    hit_bf = jnp.where(hit, 1.0, 0.0).astype(BF16)
    before = jnp.dot(hit_bf, earlier, preferred_element_type=F32)
    return jnp.where(hit, before, -2.0), first


def pack_kernel(capacity, ids_hbm, x_hbm, g_hbm, out_ref, ids_ref, x_ref, g_ref, sems):
    copies = [
        pltpu.make_async_copy(src, dst, sems.at[i])
        for i, (src, dst) in enumerate(((ids_hbm, ids_ref), (x_hbm, x_ref), (g_hbm, g_ref)))
    ]
    for copy in copies:
        copy.start()
    nya, nz, nxa = out_ref.shape[:3]
    feats, tokens = x_ref.shape
    parts = feats // FINE
    lanes = nz * LANES
    part = lane_parts((FINE, lanes), 1, capacity)
    slot_of_lane = lane_slots(tokens, capacity, parts)
    copies[0].wait()
    slots, _ = token_slots(ids_ref[...].astype(F32), nz)
    place = jnp.concatenate(
        [jnp.where(slots[z : z + 1] == slot_of_lane, 1.0, 0.0).astype(BF16) for z in range(nz)],
        axis=0,
    )
    for kind, ref in enumerate((x_ref, g_ref)):
        copies[1 + kind].wait()
        spread = lax.dot_general(
            ref[...],
            place,
            (((1,), (1,)), ((), ())),
            preferred_element_type=F32,
        )
        block = jnp.zeros((FINE, lanes), F32)
        for p in range(parts):
            block = jnp.where(part == p, spread[p * FINE : (p + 1) * FINE], block)
        block = block.astype(BF16)
        for z in range(nz):
            piece = block[:, z * LANES : (z + 1) * LANES]
            for ya in range(nya):
                for xa in range(nxa):
                    out_ref[ya, z, xa, kind * FINE : (kind + 1) * FINE, :] = piece


def unpack_kernel(capacity, parts, in_ref, out_ref):
    nx, _, wide = out_ref.shape
    nz = in_ref.shape[1]
    span = wide // parts
    rows = nz * capacity
    for kind in range(2):
        for pair in range(0, nz, 2):
            turned = []
            for z in (pair, pair + 1):
                block = in_ref[:, z, :, kind * FINE : (kind + 1) * FINE, :]
                turned.append(block.reshape(span, LANES).astype(F32).T)
            start = kind * rows + pair * capacity
            for p in range(parts):
                piece = jnp.concatenate(
                    [t[p * capacity : (p + 1) * capacity] for t in turned], axis=0
                ).astype(BF16)
                for i in range(nx):
                    out_ref[i, start : start + 2 * capacity, p * span : (p + 1) * span] = piece


def repack_kernel(capacity, parts, in_ref, out_ref):
    nx, rows, wide = in_ref.shape
    span = wide // parts
    for pair in range(0, rows // capacity, 2):
        here = slice(pair * capacity, (pair + 2) * capacity)
        total = in_ref[0, here, :].astype(F32)
        for i in range(1, nx):
            total += in_ref[i, here, :].astype(F32)
        for half in range(2):
            block = total[half * capacity : (half + 1) * capacity]
            pieces = [block[:, p * span : (p + 1) * span] for p in range(parts)]
            pieces.append(jnp.zeros((LANES - parts * capacity, span), F32))
            turned = jnp.concatenate(pieces, axis=0).T.astype(BF16)
            z = pair + half
            out_ref[:, z] = turned.reshape(out_ref.shape[0], out_ref.shape[2], FINE, LANES)


def order_kernel(*refs):
    core = lax.axis_index("c")
    srcs, own, sent, sems = refs[:3], refs[3:6], refs[6:9], refs[9]
    copies = []
    for outs, c in ((own, core), (sent, 1 - core)):
        for src, out_ref in zip(srcs, outs):
            for yb in range(2):
                for xb in range(2):
                    for p in range(src.shape[5]):
                        copies.append(
                            pltpu.make_async_copy(
                                src.at[:, yb, :, xb, c, p],
                                out_ref.at[2 * yb + xb, p],
                                sems.at[len(copies)],
                            )
                        )
    for copy in copies:
        copy.start()
    for copy in copies:
        copy.wait()


def project_kernel(in_ref, gate_ref, up_ref, down_ref, out_ref):
    members = in_ref.shape[0]
    rows = out_ref.shape[0]
    hidden = gate_ref.shape[1]
    x = jnp.concatenate([in_ref[i, :rows, :] for i in range(members)], axis=1)
    out_ref[:, :hidden] = jnp.dot(x, gate_ref[...], preferred_element_type=F32)
    out_ref[:, hidden : 2 * hidden] = jnp.dot(x, up_ref[...], preferred_element_type=F32)
    g = jnp.concatenate([in_ref[i, rows:, :] for i in range(members)], axis=1)
    out_ref[:, 2 * hidden :] = jnp.dot(g, down_ref[...], preferred_element_type=F32)


def tail_kernel(a_ref, b_ref, out_ref):
    hidden = a_ref.shape[1] // 3
    gate, upper, back = (
        a_ref[:, k * hidden : (k + 1) * hidden] + b_ref[:, k * hidden : (k + 1) * hidden]
        for k in range(3)
    )
    d_gate, d_upper = backward_tail(gate, upper, back)
    out_ref[:, :hidden] = d_gate
    out_ref[:, hidden:] = d_upper


def return_part(d_ref, gate_ref, up_ref, here):
    hidden = gate_ref.shape[1]
    across = (((1,), (1,)), ((), ()))
    part = lax.dot_general(
        d_ref[:, :hidden], gate_ref[here, :], across, preferred_element_type=F32
    )
    return part + lax.dot_general(
        d_ref[:, hidden:], up_ref[here, :], across, preferred_element_type=F32
    )


def return_kernel(d_ref, gate_ref, up_ref, out_ref):
    out_ref[...] = return_part(d_ref, gate_ref, up_ref, slice(None))


def return_add_kernel(d_ref, gate_ref, up_ref, sum_ref, out_ref):
    members, _, wide = out_ref.shape
    for i in range(members):
        here = slice(i * wide, (i + 1) * wide)
        part = return_part(d_ref, gate_ref, up_ref, here)
        out_ref[i] = (part + sum_ref[:, here]).astype(out_ref.dtype)


def combine_kernel(capacity, parts, ids_ref, prob_ref, scale_ref, out_ref):
    lanes, tokens = out_ref.shape
    experts = lanes // LANES
    slots, first = token_slots(ids_ref[...].astype(F32), experts)
    weights = jnp.where(first, prob_ref[0:1, :], prob_ref[1:2, :]) * scale_ref[...]
    slot_of_lane = lane_slots(tokens, capacity, parts)
    for z in range(experts):
        out_ref[z * LANES : (z + 1) * LANES, :] = jnp.where(
            slots[z : z + 1] == slot_of_lane, weights[z : z + 1], 0.0
        )


def final_kernel(capacity, parts, combine_ref, in_ref, out_ref):
    lanes = combine_ref.shape[0]
    nz = lanes // LANES
    sums = []
    for z in range(nz):
        total = jnp.zeros((FINE, LANES), F32)
        for ya in range(in_ref.shape[0]):
            for xa in range(in_ref.shape[2]):
                total += in_ref[ya, z, xa].astype(F32)
        sums.append(total)
    sums = jnp.concatenate(sums, axis=1)
    part = lane_parts(sums.shape, 1, capacity)
    spread = jnp.concatenate([jnp.where(part == p, sums, 0.0) for p in range(parts)], axis=0)
    out_ref[...] = lax.dot_general(
        spread,
        combine_ref[...],
        (((1,), (0,)), ((), ())),
        precision=lax.Precision.HIGHEST,
        preferred_element_type=F32,
    ).astype(out_ref.dtype)


def call(kernel, shape, dtype, *operands, flops=0):
    moved = sum(o.size * o.dtype.itemsize for o in operands)
    moved += math.prod(shape) * jnp.dtype(dtype).itemsize
    return pl.pallas_call(
        kernel,
        out_shape=jax.ShapeDtypeStruct(shape, dtype),
        in_specs=[pl.BlockSpec(memory_space=pltpu.VMEM)] * len(operands),
        out_specs=pl.BlockSpec(memory_space=pltpu.VMEM),
        compiler_params=pltpu.CompilerParams(vmem_limit_bytes=VMEM_LIMIT),
        cost_estimate=pl.CostEstimate(flops=flops, bytes_accessed=moved, transcendentals=0),
    )(*operands)


def exchange_groups(nz, ny, nx, nc):
    def index(z, y, x, c):
        return ((z * ny + y % ny) * nx + x % nx) * nc + c

    halves = [(yb, xb) for yb in range(2) for xb in range(2)]
    places = [(2 * ya, 2 * xa) for ya in range(ny // 2) for xa in range(nx // 2)]
    far = [
        [
            index(z, 2 * ya + yb, 2 * xa + xb, c)
            for ya in range(ny // 2)
            for z in range(nz)
            for xa in range(nx // 2)
        ]
        for c in range(nc)
        for yb, xb in halves
    ]
    near = [
        [index(z, y + c + (yb + c) % 2, x + c + (xb + c) % 2, c) for yb, xb in halves]
        for z in range(nz)
        for c in range(nc)
        for y, x in places
    ]
    return far, near


def swap(blocks, groups):
    return lax.all_to_all(
        blocks, AXES, split_axis=0, concat_axis=0, axis_index_groups=groups, tiled=True
    )


def other_core(values):
    return lax.ppermute(values, "c", [(0, 1), (1, 0)])


def shards(activations, out_grad, token_scale, route_prob, route_ids, w_gate, w_up, w_down):
    nz, ny, nx, nc = (lax.axis_size(a) for a in AXES)
    far, near = exchange_groups(nz, ny, nx, nc)
    spread = ny * nx // 4
    members = 4
    core = lax.axis_index("c")
    tokens, feats = activations.shape
    capacity = min(tokens, 5 * tokens // (2 * nz))
    parts = feats // FINE
    hidden = w_gate.shape[2]
    rows = nz * capacity
    wide = feats * spread

    heads = [route_ids.T, activations.T, out_grad.T]
    send = pl.pallas_call(
        functools.partial(pack_kernel, capacity),
        out_shape=jax.ShapeDtypeStruct((ny // 2, nz, nx // 2, 2 * FINE, LANES), BF16),
        in_specs=[pl.BlockSpec(memory_space=pl.ANY)] * 3,
        out_specs=pl.BlockSpec(memory_space=pltpu.VMEM),
        scratch_shapes=[pltpu.VMEM(h.shape, h.dtype) for h in heads]
        + [pltpu.SemaphoreType.DMA((3,))],
        compiler_params=pltpu.CompilerParams(vmem_limit_bytes=VMEM_LIMIT),
    )(*(pltpu.with_memory_space_constraint(h, pltpu.HBM) for h in heads))
    got = swap(send.reshape(nz * spread, 2 * FINE, LANES), far)

    views = (ny // 2, 2, nx // 2, 2, nc, parts, FINE, hidden)
    ordered = (members, parts, ny // 2, nx // 2, FINE, hidden)
    weights = pl.pallas_call(
        order_kernel,
        out_shape=[pltpu.HBM(ordered, BF16)] * 3 + [jax.ShapeDtypeStruct(ordered, BF16)] * 3,
        in_specs=[pl.BlockSpec(memory_space=pl.ANY)] * 3,
        out_specs=[pl.BlockSpec(memory_space=m) for m in [pltpu.HBM] * 3 + [pltpu.VMEM] * 3],
        scratch_shapes=[pltpu.SemaphoreType.DMA((2 * 3 * members * parts,))],
        compiler_params=pltpu.CompilerParams(vmem_limit_bytes=VMEM_LIMIT),
        cost_estimate=pl.CostEstimate(flops=0, bytes_accessed=12 * 1024 * 1024, transcendentals=0),
    )(
        pltpu.with_memory_space_constraint(w_gate.reshape(views), pltpu.HBM),
        pltpu.with_memory_space_constraint(w_up.reshape(views), pltpu.HBM),
        w_down[0].T.reshape(views),
    )
    weights = [w.reshape(members * wide, hidden) for w in weights]
    own, other = weights[:3], [other_core(w) for w in weights[3:]]
    got, own, other = lax.optimization_barrier((got, own, other))

    copies = call(
        functools.partial(unpack_kernel, capacity, parts),
        (members, 2 * rows, wide),
        BF16,
        got.reshape(ny // 2, nz, nx // 2, 2 * FINE, LANES),
    )
    block = swap(copies, near)

    flops = 2 * rows * members * wide * 3 * hidden

    def project(w):
        return call(project_kernel, (rows, 3 * hidden), F32, block, *w, flops=flops)

    def tail(a, b):
        return call(tail_kernel, (rows, 2 * hidden), BF16, a, b)

    part_other = project(other)
    rest_own = other_core(part_other)
    part_own = project(own)
    rest_other = other_core(part_own)
    d_own = tail(part_own, rest_own)
    flops = flops // 3 * 2
    part = call(return_kernel, (rows, members * wide), F32, d_own, *own[:2], flops=flops)
    combine = call(
        functools.partial(combine_kernel, capacity, parts),
        (nz * LANES, tokens),
        F32,
        route_ids.T,
        route_prob.T,
        token_scale.reshape(1, tokens),
    )
    part, combine = lax.optimization_barrier((part, combine))
    d_other = tail(part_other, rest_other)
    part = call(
        return_add_kernel, (members, rows, wide), BF16, d_other, *other[:2], part, flops=flops
    )
    part = swap(part, near)
    part = call(
        functools.partial(repack_kernel, capacity, parts),
        (ny // 2, nz, nx // 2, FINE, LANES),
        BF16,
        part,
    )
    part = swap(part.reshape(nz * spread, FINE, LANES), far)
    return call(
        functools.partial(final_kernel, capacity, parts),
        (feats, tokens),
        BF16,
        combine,
        part.reshape(ny // 2, nz, nx // 2, FINE, LANES),
    ).T


def solution(mesh):
    devices = mesh.devices
    fine = Mesh(devices.reshape(devices.shape[0], 8, 4, 2), AXES)
    tensor = ("y", "x", "c")
    placed = (
        P("z", tensor),
        P("z", tensor),
        P("z"),
        P("z", None),
        P("z", None),
        P("z", None, tensor),
        P("z", None, tensor),
        P("z", tensor, None),
    )
    return jax.shard_map(
        shards, mesh=fine, in_specs=placed, out_specs=P("z", tensor), check_vma=False
    )
```

```python
import functools
import math

import jax
import jax.numpy as jnp
from jax import lax
from jax.experimental import pallas as pl
from jax.experimental.pallas import tpu as pltpu
from jax.sharding import Mesh, PartitionSpec as P

BF16 = jnp.bfloat16
F32 = jnp.float32
LANES = 128
FINE = 16
VMEM_LIMIT = 16 * 1024 * 1024
AXES = ("z", "y", "x", "c")


def backward_tail(gate, upper, back):
    sigmoid_g = jax.nn.sigmoid(gate)
    slope = sigmoid_g * (1.0 + gate * (1.0 - sigmoid_g))
    d_gate = (back * upper * slope).astype(BF16)
    d_upper = (back * gate * sigmoid_g).astype(BF16)
    return d_gate, d_upper


def lane_parts(shape, axis, capacity):
    inner = lax.broadcasted_iota(jnp.int32, shape, axis) % LANES
    return inner // capacity


def lane_slots(tokens, capacity, parts):
    inner = lax.broadcasted_iota(jnp.int32, (LANES, tokens), 0)
    part = inner // capacity
    return jnp.where(part < parts, inner - part * capacity, -1).astype(F32)


def token_slots(ids, experts):
    tokens = ids.shape[1]
    expert = lax.broadcasted_iota(jnp.int32, (experts, tokens), 0).astype(F32)
    first = ids[0:1, :] == expert
    hit = first | (ids[1:2, :] == expert)
    row = lax.broadcasted_iota(jnp.int32, (tokens, tokens), 0)
    col = lax.broadcasted_iota(jnp.int32, (tokens, tokens), 1)
    earlier = jnp.where(row < col, 1.0, 0.0).astype(BF16)
    hit_bf = jnp.where(hit, 1.0, 0.0).astype(BF16)
    before = jnp.dot(hit_bf, earlier, preferred_element_type=F32)
    return jnp.where(hit, before, -2.0), first


def pack_kernel(capacity, ids_hbm, x_hbm, g_hbm, out_ref, ids_ref, x_ref, g_ref, sems):
    copies = [
        pltpu.make_async_copy(src, dst, sems.at[i])
        for i, (src, dst) in enumerate(((ids_hbm, ids_ref), (x_hbm, x_ref), (g_hbm, g_ref)))
    ]
    for copy in copies:
        copy.start()
    nya, nz, nxa = out_ref.shape[:3]
    feats, tokens = x_ref.shape
    parts = feats // FINE
    lanes = nz * LANES
    part = lane_parts((FINE, lanes), 1, capacity)
    slot_of_lane = lane_slots(tokens, capacity, parts)
    copies[0].wait()
    slots, _ = token_slots(ids_ref[...].astype(F32), nz)
    place = jnp.concatenate(
        [jnp.where(slots[z : z + 1] == slot_of_lane, 1.0, 0.0).astype(BF16) for z in range(nz)],
        axis=0,
    )
    for kind, ref in enumerate((x_ref, g_ref)):
        copies[1 + kind].wait()
        spread = lax.dot_general(
            ref[...],
            place,
            (((1,), (1,)), ((), ())),
            preferred_element_type=F32,
        )
        block = jnp.zeros((FINE, lanes), F32)
        for p in range(parts):
            block = jnp.where(part == p, spread[p * FINE : (p + 1) * FINE], block)
        block = block.astype(BF16)
        for z in range(nz):
            piece = block[:, z * LANES : (z + 1) * LANES]
            for ya in range(nya):
                for xa in range(nxa):
                    out_ref[ya, z, xa, kind * FINE : (kind + 1) * FINE, :] = piece


def unpack_kernel(capacity, parts, in_ref, out_ref):
    nx, _, wide = out_ref.shape
    nz = in_ref.shape[1]
    span = wide // parts
    rows = nz * capacity
    for kind in range(2):
        for pair in range(0, nz, 2):
            turned = []
            for z in (pair, pair + 1):
                block = in_ref[:, z, :, kind * FINE : (kind + 1) * FINE, :]
                turned.append(block.reshape(span, LANES).astype(F32).T)
            start = kind * rows + pair * capacity
            for p in range(parts):
                piece = jnp.concatenate(
                    [t[p * capacity : (p + 1) * capacity] for t in turned], axis=0
                ).astype(BF16)
                for i in range(nx):
                    out_ref[i, start : start + 2 * capacity, p * span : (p + 1) * span] = piece


def repack_kernel(capacity, parts, in_ref, out_ref):
    nx, rows, wide = in_ref.shape
    span = wide // parts
    for pair in range(0, rows // capacity, 2):
        here = slice(pair * capacity, (pair + 2) * capacity)
        total = in_ref[0, here, :].astype(F32)
        for i in range(1, nx):
            total += in_ref[i, here, :].astype(F32)
        for half in range(2):
            block = total[half * capacity : (half + 1) * capacity]
            pieces = [block[:, p * span : (p + 1) * span] for p in range(parts)]
            pieces.append(jnp.zeros((LANES - parts * capacity, span), F32))
            turned = jnp.concatenate(pieces, axis=0).T.astype(BF16)
            z = pair + half
            out_ref[:, z] = turned.reshape(out_ref.shape[0], out_ref.shape[2], FINE, LANES)


def gather(src, half, dst, sems, first):
    copies = []
    for member in range(4):
        for p in range(src.shape[5]):
            copies.append(
                pltpu.make_async_copy(
                    src.at[:, member // 2, :, member % 2, half, p],
                    dst.at[member, p],
                    sems.at[first + len(copies)],
                )
            )
    for copy in copies:
        copy.start()
    return copies


def order_kernel(kept, *refs):
    core = lax.axis_index("c")
    sent, out_refs = len(kept[0]), len(kept[0]) + len(kept[1])
    sources = refs[: kept[2]]
    outs = refs[kept[2] : kept[2] + out_refs]
    sems = refs[kept[2] + out_refs]
    held = refs[kept[2] + out_refs + 1 :]
    waits, each = [], 4 * sources[0].shape[5]
    for i, k in enumerate(kept[0]):
        waits += gather(sources[k], 1 - core, outs[i], sems, i * each)
    own = [
        gather(sources[k], core, held[i], sems, (sent + i) * each) for i, k in enumerate(kept[1])
    ]
    for i, copies in enumerate(own):
        for copy in copies:
            copy.wait()
        copy = pltpu.make_async_copy(held[i], outs[sent + i], sems.at[out_refs * each + i])
        copy.start()
        waits.append(copy)
    for copy in waits:
        copy.wait()


def project_kernel(in_ref, gate_ref, up_ref, down_ref, out_ref):
    members = in_ref.shape[0]
    rows = out_ref.shape[0]
    hidden = gate_ref.shape[1]
    x = jnp.concatenate([in_ref[i, :rows, :] for i in range(members)], axis=1)
    out_ref[:, :hidden] = jnp.dot(x, gate_ref[...], preferred_element_type=F32)
    out_ref[:, hidden : 2 * hidden] = jnp.dot(x, up_ref[...], preferred_element_type=F32)
    g = jnp.concatenate([in_ref[i, rows:, :] for i in range(members)], axis=1)
    out_ref[:, 2 * hidden :] = jnp.dot(g, down_ref[...], preferred_element_type=F32)


def tail_kernel(a_ref, b_ref, out_ref):
    hidden = a_ref.shape[1] // 3
    gate, upper, back = (
        a_ref[:, k * hidden : (k + 1) * hidden] + b_ref[:, k * hidden : (k + 1) * hidden]
        for k in range(3)
    )
    d_gate, d_upper = backward_tail(gate, upper, back)
    out_ref[:, :hidden] = d_gate
    out_ref[:, hidden:] = d_upper


def return_part(d_ref, gate_ref, up_ref, here):
    hidden = gate_ref.shape[1]
    across = (((1,), (1,)), ((), ()))
    part = lax.dot_general(
        d_ref[:, :hidden], gate_ref[here, :], across, preferred_element_type=F32
    )
    return part + lax.dot_general(
        d_ref[:, hidden:], up_ref[here, :], across, preferred_element_type=F32
    )


def return_kernel(d_ref, gate_ref, up_ref, out_ref):
    out_ref[...] = return_part(d_ref, gate_ref, up_ref, slice(None))


def return_add_kernel(d_ref, gate_ref, up_ref, sum_ref, out_ref):
    members, _, wide = out_ref.shape
    for i in range(members):
        here = slice(i * wide, (i + 1) * wide)
        part = return_part(d_ref, gate_ref, up_ref, here)
        out_ref[i] = (part + sum_ref[:, here]).astype(out_ref.dtype)


def combine_kernel(capacity, parts, ids_ref, prob_ref, scale_ref, out_ref):
    lanes, tokens = out_ref.shape
    experts = lanes // LANES
    slots, first = token_slots(ids_ref[...].astype(F32), experts)
    weights = jnp.where(first, prob_ref[0:1, :], prob_ref[1:2, :]) * scale_ref[...]
    slot_of_lane = lane_slots(tokens, capacity, parts)
    for z in range(experts):
        out_ref[z * LANES : (z + 1) * LANES, :] = jnp.where(
            slots[z : z + 1] == slot_of_lane, weights[z : z + 1], 0.0
        )


def final_kernel(capacity, parts, combine_ref, in_ref, out_ref):
    lanes = combine_ref.shape[0]
    nz = lanes // LANES
    sums = []
    for z in range(nz):
        total = jnp.zeros((FINE, LANES), F32)
        for ya in range(in_ref.shape[0]):
            for xa in range(in_ref.shape[2]):
                total += in_ref[ya, z, xa].astype(F32)
        sums.append(total)
    sums = jnp.concatenate(sums, axis=1)
    part = lane_parts(sums.shape, 1, capacity)
    spread = jnp.concatenate([jnp.where(part == p, sums, 0.0) for p in range(parts)], axis=0)
    out_ref[...] = lax.dot_general(
        spread,
        combine_ref[...],
        (((1,), (0,)), ((), ())),
        precision=lax.Precision.HIGHEST,
        preferred_element_type=F32,
    ).astype(out_ref.dtype)


def call(kernel, shape, dtype, *operands, flops=0):
    moved = sum(o.size * o.dtype.itemsize for o in operands)
    moved += math.prod(shape) * jnp.dtype(dtype).itemsize
    return pl.pallas_call(
        kernel,
        out_shape=jax.ShapeDtypeStruct(shape, dtype),
        in_specs=[pl.BlockSpec(memory_space=pltpu.VMEM)] * len(operands),
        out_specs=pl.BlockSpec(memory_space=pltpu.VMEM),
        compiler_params=pltpu.CompilerParams(vmem_limit_bytes=VMEM_LIMIT),
        cost_estimate=pl.CostEstimate(flops=flops, bytes_accessed=moved, transcendentals=0),
    )(*operands)


def exchange_groups(nz, ny, nx, nc):
    def index(z, y, x, c):
        return ((z * ny + y % ny) * nx + x % nx) * nc + c

    halves = [(yb, xb) for yb in range(2) for xb in range(2)]
    places = [(2 * ya, 2 * xa) for ya in range(ny // 2) for xa in range(nx // 2)]
    far = [
        [
            index(z, 2 * ya + yb, 2 * xa + xb, c)
            for ya in range(ny // 2)
            for z in range(nz)
            for xa in range(nx // 2)
        ]
        for c in range(nc)
        for yb, xb in halves
    ]
    near = [
        [index(z, y + c + (yb + c) % 2, x + c + (xb + c) % 2, c) for yb, xb in halves]
        for z in range(nz)
        for c in range(nc)
        for y, x in places
    ]
    return far, near


def swap(blocks, groups):
    return lax.all_to_all(
        blocks, AXES, split_axis=0, concat_axis=0, axis_index_groups=groups, tiled=True
    )


def other_core(values):
    return lax.ppermute(values, "c", [(0, 1), (1, 0)])


def shards(activations, out_grad, token_scale, route_prob, route_ids, w_gate, w_up, w_down):
    nz, ny, nx, nc = (lax.axis_size(a) for a in AXES)
    far, near = exchange_groups(nz, ny, nx, nc)
    spread = ny * nx // 4
    members = 4
    core = lax.axis_index("c")
    tokens, feats = activations.shape
    capacity = min(tokens, 5 * tokens // (2 * nz))
    parts = feats // FINE
    hidden = w_gate.shape[2]
    rows = nz * capacity
    wide = feats * spread

    heads = [route_ids.T, activations.T, out_grad.T]
    send = pl.pallas_call(
        functools.partial(pack_kernel, capacity),
        out_shape=jax.ShapeDtypeStruct((ny // 2, nz, nx // 2, 2 * FINE, LANES), BF16),
        in_specs=[pl.BlockSpec(memory_space=pl.ANY)] * 3,
        out_specs=pl.BlockSpec(memory_space=pltpu.VMEM),
        scratch_shapes=[pltpu.VMEM(h.shape, h.dtype) for h in heads]
        + [pltpu.SemaphoreType.DMA((3,))],
        compiler_params=pltpu.CompilerParams(vmem_limit_bytes=VMEM_LIMIT),
    )(*(pltpu.with_memory_space_constraint(h, pltpu.HBM) for h in heads))
    got = swap(send.reshape(nz * spread, 2 * FINE, LANES), far)

    views = (ny // 2, 2, nx // 2, 2, nc, parts, FINE, hidden)
    ordered = (members, parts, ny // 2, nx // 2, FINE, hidden)
    gate, up = (
        pltpu.with_memory_space_constraint(w.reshape(views), pltpu.HBM) for w in (w_gate, w_up)
    )
    down = w_down[0].T.reshape(views)

    def order(sent, kept, *sources):
        spaces = [pltpu.VMEM] * len(sent) + [pltpu.HBM] * len(kept)
        count = len(spaces) * members * parts + len(kept)
        ordered_weights = pl.pallas_call(
            functools.partial(order_kernel, (sent, kept, len(sources))),
            out_shape=[space(ordered, BF16) for space in spaces],
            in_specs=[pl.BlockSpec(memory_space=pl.ANY)] * len(sources),
            out_specs=[pl.BlockSpec(memory_space=space) for space in spaces],
            scratch_shapes=[pltpu.SemaphoreType.DMA((count,))]
            + [pltpu.VMEM(ordered, BF16)] * len(kept),
            compiler_params=pltpu.CompilerParams(vmem_limit_bytes=VMEM_LIMIT),
            cost_estimate=pl.CostEstimate(
                flops=0, bytes_accessed=6 * 1024 * 1024, transcendentals=0
            ),
        )(*sources)
        return [w.reshape(members * wide, hidden) for w in ordered_weights]

    *sent, own_down = order((0, 1, 2), (2,), gate, up, down)
    own = [*order((), (0, 1), gate, up), own_down]
    other = [other_core(w) for w in sent]
    got, own, other = lax.optimization_barrier((got, own, other))

    copies = call(
        functools.partial(unpack_kernel, capacity, parts),
        (members, 2 * rows, wide),
        BF16,
        got.reshape(ny // 2, nz, nx // 2, 2 * FINE, LANES),
    )
    block = swap(copies, near)

    flops = 2 * rows * members * wide * 3 * hidden

    def project(w):
        return call(project_kernel, (rows, 3 * hidden), F32, block, *w, flops=flops)

    def tail(a, b):
        return call(tail_kernel, (rows, 2 * hidden), BF16, a, b)

    part_other = project(other)
    rest_own = other_core(part_other)
    part_own = project(own)
    rest_other = other_core(part_own)
    d_own = tail(part_own, rest_own)
    flops = flops // 3 * 2
    part = call(return_kernel, (rows, members * wide), F32, d_own, *own[:2], flops=flops)
    combine = call(
        functools.partial(combine_kernel, capacity, parts),
        (nz * LANES, tokens),
        F32,
        route_ids.T,
        route_prob.T,
        token_scale.reshape(1, tokens),
    )
    part, combine = lax.optimization_barrier((part, combine))
    d_other = tail(part_other, rest_other)
    part = call(
        return_add_kernel, (members, rows, wide), BF16, d_other, *other[:2], part, flops=flops
    )
    part = swap(part, near)
    part = call(
        functools.partial(repack_kernel, capacity, parts),
        (ny // 2, nz, nx // 2, FINE, LANES),
        BF16,
        part,
    )
    part = swap(part.reshape(nz * spread, FINE, LANES), far)
    return call(
        functools.partial(final_kernel, capacity, parts),
        (feats, tokens),
        BF16,
        combine,
        part.reshape(ny // 2, nz, nx // 2, FINE, LANES),
    ).T


def solution(mesh):
    devices = mesh.devices
    fine = Mesh(devices.reshape(devices.shape[0], 8, 4, 2), AXES)
    tensor = ("y", "x", "c")
    placed = (
        P("z", tensor),
        P("z", tensor),
        P("z"),
        P("z", None),
        P("z", None),
        P("z", None, tensor),
        P("z", None, tensor),
        P("z", tensor, None),
    )
    return jax.shard_map(
        shards, mesh=fine, in_specs=placed, out_specs=P("z", tensor), check_vma=False
    )
```

```python
import functools
import math

import jax
import jax.numpy as jnp
from jax import lax
from jax.experimental import pallas as pl
from jax.experimental.pallas import tpu as pltpu
from jax.sharding import Mesh, PartitionSpec as P

BF16 = jnp.bfloat16
F32 = jnp.float32
LANES = 128
FINE = 16
VMEM_LIMIT = 16 * 1024 * 1024
AXES = ("z", "y", "x", "c")


def backward_tail(gate, upper, back):
    sigmoid_g = jax.nn.sigmoid(gate)
    slope = sigmoid_g * (1.0 + gate * (1.0 - sigmoid_g))
    d_gate = (back * upper * slope).astype(BF16)
    d_upper = (back * gate * sigmoid_g).astype(BF16)
    return d_gate, d_upper


def lane_parts(shape, axis, capacity):
    inner = lax.broadcasted_iota(jnp.int32, shape, axis) % LANES
    return inner // capacity


def lane_slots(tokens, capacity, parts):
    inner = lax.broadcasted_iota(jnp.int32, (LANES, tokens), 0)
    part = inner // capacity
    return jnp.where(part < parts, inner - part * capacity, -1).astype(F32)


def token_slots(ids, experts):
    tokens = ids.shape[1]
    expert = lax.broadcasted_iota(jnp.int32, (experts, tokens), 0).astype(F32)
    first = ids[0:1, :] == expert
    hit = first | (ids[1:2, :] == expert)
    row = lax.broadcasted_iota(jnp.int32, (tokens, tokens), 0)
    col = lax.broadcasted_iota(jnp.int32, (tokens, tokens), 1)
    earlier = jnp.where(row < col, 1.0, 0.0).astype(BF16)
    hit_bf = jnp.where(hit, 1.0, 0.0).astype(BF16)
    before = jnp.dot(hit_bf, earlier, preferred_element_type=F32)
    return jnp.where(hit, before, -2.0), first


def pack_kernel(capacity, ids_hbm, x_hbm, g_hbm, out_hbm, ids_ref, x_ref, g_ref, held, sems):
    copies = [
        pltpu.make_async_copy(src, dst, sems.at[i])
        for i, (src, dst) in enumerate(((ids_hbm, ids_ref), (x_hbm, x_ref), (g_hbm, g_ref)))
    ]
    for copy in copies:
        copy.start()
    nya, nz, nxa = out_hbm.shape[:3]
    feats, tokens = x_ref.shape
    parts = feats // FINE
    lanes = nz * LANES
    part = lane_parts((FINE, lanes), 1, capacity)
    slot_of_lane = lane_slots(tokens, capacity, parts)
    copies[0].wait()
    slots, _ = token_slots(ids_ref[...].astype(F32), nz)
    place = jnp.concatenate(
        [jnp.where(slots[z : z + 1] == slot_of_lane, 1.0, 0.0).astype(BF16) for z in range(nz)],
        axis=0,
    )
    for kind, ref in enumerate((x_ref, g_ref)):
        copies[1 + kind].wait()
        spread = lax.dot_general(
            ref[...],
            place,
            (((1,), (1,)), ((), ())),
            preferred_element_type=F32,
        )
        block = jnp.zeros((FINE, lanes), F32)
        for p in range(parts):
            block = jnp.where(part == p, spread[p * FINE : (p + 1) * FINE], block)
        block = block.astype(BF16)
        here = pl.ds(kind * FINE, FINE)
        for z in range(nz):
            held[z, kind * FINE : (kind + 1) * FINE, :] = block[:, z * LANES : (z + 1) * LANES]
        for ya in range(nya):
            for xa in range(nxa):
                copies.append(
                    pltpu.make_async_copy(
                        held.at[:, here], out_hbm.at[ya, :, xa, here], sems.at[len(copies)]
                    )
                )
                copies[-1].start()
    for copy in copies[3:]:
        copy.wait()


def unpack_kernel(capacity, parts, in_ref, out_ref):
    nx, _, wide = out_ref.shape
    nz = in_ref.shape[1]
    span = wide // parts
    rows = nz * capacity
    for kind in range(2):
        for pair in range(0, nz, 2):
            turned = []
            for z in (pair, pair + 1):
                block = in_ref[:, z, :, kind * FINE : (kind + 1) * FINE, :]
                turned.append(block.reshape(span, LANES).astype(F32).T)
            start = kind * rows + pair * capacity
            for p in range(parts):
                piece = jnp.concatenate(
                    [t[p * capacity : (p + 1) * capacity] for t in turned], axis=0
                ).astype(BF16)
                for i in range(nx):
                    out_ref[i, start : start + 2 * capacity, p * span : (p + 1) * span] = piece


def repack_kernel(capacity, parts, in_ref, out_ref):
    nx, rows, wide = in_ref.shape
    span = wide // parts
    for pair in range(0, rows // capacity, 2):
        here = slice(pair * capacity, (pair + 2) * capacity)
        total = in_ref[0, here, :].astype(F32)
        for i in range(1, nx):
            total += in_ref[i, here, :].astype(F32)
        for half in range(2):
            block = total[half * capacity : (half + 1) * capacity]
            pieces = [block[:, p * span : (p + 1) * span] for p in range(parts)]
            pieces.append(jnp.zeros((LANES - parts * capacity, span), F32))
            turned = jnp.concatenate(pieces, axis=0).T.astype(BF16)
            z = pair + half
            out_ref[:, z] = turned.reshape(out_ref.shape[0], out_ref.shape[2], FINE, LANES)


def gather(src, half, dst, sems, first):
    copies = []
    for member in range(4):
        for p in range(src.shape[5]):
            copies.append(
                pltpu.make_async_copy(
                    src.at[:, member // 2, :, member % 2, half, p],
                    dst.at[member, p],
                    sems.at[first + len(copies)],
                )
            )
    for copy in copies:
        copy.start()
    return copies


def order_kernel(kept, *refs):
    core = lax.axis_index("c")
    sent, out_refs = len(kept[0]), len(kept[0]) + len(kept[1])
    sources = refs[: kept[2]]
    outs = refs[kept[2] : kept[2] + out_refs]
    sems = refs[kept[2] + out_refs]
    held = refs[kept[2] + out_refs + 1 :]
    waits, each = [], 4 * sources[0].shape[5]
    for i, k in enumerate(kept[0]):
        waits += gather(sources[k], 1 - core, outs[i], sems, i * each)
    own = [
        gather(sources[k], core, held[i], sems, (sent + i) * each) for i, k in enumerate(kept[1])
    ]
    for i, copies in enumerate(own):
        for copy in copies:
            copy.wait()
        copy = pltpu.make_async_copy(held[i], outs[sent + i], sems.at[out_refs * each + i])
        copy.start()
        waits.append(copy)
    for copy in waits:
        copy.wait()


def project_kernel(in_ref, gate_ref, up_ref, down_ref, out_ref):
    members = in_ref.shape[0]
    rows = out_ref.shape[0]
    hidden = gate_ref.shape[1]
    x = jnp.concatenate([in_ref[i, :rows, :] for i in range(members)], axis=1)
    out_ref[:, :hidden] = jnp.dot(x, gate_ref[...], preferred_element_type=F32)
    out_ref[:, hidden : 2 * hidden] = jnp.dot(x, up_ref[...], preferred_element_type=F32)
    g = jnp.concatenate([in_ref[i, rows:, :] for i in range(members)], axis=1)
    out_ref[:, 2 * hidden :] = jnp.dot(g, down_ref[...], preferred_element_type=F32)


def return_part(a_ref, b_ref, gate_ref, up_ref):
    hidden = gate_ref.shape[1]
    gate, upper, back = (
        a_ref[:, k * hidden : (k + 1) * hidden] + b_ref[:, k * hidden : (k + 1) * hidden]
        for k in range(3)
    )
    d_gate, d_upper = backward_tail(gate, upper, back)
    across = (((1,), (1,)), ((), ()))
    part = lax.dot_general(d_gate, gate_ref[...], across, preferred_element_type=F32)
    return part + lax.dot_general(d_upper, up_ref[...], across, preferred_element_type=F32)


def return_kernel(a_ref, b_ref, gate_ref, up_ref, out_ref):
    out_ref[...] = return_part(a_ref, b_ref, gate_ref, up_ref)


def return_add_kernel(a_ref, b_ref, gate_ref, up_ref, sum_ref, out_ref):
    members, _, wide = out_ref.shape
    part = (return_part(a_ref, b_ref, gate_ref, up_ref) + sum_ref[...]).astype(out_ref.dtype)
    for i in range(members):
        out_ref[i] = part[:, i * wide : (i + 1) * wide]


def two_parts(values):
    high = values.astype(BF16)
    return high, (values - high.astype(F32)).astype(BF16)


def combine_kernel(capacity, parts, ids_ref, prob_ref, scale_ref, out_ref):
    _, lanes, tokens = out_ref.shape
    experts = lanes // LANES
    slots, first = token_slots(ids_ref[...].astype(F32), experts)
    weights = jnp.where(first, prob_ref[0:1, :], prob_ref[1:2, :]) * scale_ref[...]
    slot_of_lane = lane_slots(tokens, capacity, parts)
    for z in range(experts):
        here = slice(z * LANES, (z + 1) * LANES)
        weight = jnp.where(slots[z : z + 1] == slot_of_lane, weights[z : z + 1], 0.0)
        out_ref[0, here, :], out_ref[1, here, :] = two_parts(weight)


def final_kernel(capacity, parts, combine_ref, in_ref, out_ref):
    nz = combine_ref.shape[1] // LANES
    feats = out_ref.shape[0]
    sums = []
    for z in range(nz):
        total = jnp.zeros((FINE, LANES), F32)
        for ya in range(in_ref.shape[0]):
            for xa in range(in_ref.shape[2]):
                total += in_ref[ya, z, xa].astype(F32)
        sums.append(total)
    sums = jnp.concatenate(sums, axis=1)
    part = lane_parts(sums.shape, 1, capacity)
    spread = jnp.concatenate([jnp.where(part == p, sums, 0.0) for p in range(parts)], axis=0)
    high, low = two_parts(spread)
    first = jnp.dot(
        jnp.concatenate([high, low], axis=0), combine_ref[0], preferred_element_type=F32
    )
    second = jnp.dot(high, combine_ref[1], preferred_element_type=F32)
    out_ref[...] = (first[:feats] + first[feats:] + second).astype(out_ref.dtype)


def call(kernel, shape, dtype, *operands, flops=0):
    moved = sum(o.size * o.dtype.itemsize for o in operands)
    moved += math.prod(shape) * jnp.dtype(dtype).itemsize
    return pl.pallas_call(
        kernel,
        out_shape=jax.ShapeDtypeStruct(shape, dtype),
        in_specs=[pl.BlockSpec(memory_space=pltpu.VMEM)] * len(operands),
        out_specs=pl.BlockSpec(memory_space=pltpu.VMEM),
        compiler_params=pltpu.CompilerParams(vmem_limit_bytes=VMEM_LIMIT),
        cost_estimate=pl.CostEstimate(flops=flops, bytes_accessed=moved, transcendentals=0),
    )(*operands)


def exchange_groups(nz, ny, nx, nc):
    def index(z, y, x, c):
        return ((z * ny + y % ny) * nx + x % nx) * nc + c

    halves = [(yb, xb) for yb in range(2) for xb in range(2)]
    places = [(2 * ya, 2 * xa) for ya in range(ny // 2) for xa in range(nx // 2)]
    far = [
        [
            index(z, 2 * ya + yb, 2 * xa + xb, c)
            for ya in range(ny // 2)
            for z in range(nz)
            for xa in range(nx // 2)
        ]
        for c in range(nc)
        for yb, xb in halves
    ]
    near = [
        [index(z, y + c + (yb + c) % 2, x + c + (xb + c) % 2, c) for yb, xb in halves]
        for z in range(nz)
        for c in range(nc)
        for y, x in places
    ]
    return far, near


def swap(blocks, groups):
    return lax.all_to_all(
        blocks, AXES, split_axis=0, concat_axis=0, axis_index_groups=groups, tiled=True
    )


def other_core(values):
    return lax.ppermute(values, "c", [(0, 1), (1, 0)])


def shards(activations, out_grad, token_scale, route_prob, route_ids, w_gate, w_up, w_down):
    nz, ny, nx, nc = (lax.axis_size(a) for a in AXES)
    far, near = exchange_groups(nz, ny, nx, nc)
    spread = ny * nx // 4
    members = 4
    core = lax.axis_index("c")
    tokens, feats = activations.shape
    capacity = min(tokens, 5 * tokens // (2 * nz))
    parts = feats // FINE
    hidden = w_gate.shape[2]
    rows = nz * capacity
    wide = feats * spread

    heads = [route_ids.T, activations.T, out_grad.T]
    send = pl.pallas_call(
        functools.partial(pack_kernel, capacity),
        out_shape=pltpu.HBM((ny // 2, nz, nx // 2, 2 * FINE, LANES), BF16),
        in_specs=[pl.BlockSpec(memory_space=pl.ANY)] * 3,
        out_specs=pl.BlockSpec(memory_space=pltpu.HBM),
        scratch_shapes=[pltpu.VMEM(h.shape, h.dtype) for h in heads]
        + [pltpu.VMEM((nz, 2 * FINE, LANES), BF16), pltpu.SemaphoreType.DMA((3 + 2 * spread,))],
        compiler_params=pltpu.CompilerParams(vmem_limit_bytes=VMEM_LIMIT),
    )(*(pltpu.with_memory_space_constraint(h, pltpu.HBM) for h in heads))
    got = swap(send.reshape(nz * spread, 2 * FINE, LANES), far)

    views = (ny // 2, 2, nx // 2, 2, nc, parts, FINE, hidden)
    ordered = (members, parts, ny // 2, nx // 2, FINE, hidden)
    gate, up = (
        pltpu.with_memory_space_constraint(w.reshape(views), pltpu.HBM) for w in (w_gate, w_up)
    )
    down = w_down[0].T.reshape(views)

    def order(sent, kept, *sources):
        spaces = [pltpu.VMEM] * len(sent) + [pltpu.HBM] * len(kept)
        count = len(spaces) * members * parts + len(kept)
        ordered_weights = pl.pallas_call(
            functools.partial(order_kernel, (sent, kept, len(sources))),
            out_shape=[space(ordered, BF16) for space in spaces],
            in_specs=[pl.BlockSpec(memory_space=pl.ANY)] * len(sources),
            out_specs=[pl.BlockSpec(memory_space=space) for space in spaces],
            scratch_shapes=[pltpu.SemaphoreType.DMA((count,))]
            + [pltpu.VMEM(ordered, BF16)] * len(kept),
            compiler_params=pltpu.CompilerParams(vmem_limit_bytes=VMEM_LIMIT),
            cost_estimate=pl.CostEstimate(
                flops=0, bytes_accessed=6 * 1024 * 1024, transcendentals=0
            ),
        )(*sources)
        return [w.reshape(members * wide, hidden) for w in ordered_weights]

    *sent, own_down = order((0, 1, 2), (2,), gate, up, down)
    own = [*order((), (0, 1), gate, up), own_down]
    other = [other_core(w) for w in sent]
    got, own, other = lax.optimization_barrier((got, own, other))

    copies = call(
        functools.partial(unpack_kernel, capacity, parts),
        (members, 2 * rows, wide),
        BF16,
        got.reshape(ny // 2, nz, nx // 2, 2 * FINE, LANES),
    )
    block = swap(copies, near)

    flops = 2 * rows * members * wide * 3 * hidden

    def project(w):
        return call(project_kernel, (rows, 3 * hidden), F32, block, *w, flops=flops)

    part_other = project(other)
    rest_own = other_core(part_other)
    part_own = project(own)
    rest_other = other_core(part_own)
    flops = flops // 3 * 2
    part = call(
        return_kernel, (rows, members * wide), F32, part_own, rest_own, *own[:2], flops=flops
    )
    combine = call(
        functools.partial(combine_kernel, capacity, parts),
        (2, nz * LANES, tokens),
        BF16,
        route_ids.T,
        route_prob.T,
        token_scale.reshape(1, tokens),
    )
    part, combine = lax.optimization_barrier((part, combine))
    part = call(
        return_add_kernel,
        (members, rows, wide),
        BF16,
        part_other,
        rest_other,
        *other[:2],
        part,
        flops=flops,
    )
    part = swap(part, near)
    part = call(
        functools.partial(repack_kernel, capacity, parts),
        (ny // 2, nz, nx // 2, FINE, LANES),
        BF16,
        part,
    )
    part = swap(part.reshape(nz * spread, FINE, LANES), far)
    return call(
        functools.partial(final_kernel, capacity, parts),
        (feats, tokens),
        BF16,
        combine,
        part.reshape(ny // 2, nz, nx // 2, FINE, LANES),
    ).T


def solution(mesh):
    devices = mesh.devices
    fine = Mesh(devices.reshape(devices.shape[0], 8, 4, 2), AXES)
    tensor = ("y", "x", "c")
    placed = (
        P("z", tensor),
        P("z", tensor),
        P("z"),
        P("z", None),
        P("z", None),
        P("z", None, tensor),
        P("z", None, tensor),
        P("z", tensor, None),
    )
    return jax.shard_map(
        shards, mesh=fine, in_specs=placed, out_specs=P("z", tensor), check_vma=False
    )
```

```python
import functools
import math

import jax
import jax.numpy as jnp
from jax import lax
from jax.experimental import pallas as pl
from jax.experimental.pallas import tpu as pltpu
from jax.sharding import Mesh, PartitionSpec as P

BF16 = jnp.bfloat16
F32 = jnp.float32
LANES = 128
FINE = 16
VMEM_LIMIT = 16 * 1024 * 1024
AXES = ("z", "y", "x", "c")


def backward_tail(gate, upper, back):
    sigmoid_g = jax.nn.sigmoid(gate)
    slope = sigmoid_g * (1.0 + gate * (1.0 - sigmoid_g))
    d_gate = (back * upper * slope).astype(BF16)
    d_upper = (back * gate * sigmoid_g).astype(BF16)
    return d_gate, d_upper


def lane_parts(shape, axis, capacity):
    inner = lax.broadcasted_iota(jnp.int32, shape, axis) % LANES
    return inner // capacity


def lane_slots(tokens, capacity, parts):
    inner = lax.broadcasted_iota(jnp.int32, (LANES, tokens), 0)
    part = inner // capacity
    return jnp.where(part < parts, inner - part * capacity, -1).astype(F32)


def token_slots(ids, experts):
    tokens = ids.shape[1]
    expert = lax.broadcasted_iota(jnp.int32, (experts, tokens), 0).astype(F32)
    first = ids[0:1, :] == expert
    hit = first | (ids[1:2, :] == expert)
    row = lax.broadcasted_iota(jnp.int32, (tokens, tokens), 0)
    col = lax.broadcasted_iota(jnp.int32, (tokens, tokens), 1)
    earlier = jnp.where(row < col, 1.0, 0.0).astype(BF16)
    hit_bf = jnp.where(hit, 1.0, 0.0).astype(BF16)
    before = jnp.dot(hit_bf, earlier, preferred_element_type=F32)
    return jnp.where(hit, before, -2.0), first


def pack_kernel(capacity, ids_hbm, x_hbm, g_hbm, out_hbm, ids_ref, x_ref, g_ref, held, sems):
    copies = [
        pltpu.make_async_copy(src, dst, sems.at[i])
        for i, (src, dst) in enumerate(((ids_hbm, ids_ref), (x_hbm, x_ref), (g_hbm, g_ref)))
    ]
    for copy in copies:
        copy.start()
    nya, nz, nxa = out_hbm.shape[:3]
    feats, tokens = x_ref.shape
    parts = feats // FINE
    lanes = nz * LANES
    part = lane_parts((FINE, lanes), 1, capacity)
    slot_of_lane = lane_slots(tokens, capacity, parts)
    copies[0].wait()
    slots, _ = token_slots(ids_ref[...].astype(F32), nz)
    place = jnp.concatenate(
        [jnp.where(slots[z : z + 1] == slot_of_lane, 1.0, 0.0).astype(BF16) for z in range(nz)],
        axis=0,
    )
    for kind, ref in enumerate((x_ref, g_ref)):
        copies[1 + kind].wait()
        spread = lax.dot_general(
            ref[...],
            place,
            (((1,), (1,)), ((), ())),
            preferred_element_type=F32,
        )
        block = jnp.zeros((FINE, lanes), F32)
        for p in range(parts):
            block = jnp.where(part == p, spread[p * FINE : (p + 1) * FINE], block)
        block = block.astype(BF16)
        here = pl.ds(kind * FINE, FINE)
        for z in range(nz):
            held[z, kind * FINE : (kind + 1) * FINE, :] = block[:, z * LANES : (z + 1) * LANES]
        for ya in range(nya):
            for xa in range(nxa):
                copies.append(
                    pltpu.make_async_copy(
                        held.at[:, here], out_hbm.at[ya, :, xa, here], sems.at[len(copies)]
                    )
                )
                copies[-1].start()
    for copy in copies[3:]:
        copy.wait()


def unpack_kernel(capacity, parts, in_ref, out_ref):
    nx, _, wide = out_ref.shape
    nz = in_ref.shape[1]
    span = wide // parts
    rows = nz * capacity
    for kind in range(2):
        for pair in range(0, nz, 2):
            turned = []
            for z in (pair, pair + 1):
                block = in_ref[:, z, :, kind * FINE : (kind + 1) * FINE, :]
                turned.append(block.reshape(span, LANES).astype(F32).T)
            start = kind * rows + pair * capacity
            for p in range(parts):
                piece = jnp.concatenate(
                    [t[p * capacity : (p + 1) * capacity] for t in turned], axis=0
                ).astype(BF16)
                for i in range(nx):
                    out_ref[i, start : start + 2 * capacity, p * span : (p + 1) * span] = piece


def repack_kernel(capacity, parts, in_ref, out_ref):
    nx, rows, wide = in_ref.shape
    span = wide // parts
    for pair in range(0, rows // capacity, 2):
        here = slice(pair * capacity, (pair + 2) * capacity)
        total = in_ref[0, here, :].astype(F32)
        for i in range(1, nx):
            total += in_ref[i, here, :].astype(F32)
        for half in range(2):
            block = total[half * capacity : (half + 1) * capacity]
            pieces = [block[:, p * span : (p + 1) * span] for p in range(parts)]
            pieces.append(jnp.zeros((LANES - parts * capacity, span), F32))
            turned = jnp.concatenate(pieces, axis=0).T.astype(BF16)
            z = pair + half
            out_ref[:, z] = turned.reshape(out_ref.shape[0], out_ref.shape[2], FINE, LANES)


def gather(src, half, dst, sems, first):
    pieces = (
        (0, pl.ds(0, 1), pl.ds(0, 1)),
        (0, pl.ds(1, 1), pl.ds(3 - 2 * half, 1)),
        (1, pl.ds(0, 2), pl.ds(1 + half, 2)),
    )
    copies = []
    for yb in range(2):
        for column, there, here in pieces:
            for p in range(src.shape[4]):
                copies.append(
                    pltpu.make_async_copy(
                        src.at[:, yb, here, half, p],
                        dst.at[2 * yb + column, p, :, there],
                        sems.at[first + len(copies)],
                    )
                )
    for copy in copies:
        copy.start()
    return copies


def order_kernel(kept, *refs):
    core = lax.axis_index("c")
    sent, out_refs = len(kept[0]), len(kept[0]) + len(kept[1])
    sources = refs[: kept[2]]
    outs = refs[kept[2] : kept[2] + out_refs]
    sems = refs[kept[2] + out_refs]
    held = refs[kept[2] + out_refs + 1 :]
    waits, each = [], 6 * sources[0].shape[4]
    for i, k in enumerate(kept[0]):
        waits += gather(sources[k], 1 - core, outs[i], sems, i * each)
    own = [
        gather(sources[k], core, held[i], sems, (sent + i) * each) for i, k in enumerate(kept[1])
    ]
    for i, copies in enumerate(own):
        for copy in copies:
            copy.wait()
        copy = pltpu.make_async_copy(held[i], outs[sent + i], sems.at[out_refs * each + i])
        copy.start()
        waits.append(copy)
    for copy in waits:
        copy.wait()


def project_kernel(in_ref, gate_ref, up_ref, down_ref, out_ref):
    members = in_ref.shape[0]
    rows = out_ref.shape[0]
    hidden = gate_ref.shape[1]
    x = jnp.concatenate([in_ref[i, :rows, :] for i in range(members)], axis=1)
    out_ref[:, :hidden] = jnp.dot(x, gate_ref[...], preferred_element_type=F32)
    out_ref[:, hidden : 2 * hidden] = jnp.dot(x, up_ref[...], preferred_element_type=F32)
    g = jnp.concatenate([in_ref[i, rows:, :] for i in range(members)], axis=1)
    out_ref[:, 2 * hidden :] = jnp.dot(g, down_ref[...], preferred_element_type=F32)


def return_part(a_ref, b_ref, gate_ref, up_ref):
    hidden = gate_ref.shape[1]
    gate, upper, back = (
        a_ref[:, k * hidden : (k + 1) * hidden] + b_ref[:, k * hidden : (k + 1) * hidden]
        for k in range(3)
    )
    d_gate, d_upper = backward_tail(gate, upper, back)
    across = (((1,), (1,)), ((), ()))
    part = lax.dot_general(d_gate, gate_ref[...], across, preferred_element_type=F32)
    return part + lax.dot_general(d_upper, up_ref[...], across, preferred_element_type=F32)


def return_kernel(a_ref, b_ref, gate_ref, up_ref, out_ref):
    out_ref[...] = return_part(a_ref, b_ref, gate_ref, up_ref)


def return_add_kernel(a_ref, b_ref, gate_ref, up_ref, sum_ref, out_ref):
    members, _, wide = out_ref.shape
    part = (return_part(a_ref, b_ref, gate_ref, up_ref) + sum_ref[...]).astype(out_ref.dtype)
    for i in range(members):
        out_ref[i] = part[:, i * wide : (i + 1) * wide]


def two_parts(values):
    high = values.astype(BF16)
    return high, (values - high.astype(F32)).astype(BF16)


def combine_kernel(capacity, parts, ids_ref, prob_ref, scale_ref, out_ref):
    _, lanes, tokens = out_ref.shape
    experts = lanes // LANES
    slots, first = token_slots(ids_ref[...].astype(F32), experts)
    weights = jnp.where(first, prob_ref[0:1, :], prob_ref[1:2, :]) * scale_ref[...]
    slot_of_lane = lane_slots(tokens, capacity, parts)
    for z in range(experts):
        here = slice(z * LANES, (z + 1) * LANES)
        weight = jnp.where(slots[z : z + 1] == slot_of_lane, weights[z : z + 1], 0.0)
        out_ref[0, here, :], out_ref[1, here, :] = two_parts(weight)


def final_kernel(capacity, parts, combine_ref, in_ref, out_ref):
    nz = combine_ref.shape[1] // LANES
    feats = out_ref.shape[0]
    sums = []
    for z in range(nz):
        total = jnp.zeros((FINE, LANES), F32)
        for ya in range(in_ref.shape[0]):
            for xa in range(in_ref.shape[2]):
                total += in_ref[ya, z, xa].astype(F32)
        sums.append(total)
    sums = jnp.concatenate(sums, axis=1)
    part = lane_parts(sums.shape, 1, capacity)
    spread = jnp.concatenate([jnp.where(part == p, sums, 0.0) for p in range(parts)], axis=0)
    high, low = two_parts(spread)
    first = jnp.dot(
        jnp.concatenate([high, low], axis=0), combine_ref[0], preferred_element_type=F32
    )
    second = jnp.dot(high, combine_ref[1], preferred_element_type=F32)
    out_ref[...] = (first[:feats] + first[feats:] + second).astype(out_ref.dtype)


def call(kernel, shape, dtype, *operands, flops=0):
    moved = sum(o.size * o.dtype.itemsize for o in operands)
    moved += math.prod(shape) * jnp.dtype(dtype).itemsize
    return pl.pallas_call(
        kernel,
        out_shape=jax.ShapeDtypeStruct(shape, dtype),
        in_specs=[pl.BlockSpec(memory_space=pltpu.VMEM)] * len(operands),
        out_specs=pl.BlockSpec(memory_space=pltpu.VMEM),
        compiler_params=pltpu.CompilerParams(vmem_limit_bytes=VMEM_LIMIT),
        cost_estimate=pl.CostEstimate(flops=flops, bytes_accessed=moved, transcendentals=0),
    )(*operands)


def columns(half, nx):
    return (
        [x for a in range(0, nx, 4) for x in (a, a + 3 - 2 * half)],
        [x for a in range(0, nx, 4) for x in (a + 1 + half, a + 2 + half)],
    )


def exchange_groups(nz, ny, nx, nc):
    def index(z, y, x, c):
        return ((z * ny + y % ny) * nx + x % nx) * nc + c

    far = [
        [index(z, y, x, c) for y in range(yb, ny, 2) for z in range(nz) for x in xs]
        for c in range(nc)
        for yb in range(2)
        for xs in columns(c, nx)
    ]
    near = [
        [
            index(z, y + c + (yb + c) % 2, next(v for v in (x + c, x + c + 1) if v % nx in xs), c)
            for yb in range(2)
            for xs in columns(c, nx)
        ]
        for z in range(nz)
        for c in range(nc)
        for y in range(0, ny, 2)
        for x in range(0, nx, 2)
    ]
    return far, near


def swap(blocks, groups):
    return lax.all_to_all(
        blocks, AXES, split_axis=0, concat_axis=0, axis_index_groups=groups, tiled=True
    )


def other_core(values):
    return lax.ppermute(values, "c", [(0, 1), (1, 0)])


def shards(activations, out_grad, token_scale, route_prob, route_ids, w_gate, w_up, w_down):
    nz, ny, nx, nc = (lax.axis_size(a) for a in AXES)
    far, near = exchange_groups(nz, ny, nx, nc)
    spread = ny * nx // 4
    members = 4
    core = lax.axis_index("c")
    tokens, feats = activations.shape
    capacity = min(tokens, 5 * tokens // (2 * nz))
    parts = feats // FINE
    hidden = w_gate.shape[2]
    rows = nz * capacity
    wide = feats * spread

    heads = [route_ids.T, activations.T, out_grad.T]
    send = pl.pallas_call(
        functools.partial(pack_kernel, capacity),
        out_shape=pltpu.HBM((ny // 2, nz, nx // 2, 2 * FINE, LANES), BF16),
        in_specs=[pl.BlockSpec(memory_space=pl.ANY)] * 3,
        out_specs=pl.BlockSpec(memory_space=pltpu.HBM),
        scratch_shapes=[pltpu.VMEM(h.shape, h.dtype) for h in heads]
        + [pltpu.VMEM((nz, 2 * FINE, LANES), BF16), pltpu.SemaphoreType.DMA((3 + 2 * spread,))],
        compiler_params=pltpu.CompilerParams(vmem_limit_bytes=VMEM_LIMIT),
    )(*(pltpu.with_memory_space_constraint(h, pltpu.HBM) for h in heads))
    got = swap(send.reshape(nz * spread, 2 * FINE, LANES), far)

    views = (ny // 2, 2, nx, nc, parts, FINE, hidden)
    ordered = (members, parts, ny // 2, nx // 2, FINE, hidden)
    gate, up = (
        pltpu.with_memory_space_constraint(w.reshape(views), pltpu.HBM) for w in (w_gate, w_up)
    )
    down = w_down[0].T.reshape(views)

    def order(sent, kept, *sources):
        spaces = [pltpu.VMEM] * len(sent) + [pltpu.HBM] * len(kept)
        count = len(spaces) * 6 * parts + len(kept)
        ordered_weights = pl.pallas_call(
            functools.partial(order_kernel, (sent, kept, len(sources))),
            out_shape=[space(ordered, BF16) for space in spaces],
            in_specs=[pl.BlockSpec(memory_space=pl.ANY)] * len(sources),
            out_specs=[pl.BlockSpec(memory_space=space) for space in spaces],
            scratch_shapes=[pltpu.SemaphoreType.DMA((count,))]
            + [pltpu.VMEM(ordered, BF16)] * len(kept),
            compiler_params=pltpu.CompilerParams(vmem_limit_bytes=VMEM_LIMIT),
            cost_estimate=pl.CostEstimate(
                flops=0, bytes_accessed=6 * 1024 * 1024, transcendentals=0
            ),
        )(*sources)
        return [w.reshape(members * wide, hidden) for w in ordered_weights]

    *sent, own_down = order((0, 1, 2), (2,), gate, up, down)
    own = [*order((), (0, 1), gate, up), own_down]
    other = [other_core(w) for w in sent]
    got, own, other = lax.optimization_barrier((got, own, other))

    copies = call(
        functools.partial(unpack_kernel, capacity, parts),
        (members, 2 * rows, wide),
        BF16,
        got.reshape(ny // 2, nz, nx // 2, 2 * FINE, LANES),
    )
    block = swap(copies, near)

    flops = 2 * rows * members * wide * 3 * hidden

    def project(w):
        return call(project_kernel, (rows, 3 * hidden), F32, block, *w, flops=flops)

    part_other = project(other)
    rest_own = other_core(part_other)
    part_own = project(own)
    rest_other = other_core(part_own)
    flops = flops // 3 * 2
    part = call(
        return_kernel, (rows, members * wide), F32, part_own, rest_own, *own[:2], flops=flops
    )
    combine = call(
        functools.partial(combine_kernel, capacity, parts),
        (2, nz * LANES, tokens),
        BF16,
        route_ids.T,
        route_prob.T,
        token_scale.reshape(1, tokens),
    )
    part, combine = lax.optimization_barrier((part, combine))
    part = call(
        return_add_kernel,
        (members, rows, wide),
        BF16,
        part_other,
        rest_other,
        *other[:2],
        part,
        flops=flops,
    )
    part = swap(part, near)
    part = call(
        functools.partial(repack_kernel, capacity, parts),
        (ny // 2, nz, nx // 2, FINE, LANES),
        BF16,
        part,
    )
    part = swap(part.reshape(nz * spread, FINE, LANES), far)
    return call(
        functools.partial(final_kernel, capacity, parts),
        (feats, tokens),
        BF16,
        combine,
        part.reshape(ny // 2, nz, nx // 2, FINE, LANES),
    ).T


def solution(mesh):
    devices = mesh.devices
    fine = Mesh(devices.reshape(devices.shape[0], 8, 4, 2), AXES)
    tensor = ("y", "x", "c")
    placed = (
        P("z", tensor),
        P("z", tensor),
        P("z"),
        P("z", None),
        P("z", None),
        P("z", None, tensor),
        P("z", None, tensor),
        P("z", tensor, None),
    )
    return jax.shard_map(
        shards, mesh=fine, in_specs=placed, out_specs=P("z", tensor), check_vma=False
    )
```

```python
import functools
import math

import jax
import jax.numpy as jnp
from jax import lax
from jax.experimental import pallas as pl
from jax.experimental.pallas import tpu as pltpu
from jax.sharding import Mesh, PartitionSpec as P

BF16 = jnp.bfloat16
F32 = jnp.float32
LANES = 128
FINE = 16
VMEM_LIMIT = 16 * 1024 * 1024
AXES = ("z", "y", "x", "c")


def backward_tail(gate, upper, back):
    sigmoid_g = jax.nn.sigmoid(gate)
    slope = sigmoid_g * (1.0 + gate * (1.0 - sigmoid_g))
    d_gate = (back * upper * slope).astype(BF16)
    d_upper = (back * gate * sigmoid_g).astype(BF16)
    return d_gate, d_upper


def lane_parts(shape, axis, capacity):
    inner = lax.broadcasted_iota(jnp.int32, shape, axis) % LANES
    return inner // capacity


def lane_slots(tokens, capacity, parts):
    inner = lax.broadcasted_iota(jnp.int32, (LANES, tokens), 0)
    part = inner // capacity
    return jnp.where(part < parts, inner - part * capacity, -1).astype(F32)


def token_slots(ids, experts):
    tokens = ids.shape[1]
    expert = lax.broadcasted_iota(jnp.int32, (experts, tokens), 0).astype(F32)
    first = ids[0:1, :] == expert
    hit = first | (ids[1:2, :] == expert)
    row = lax.broadcasted_iota(jnp.int32, (tokens, tokens), 0)
    col = lax.broadcasted_iota(jnp.int32, (tokens, tokens), 1)
    earlier = jnp.where(row < col, 1.0, 0.0).astype(BF16)
    hit_bf = jnp.where(hit, 1.0, 0.0).astype(BF16)
    before = jnp.dot(hit_bf, earlier, preferred_element_type=F32)
    return jnp.where(hit, before, -2.0), first


def pack_kernel(capacity, ids_hbm, x_hbm, g_hbm, out_hbm, ids_ref, x_ref, g_ref, held, sems):
    copies = [
        pltpu.make_async_copy(src, dst, sems.at[i])
        for i, (src, dst) in enumerate(((ids_hbm, ids_ref), (x_hbm, x_ref), (g_hbm, g_ref)))
    ]
    for copy in copies:
        copy.start()
    nya, nz, nxa = out_hbm.shape[:3]
    feats, tokens = x_ref.shape
    parts = feats // FINE
    lanes = nz * LANES
    part = lane_parts((FINE, lanes), 1, capacity)
    slot_of_lane = lane_slots(tokens, capacity, parts)
    copies[0].wait()
    slots, _ = token_slots(ids_ref[...].astype(F32), nz)
    place = jnp.concatenate(
        [jnp.where(slots[z : z + 1] == slot_of_lane, 1.0, 0.0).astype(BF16) for z in range(nz)],
        axis=0,
    )
    for kind, ref in enumerate((x_ref, g_ref)):
        copies[1 + kind].wait()
        spread = lax.dot_general(
            ref[...],
            place,
            (((1,), (1,)), ((), ())),
            preferred_element_type=F32,
        )
        block = jnp.zeros((FINE, lanes), F32)
        for p in range(parts):
            block = jnp.where(part == p, spread[p * FINE : (p + 1) * FINE], block)
        block = block.astype(BF16)
        here = pl.ds(kind * FINE, FINE)
        for z in range(nz):
            held[z, kind * FINE : (kind + 1) * FINE, :] = block[:, z * LANES : (z + 1) * LANES]
        for ya in range(nya):
            for xa in range(nxa):
                copies.append(
                    pltpu.make_async_copy(
                        held.at[:, here], out_hbm.at[ya, :, xa, here], sems.at[len(copies)]
                    )
                )
                copies[-1].start()
    for copy in copies[3:]:
        copy.wait()


def unpack_kernel(capacity, parts, in_ref, out_ref):
    nx, _, wide = out_ref.shape
    nz = in_ref.shape[1]
    span = wide // parts
    rows = nz * capacity
    for kind in range(2):
        for pair in range(0, nz, 2):
            turned = []
            for z in (pair, pair + 1):
                block = in_ref[:, z, :, kind * FINE : (kind + 1) * FINE, :]
                turned.append(block.reshape(span, LANES).astype(F32).T)
            start = kind * rows + pair * capacity
            for p in range(parts):
                piece = jnp.concatenate(
                    [t[p * capacity : (p + 1) * capacity] for t in turned], axis=0
                ).astype(BF16)
                for i in range(nx):
                    out_ref[i, start : start + 2 * capacity, p * span : (p + 1) * span] = piece


def repack_kernel(capacity, parts, in_ref, out_ref):
    nx, rows, wide = in_ref.shape
    span = wide // parts
    for pair in range(0, rows // capacity, 2):
        here = slice(pair * capacity, (pair + 2) * capacity)
        total = in_ref[0, here, :].astype(F32)
        for i in range(1, nx):
            total += in_ref[i, here, :].astype(F32)
        for half in range(2):
            block = total[half * capacity : (half + 1) * capacity]
            pieces = [block[:, p * span : (p + 1) * span] for p in range(parts)]
            pieces.append(jnp.zeros((LANES - parts * capacity, span), F32))
            turned = jnp.concatenate(pieces, axis=0).T.astype(BF16)
            z = pair + half
            out_ref[:, z] = turned.reshape(out_ref.shape[0], out_ref.shape[2], FINE, LANES)


def gather(src, half, dst, sems, first):
    pieces = (
        (0, pl.ds(0, 1), pl.ds(0, 1)),
        (0, pl.ds(1, 1), pl.ds(3 - 2 * half, 1)),
        (1, pl.ds(0, 2), pl.ds(1 + half, 2)),
    )
    copies = []
    for yb in range(2):
        for column, there, here in pieces:
            for p in range(src.shape[4]):
                copies.append(
                    pltpu.make_async_copy(
                        src.at[:, yb, here, half, p],
                        dst.at[2 * yb + column, p, :, there],
                        sems.at[first + len(copies)],
                    )
                )
    for copy in copies:
        copy.start()
    return copies


def sent_kernel(gate_hbm, up_hbm, down_hbm, gate_ref, up_ref, down_ref, own_hbm, raw, turned, sems):
    core = lax.axis_index("c")
    chunks, _, width = raw.shape
    loads = [
        pltpu.make_async_copy(down_hbm.at[:, pl.ds(k * width, width)], raw.at[k], sems.at[k])
        for k in range(chunks)
    ]
    for copy in loads:
        copy.start()
    each = 6 * gate_hbm.shape[4]
    waits = gather(gate_hbm, 1 - core, gate_ref, sems, chunks)
    waits += gather(up_hbm, 1 - core, up_ref, sems, chunks + each)
    for k, copy in enumerate(loads):
        copy.wait()
        turned[k] = raw[k].T.reshape(turned.shape[1:])
    waits += gather(turned, 1 - core, down_ref, sems, chunks + 2 * each)
    waits += gather(turned, core, own_hbm, sems, chunks + 3 * each)
    for copy in waits:
        copy.wait()


def own_kernel(gate_hbm, up_hbm, own_gate, own_up, held, sems):
    core = lax.axis_index("c")
    each = 6 * gate_hbm.shape[4]
    parts = [
        gather(src, core, held.at[k], sems, k * each) for k, src in enumerate((gate_hbm, up_hbm))
    ]
    waits = []
    for k, out in enumerate((own_gate, own_up)):
        for copy in parts[k]:
            copy.wait()
        waits.append(pltpu.make_async_copy(held.at[k], out, sems.at[2 * each + k]))
        waits[-1].start()
    for copy in waits:
        copy.wait()


def project_kernel(in_ref, gate_ref, up_ref, down_ref, out_ref):
    members = in_ref.shape[0]
    rows = out_ref.shape[0]
    hidden = gate_ref.shape[1]
    x = jnp.concatenate([in_ref[i, :rows, :] for i in range(members)], axis=1)
    out_ref[:, :hidden] = jnp.dot(x, gate_ref[...], preferred_element_type=F32)
    out_ref[:, hidden : 2 * hidden] = jnp.dot(x, up_ref[...], preferred_element_type=F32)
    g = jnp.concatenate([in_ref[i, rows:, :] for i in range(members)], axis=1)
    out_ref[:, 2 * hidden :] = jnp.dot(g, down_ref[...], preferred_element_type=F32)


def return_part(a_ref, b_ref, gate_ref, up_ref):
    hidden = gate_ref.shape[1]
    gate, upper, back = (
        a_ref[:, k * hidden : (k + 1) * hidden] + b_ref[:, k * hidden : (k + 1) * hidden]
        for k in range(3)
    )
    d_gate, d_upper = backward_tail(gate, upper, back)
    across = (((1,), (1,)), ((), ()))
    part = lax.dot_general(d_gate, gate_ref[...], across, preferred_element_type=F32)
    return part + lax.dot_general(d_upper, up_ref[...], across, preferred_element_type=F32)


def return_kernel(a_ref, b_ref, gate_ref, up_ref, out_ref):
    out_ref[...] = return_part(a_ref, b_ref, gate_ref, up_ref)


def return_add_kernel(a_ref, b_ref, gate_ref, up_ref, sum_ref, out_ref):
    members, _, wide = out_ref.shape
    part = (return_part(a_ref, b_ref, gate_ref, up_ref) + sum_ref[...]).astype(out_ref.dtype)
    for i in range(members):
        out_ref[i] = part[:, i * wide : (i + 1) * wide]


def two_parts(values):
    high = values.astype(BF16)
    return high, (values - high.astype(F32)).astype(BF16)


def combine_kernel(capacity, parts, ids_ref, prob_ref, scale_ref, out_ref):
    _, lanes, tokens = out_ref.shape
    experts = lanes // LANES
    slots, first = token_slots(ids_ref[...].astype(F32), experts)
    weights = jnp.where(first, prob_ref[0:1, :], prob_ref[1:2, :]) * scale_ref[...]
    slot_of_lane = lane_slots(tokens, capacity, parts)
    for z in range(experts):
        here = slice(z * LANES, (z + 1) * LANES)
        weight = jnp.where(slots[z : z + 1] == slot_of_lane, weights[z : z + 1], 0.0)
        out_ref[0, here, :], out_ref[1, here, :] = two_parts(weight)


def final_kernel(capacity, parts, combine_ref, in_ref, out_ref):
    nz = combine_ref.shape[1] // LANES
    feats = out_ref.shape[0]
    sums = []
    for z in range(nz):
        total = jnp.zeros((FINE, LANES), F32)
        for ya in range(in_ref.shape[0]):
            for xa in range(in_ref.shape[2]):
                total += in_ref[ya, z, xa].astype(F32)
        sums.append(total)
    sums = jnp.concatenate(sums, axis=1)
    part = lane_parts(sums.shape, 1, capacity)
    spread = jnp.concatenate([jnp.where(part == p, sums, 0.0) for p in range(parts)], axis=0)
    high, low = two_parts(spread)
    first = jnp.dot(
        jnp.concatenate([high, low], axis=0), combine_ref[0], preferred_element_type=F32
    )
    second = jnp.dot(high, combine_ref[1], preferred_element_type=F32)
    out_ref[...] = (first[:feats] + first[feats:] + second).astype(out_ref.dtype)


def call(kernel, shape, dtype, *operands, flops=0):
    moved = sum(o.size * o.dtype.itemsize for o in operands)
    moved += math.prod(shape) * jnp.dtype(dtype).itemsize
    return pl.pallas_call(
        kernel,
        out_shape=jax.ShapeDtypeStruct(shape, dtype),
        in_specs=[pl.BlockSpec(memory_space=pltpu.VMEM)] * len(operands),
        out_specs=pl.BlockSpec(memory_space=pltpu.VMEM),
        compiler_params=pltpu.CompilerParams(vmem_limit_bytes=VMEM_LIMIT),
        cost_estimate=pl.CostEstimate(flops=flops, bytes_accessed=moved, transcendentals=0),
    )(*operands)


def columns(half, nx):
    return (
        [x for a in range(0, nx, 4) for x in (a, a + 3 - 2 * half)],
        [x for a in range(0, nx, 4) for x in (a + 1 + half, a + 2 + half)],
    )


def exchange_groups(nz, ny, nx, nc):
    def index(z, y, x, c):
        return ((z * ny + y % ny) * nx + x % nx) * nc + c

    far = [
        [index(z, y, x, c) for y in range(yb, ny, 2) for z in range(nz) for x in xs]
        for c in range(nc)
        for yb in range(2)
        for xs in columns(c, nx)
    ]
    near = [
        [
            index(z, y + c + (yb + c) % 2, next(v for v in (x + c, x + c + 1) if v % nx in xs), c)
            for yb in range(2)
            for xs in columns(c, nx)
        ]
        for z in range(nz)
        for c in range(nc)
        for y in range(0, ny, 2)
        for x in range(0, nx, 2)
    ]
    return far, near


def swap(blocks, groups):
    return lax.all_to_all(
        blocks, AXES, split_axis=0, concat_axis=0, axis_index_groups=groups, tiled=True
    )


def other_core(values):
    return lax.ppermute(values, "c", [(0, 1), (1, 0)])


def shards(activations, out_grad, token_scale, route_prob, route_ids, w_gate, w_up, w_down):
    nz, ny, nx, nc = (lax.axis_size(a) for a in AXES)
    far, near = exchange_groups(nz, ny, nx, nc)
    spread = ny * nx // 4
    members = 4
    core = lax.axis_index("c")
    tokens, feats = activations.shape
    capacity = min(tokens, 5 * tokens // (2 * nz))
    parts = feats // FINE
    hidden = w_gate.shape[2]
    rows = nz * capacity
    wide = feats * spread

    heads = [route_ids.T, activations.T, out_grad.T]
    send = pl.pallas_call(
        functools.partial(pack_kernel, capacity),
        out_shape=pltpu.HBM((ny // 2, nz, nx // 2, 2 * FINE, LANES), BF16),
        in_specs=[pl.BlockSpec(memory_space=pl.ANY)] * 3,
        out_specs=pl.BlockSpec(memory_space=pltpu.HBM),
        scratch_shapes=[pltpu.VMEM(h.shape, h.dtype) for h in heads]
        + [pltpu.VMEM((nz, 2 * FINE, LANES), BF16), pltpu.SemaphoreType.DMA((3 + 2 * spread,))],
        compiler_params=pltpu.CompilerParams(vmem_limit_bytes=VMEM_LIMIT),
    )(*(pltpu.with_memory_space_constraint(h, pltpu.HBM) for h in heads))
    got = swap(send.reshape(nz * spread, 2 * FINE, LANES), far)

    views = (ny // 2, 2, nx, nc, parts, FINE, hidden)
    ordered = (members, parts, ny // 2, nx // 2, FINE, hidden)
    gate, up = (
        pltpu.with_memory_space_constraint(w.reshape(views), pltpu.HBM) for w in (w_gate, w_up)
    )
    down = pltpu.with_memory_space_constraint(w_down[0], pltpu.HBM)
    chunks, each = ny // 2, 6 * parts

    def order(kernel, spaces, scratch, *sources):
        ordered_weights = pl.pallas_call(
            kernel,
            out_shape=[space(ordered, BF16) for space in spaces],
            in_specs=[pl.BlockSpec(memory_space=pl.ANY)] * len(sources),
            out_specs=[pl.BlockSpec(memory_space=space) for space in spaces],
            scratch_shapes=scratch,
            compiler_params=pltpu.CompilerParams(vmem_limit_bytes=VMEM_LIMIT),
            cost_estimate=pl.CostEstimate(
                flops=0, bytes_accessed=6 * 1024 * 1024, transcendentals=0
            ),
        )(*sources)
        return [w.reshape(members * wide, hidden) for w in ordered_weights]

    *sent, own_down = order(
        sent_kernel,
        [pltpu.VMEM] * 3 + [pltpu.HBM],
        [
            pltpu.VMEM((chunks, hidden, down.shape[1] // chunks), BF16),
            pltpu.VMEM(views, BF16),
            pltpu.SemaphoreType.DMA((chunks + 4 * each,)),
        ],
        gate,
        up,
        down,
    )
    own = order(
        own_kernel,
        [pltpu.HBM] * 2,
        [pltpu.VMEM((2,) + ordered, BF16), pltpu.SemaphoreType.DMA((2 * each + 2,))],
        gate,
        up,
    )
    own = [*own, own_down]
    other = [other_core(w) for w in sent]
    got, own, other = lax.optimization_barrier((got, own, other))

    copies = call(
        functools.partial(unpack_kernel, capacity, parts),
        (members, 2 * rows, wide),
        BF16,
        got.reshape(ny // 2, nz, nx // 2, 2 * FINE, LANES),
    )
    block = swap(copies, near)

    flops = 2 * rows * members * wide * 3 * hidden

    def project(w):
        return call(project_kernel, (rows, 3 * hidden), F32, block, *w, flops=flops)

    part_other = project(other)
    rest_own = other_core(part_other)
    part_own = project(own)
    rest_other = other_core(part_own)
    flops = flops // 3 * 2
    part = call(
        return_kernel, (rows, members * wide), F32, part_own, rest_own, *own[:2], flops=flops
    )
    combine = call(
        functools.partial(combine_kernel, capacity, parts),
        (2, nz * LANES, tokens),
        BF16,
        route_ids.T,
        route_prob.T,
        token_scale.reshape(1, tokens),
    )
    part, combine = lax.optimization_barrier((part, combine))
    part = call(
        return_add_kernel,
        (members, rows, wide),
        BF16,
        part_other,
        rest_other,
        *other[:2],
        part,
        flops=flops,
    )
    part = swap(part, near)
    part = call(
        functools.partial(repack_kernel, capacity, parts),
        (ny // 2, nz, nx // 2, FINE, LANES),
        BF16,
        part,
    )
    part = swap(part.reshape(nz * spread, FINE, LANES), far)
    return call(
        functools.partial(final_kernel, capacity, parts),
        (feats, tokens),
        BF16,
        combine,
        part.reshape(ny // 2, nz, nx // 2, FINE, LANES),
    ).T


def solution(mesh):
    devices = mesh.devices
    fine = Mesh(devices.reshape(devices.shape[0], 8, 4, 2), AXES)
    tensor = ("y", "x", "c")
    placed = (
        P("z", tensor),
        P("z", tensor),
        P("z"),
        P("z", None),
        P("z", None),
        P("z", None, tensor),
        P("z", None, tensor),
        P("z", tensor, None),
    )
    return jax.shard_map(
        shards, mesh=fine, in_specs=placed, out_specs=P("z", tensor), check_vma=False
    )
```

```python
import functools
import math

import jax
import jax.numpy as jnp
from jax import lax
from jax.experimental import pallas as pl
from jax.experimental.pallas import tpu as pltpu
from jax.sharding import Mesh, PartitionSpec as P

BF16 = jnp.bfloat16
F32 = jnp.float32
LANES = 128
FINE = 16
VMEM_LIMIT = 16 * 1024 * 1024
AXES = ("z", "y", "x", "c")


def backward_tail(gate, upper, back):
    sigmoid_g = jax.nn.sigmoid(gate)
    slope = sigmoid_g * (1.0 + gate * (1.0 - sigmoid_g))
    d_gate = (back * upper * slope).astype(BF16)
    d_upper = (back * gate * sigmoid_g).astype(BF16)
    return d_gate, d_upper


def lane_parts(shape, axis, capacity):
    inner = lax.broadcasted_iota(jnp.int32, shape, axis) % LANES
    return inner // capacity


def lane_slots(tokens, capacity, parts):
    inner = lax.broadcasted_iota(jnp.int32, (LANES, tokens), 0)
    part = inner // capacity
    return jnp.where(part < parts, inner - part * capacity, -1).astype(F32)


def token_slots(ids, experts):
    tokens = ids.shape[1]
    expert = lax.broadcasted_iota(jnp.int32, (experts, tokens), 0).astype(F32)
    first = ids[0:1, :] == expert
    hit = first | (ids[1:2, :] == expert)
    row = lax.broadcasted_iota(jnp.int32, (tokens, tokens), 0)
    col = lax.broadcasted_iota(jnp.int32, (tokens, tokens), 1)
    earlier = jnp.where(row < col, 1.0, 0.0).astype(BF16)
    hit_bf = jnp.where(hit, 1.0, 0.0).astype(BF16)
    before = jnp.dot(hit_bf, earlier, preferred_element_type=F32)
    return jnp.where(hit, before, -2.0), first


def pack_kernel(capacity, ids_hbm, x_hbm, g_hbm, out_hbm, ids_ref, x_ref, g_ref, held, sems):
    copies = [
        pltpu.make_async_copy(src, dst, sems.at[i])
        for i, (src, dst) in enumerate(((ids_hbm, ids_ref), (x_hbm, x_ref), (g_hbm, g_ref)))
    ]
    for copy in copies:
        copy.start()
    nya, nz, nxa = out_hbm.shape[:3]
    feats, tokens = x_ref.shape
    parts = feats // FINE
    lanes = nz * LANES
    part = lane_parts((FINE, lanes), 1, capacity)
    slot_of_lane = lane_slots(tokens, capacity, parts)
    copies[0].wait()
    slots, _ = token_slots(ids_ref[...].astype(F32), nz)
    place = jnp.concatenate(
        [jnp.where(slots[z : z + 1] == slot_of_lane, 1.0, 0.0).astype(BF16) for z in range(nz)],
        axis=0,
    )
    for kind, ref in enumerate((x_ref, g_ref)):
        copies[1 + kind].wait()
        spread = lax.dot_general(
            ref[...],
            place,
            (((1,), (1,)), ((), ())),
            preferred_element_type=F32,
        )
        block = jnp.zeros((FINE, lanes), F32)
        for p in range(parts):
            block = jnp.where(part == p, spread[p * FINE : (p + 1) * FINE], block)
        block = block.astype(BF16)
        here = pl.ds(kind * FINE, FINE)
        for z in range(nz):
            held[z, kind * FINE : (kind + 1) * FINE, :] = block[:, z * LANES : (z + 1) * LANES]
        for ya in range(nya):
            for xa in range(nxa):
                copies.append(
                    pltpu.make_async_copy(
                        held.at[:, here], out_hbm.at[ya, :, xa, here], sems.at[len(copies)]
                    )
                )
                copies[-1].start()
    for copy in copies[3:]:
        copy.wait()


def unpack_kernel(capacity, parts, in_ref, out_ref):
    nx, _, wide = out_ref.shape
    nz = in_ref.shape[1]
    span = wide // parts
    rows = nz * capacity
    for kind in range(2):
        for pair in range(0, nz, 2):
            turned = []
            for z in (pair, pair + 1):
                block = in_ref[:, z, :, kind * FINE : (kind + 1) * FINE, :]
                turned.append(block.reshape(span, LANES).astype(F32).T)
            start = kind * rows + pair * capacity
            for p in range(parts):
                piece = jnp.concatenate(
                    [t[p * capacity : (p + 1) * capacity] for t in turned], axis=0
                ).astype(BF16)
                for i in range(nx):
                    out_ref[i, start : start + 2 * capacity, p * span : (p + 1) * span] = piece


def repack_kernel(capacity, parts, in_ref, out_ref):
    nx, rows, wide = in_ref.shape
    span = wide // parts
    for pair in range(0, rows // capacity, 2):
        here = slice(pair * capacity, (pair + 2) * capacity)
        total = in_ref[0, here, :].astype(F32)
        for i in range(1, nx):
            total += in_ref[i, here, :].astype(F32)
        for half in range(2):
            block = total[half * capacity : (half + 1) * capacity]
            pieces = [block[:, p * span : (p + 1) * span] for p in range(parts)]
            pieces.append(jnp.zeros((LANES - parts * capacity, span), F32))
            turned = jnp.concatenate(pieces, axis=0).T.astype(BF16)
            z = pair + half
            out_ref[:, z] = turned.reshape(out_ref.shape[0], out_ref.shape[2], FINE, LANES)


def gather(src, half, dst, sems, first):
    pieces = (
        (0, pl.ds(0, 1), pl.ds(0, 1)),
        (0, pl.ds(1, 1), pl.ds(3 - 2 * half, 1)),
        (1, pl.ds(0, 2), pl.ds(1 + half, 2)),
    )
    copies = []
    for yb in range(2):
        for column, there, here in pieces:
            for p in range(src.shape[4]):
                copies.append(
                    pltpu.make_async_copy(
                        src.at[:, yb, here, half, p],
                        dst.at[2 * yb + column, p, :, there],
                        sems.at[first + len(copies)],
                    )
                )
    for copy in copies:
        copy.start()
    return copies


def sent_kernel(gate_hbm, up_hbm, down_hbm, gate_ref, up_ref, down_ref, own_hbm, raw, turned, sems):
    core = lax.axis_index("c")
    chunks, _, width = raw.shape
    loads = [
        pltpu.make_async_copy(down_hbm.at[:, pl.ds(k * width, width)], raw.at[k], sems.at[k])
        for k in range(chunks)
    ]
    for copy in loads:
        copy.start()
    each = 6 * gate_hbm.shape[4]
    waits = gather(gate_hbm, 1 - core, gate_ref, sems, chunks)
    waits += gather(up_hbm, 1 - core, up_ref, sems, chunks + each)
    for k, copy in enumerate(loads):
        copy.wait()
        turned[k] = raw[k].T.reshape(turned.shape[1:])
    waits += gather(turned, 1 - core, down_ref, sems, chunks + 2 * each)
    waits += gather(turned, core, own_hbm, sems, chunks + 3 * each)
    for copy in waits:
        copy.wait()


def own_kernel(gate_hbm, up_hbm, own_gate, own_up, held, sems):
    core = lax.axis_index("c")
    each = 6 * gate_hbm.shape[4]
    parts = [
        gather(src, core, held.at[k], sems, k * each) for k, src in enumerate((gate_hbm, up_hbm))
    ]
    waits = []
    for k, out in enumerate((own_gate, own_up)):
        for copy in parts[k]:
            copy.wait()
        waits.append(pltpu.make_async_copy(held.at[k], out, sems.at[2 * each + k]))
        waits[-1].start()
    for copy in waits:
        copy.wait()


def side_by_side(in_ref, rows):
    return jnp.concatenate([in_ref[i, rows, :] for i in range(in_ref.shape[0])], axis=1)


def first_kernel(in_ref, gate_ref, up_ref, down_ref, own_down_ref, out_ref):
    rows = out_ref.shape[0]
    hidden = gate_ref.shape[1]
    x, g = side_by_side(in_ref, slice(0, rows)), side_by_side(in_ref, slice(rows, 2 * rows))
    pairs = ((x, gate_ref), (x, up_ref), (g, down_ref), (g, own_down_ref))
    for k, (values, w_ref) in enumerate(pairs):
        out_ref[:, k * hidden : (k + 1) * hidden] = jnp.dot(
            values, w_ref[...], preferred_element_type=F32
        )


def second_kernel(in_ref, gate_ref, up_ref, out_ref):
    hidden = gate_ref.shape[1]
    x = side_by_side(in_ref, slice(0, out_ref.shape[0]))
    for k, w_ref in enumerate((gate_ref, up_ref)):
        out_ref[:, k * hidden : (k + 1) * hidden] = jnp.dot(
            x, w_ref[...], preferred_element_type=F32
        )


def return_part(gate, upper, back, gate_ref, up_ref):
    d_gate, d_upper = backward_tail(gate, upper, back)
    across = (((1,), (1,)), ((), ()))
    part = lax.dot_general(d_gate, gate_ref[...], across, preferred_element_type=F32)
    return part + lax.dot_general(d_upper, up_ref[...], across, preferred_element_type=F32)


def return_kernel(first_ref, second_ref, got_first_ref, gate_ref, up_ref, out_ref):
    hidden = gate_ref.shape[1]
    a, b, c, d = (slice(k * hidden, (k + 1) * hidden) for k in range(4))
    out_ref[...] = return_part(
        second_ref[:, a] + got_first_ref[:, a],
        second_ref[:, b] + got_first_ref[:, b],
        first_ref[:, d] + got_first_ref[:, c],
        gate_ref,
        up_ref,
    )


def return_add_kernel(
    first_ref, got_first_ref, got_second_ref, gate_ref, up_ref, sum_ref, out_ref
):
    members, _, wide = out_ref.shape
    hidden = gate_ref.shape[1]
    a, b, c, d = (slice(k * hidden, (k + 1) * hidden) for k in range(4))
    part = return_part(
        first_ref[:, a] + got_second_ref[:, a],
        first_ref[:, b] + got_second_ref[:, b],
        first_ref[:, c] + got_first_ref[:, d],
        gate_ref,
        up_ref,
    )
    part = (part + sum_ref[...]).astype(out_ref.dtype)
    for i in range(members):
        out_ref[i] = part[:, i * wide : (i + 1) * wide]


def two_parts(values):
    high = values.astype(BF16)
    return high, (values - high.astype(F32)).astype(BF16)


def combine_kernel(capacity, parts, ids_ref, prob_ref, scale_ref, out_ref):
    _, lanes, tokens = out_ref.shape
    experts = lanes // LANES
    slots, first = token_slots(ids_ref[...].astype(F32), experts)
    weights = jnp.where(first, prob_ref[0:1, :], prob_ref[1:2, :]) * scale_ref[...]
    slot_of_lane = lane_slots(tokens, capacity, parts)
    for z in range(experts):
        here = slice(z * LANES, (z + 1) * LANES)
        weight = jnp.where(slots[z : z + 1] == slot_of_lane, weights[z : z + 1], 0.0)
        out_ref[0, here, :], out_ref[1, here, :] = two_parts(weight)


def final_kernel(capacity, parts, combine_ref, in_ref, out_ref):
    nz = combine_ref.shape[1] // LANES
    feats = out_ref.shape[0]
    sums = []
    for z in range(nz):
        total = jnp.zeros((FINE, LANES), F32)
        for ya in range(in_ref.shape[0]):
            for xa in range(in_ref.shape[2]):
                total += in_ref[ya, z, xa].astype(F32)
        sums.append(total)
    sums = jnp.concatenate(sums, axis=1)
    part = lane_parts(sums.shape, 1, capacity)
    spread = jnp.concatenate([jnp.where(part == p, sums, 0.0) for p in range(parts)], axis=0)
    high, low = two_parts(spread)
    first = jnp.dot(
        jnp.concatenate([high, low], axis=0), combine_ref[0], preferred_element_type=F32
    )
    second = jnp.dot(high, combine_ref[1], preferred_element_type=F32)
    out_ref[...] = (first[:feats] + first[feats:] + second).astype(out_ref.dtype)


def call(kernel, shape, dtype, *operands, flops=0):
    moved = sum(o.size * o.dtype.itemsize for o in operands)
    moved += math.prod(shape) * jnp.dtype(dtype).itemsize
    return pl.pallas_call(
        kernel,
        out_shape=jax.ShapeDtypeStruct(shape, dtype),
        in_specs=[pl.BlockSpec(memory_space=pltpu.VMEM)] * len(operands),
        out_specs=pl.BlockSpec(memory_space=pltpu.VMEM),
        compiler_params=pltpu.CompilerParams(vmem_limit_bytes=VMEM_LIMIT),
        cost_estimate=pl.CostEstimate(flops=flops, bytes_accessed=moved, transcendentals=0),
    )(*operands)


def columns(half, nx):
    return (
        [x for a in range(0, nx, 4) for x in (a, a + 3 - 2 * half)],
        [x for a in range(0, nx, 4) for x in (a + 1 + half, a + 2 + half)],
    )


def exchange_groups(nz, ny, nx, nc):
    def index(z, y, x, c):
        return ((z * ny + y % ny) * nx + x % nx) * nc + c

    far = [
        [index(z, y, x, c) for y in range(yb, ny, 2) for z in range(nz) for x in xs]
        for c in range(nc)
        for yb in range(2)
        for xs in columns(c, nx)
    ]
    near = [
        [
            index(z, y + c + (yb + c) % 2, next(v for v in (x + c, x + c + 1) if v % nx in xs), c)
            for yb in range(2)
            for xs in columns(c, nx)
        ]
        for z in range(nz)
        for c in range(nc)
        for y in range(0, ny, 2)
        for x in range(0, nx, 2)
    ]
    return far, near


def swap(blocks, groups):
    return lax.all_to_all(
        blocks, AXES, split_axis=0, concat_axis=0, axis_index_groups=groups, tiled=True
    )


def other_core(values):
    return lax.ppermute(values, "c", [(0, 1), (1, 0)])


def shards(activations, out_grad, token_scale, route_prob, route_ids, w_gate, w_up, w_down):
    nz, ny, nx, nc = (lax.axis_size(a) for a in AXES)
    far, near = exchange_groups(nz, ny, nx, nc)
    spread = ny * nx // 4
    members = 4
    core = lax.axis_index("c")
    tokens, feats = activations.shape
    capacity = min(tokens, 5 * tokens // (2 * nz))
    parts = feats // FINE
    hidden = w_gate.shape[2]
    rows = nz * capacity
    wide = feats * spread

    heads = [route_ids.T, activations.T, out_grad.T]
    send = pl.pallas_call(
        functools.partial(pack_kernel, capacity),
        out_shape=pltpu.HBM((ny // 2, nz, nx // 2, 2 * FINE, LANES), BF16),
        in_specs=[pl.BlockSpec(memory_space=pl.ANY)] * 3,
        out_specs=pl.BlockSpec(memory_space=pltpu.HBM),
        scratch_shapes=[pltpu.VMEM(h.shape, h.dtype) for h in heads]
        + [pltpu.VMEM((nz, 2 * FINE, LANES), BF16), pltpu.SemaphoreType.DMA((3 + 2 * spread,))],
        compiler_params=pltpu.CompilerParams(vmem_limit_bytes=VMEM_LIMIT),
    )(*(pltpu.with_memory_space_constraint(h, pltpu.HBM) for h in heads))
    got = swap(send.reshape(nz * spread, 2 * FINE, LANES), far)

    views = (ny // 2, 2, nx, nc, parts, FINE, hidden)
    ordered = (members, parts, ny // 2, nx // 2, FINE, hidden)
    gate, up = (
        pltpu.with_memory_space_constraint(w.reshape(views), pltpu.HBM) for w in (w_gate, w_up)
    )
    down = pltpu.with_memory_space_constraint(w_down[0], pltpu.HBM)
    chunks, each = ny // 2, 6 * parts

    def order(kernel, spaces, scratch, *sources):
        ordered_weights = pl.pallas_call(
            kernel,
            out_shape=[space(ordered, BF16) for space in spaces],
            in_specs=[pl.BlockSpec(memory_space=pl.ANY)] * len(sources),
            out_specs=[pl.BlockSpec(memory_space=space) for space in spaces],
            scratch_shapes=scratch,
            compiler_params=pltpu.CompilerParams(vmem_limit_bytes=VMEM_LIMIT),
            cost_estimate=pl.CostEstimate(
                flops=0, bytes_accessed=6 * 1024 * 1024, transcendentals=0
            ),
        )(*sources)
        return [w.reshape(members * wide, hidden) for w in ordered_weights]

    *sent, own_down = order(
        sent_kernel,
        [pltpu.VMEM] * 3 + [pltpu.HBM],
        [
            pltpu.VMEM((chunks, hidden, down.shape[1] // chunks), BF16),
            pltpu.VMEM(views, BF16),
            pltpu.SemaphoreType.DMA((chunks + 4 * each,)),
        ],
        gate,
        up,
        down,
    )
    own = order(
        own_kernel,
        [pltpu.HBM] * 2,
        [pltpu.VMEM((2,) + ordered, BF16), pltpu.SemaphoreType.DMA((2 * each + 2,))],
        gate,
        up,
    )
    own = [*own, own_down]
    other = [other_core(w) for w in sent]
    got, own, other = lax.optimization_barrier((got, own, other))

    copies = call(
        functools.partial(unpack_kernel, capacity, parts),
        (members, 2 * rows, wide),
        BF16,
        got.reshape(ny // 2, nz, nx // 2, 2 * FINE, LANES),
    )
    block = swap(copies, near)

    flops = 2 * rows * members * wide * hidden

    first = call(
        first_kernel, (rows, 4 * hidden), F32, block, *other, own[2], flops=4 * flops
    )
    got_first = other_core(first)
    second = call(second_kernel, (rows, 2 * hidden), F32, block, *own[:2], flops=2 * flops)
    got_second = other_core(second)
    part = call(
        return_kernel,
        (rows, members * wide),
        F32,
        first,
        second,
        got_first,
        *own[:2],
        flops=2 * flops,
    )
    combine = call(
        functools.partial(combine_kernel, capacity, parts),
        (2, nz * LANES, tokens),
        BF16,
        route_ids.T,
        route_prob.T,
        token_scale.reshape(1, tokens),
    )
    part, combine = lax.optimization_barrier((part, combine))
    part = call(
        return_add_kernel,
        (members, rows, wide),
        BF16,
        first,
        got_first,
        got_second,
        *other[:2],
        part,
        flops=2 * flops,
    )
    part = swap(part, near)
    part = call(
        functools.partial(repack_kernel, capacity, parts),
        (ny // 2, nz, nx // 2, FINE, LANES),
        BF16,
        part,
    )
    part = swap(part.reshape(nz * spread, FINE, LANES), far)
    return call(
        functools.partial(final_kernel, capacity, parts),
        (feats, tokens),
        BF16,
        combine,
        part.reshape(ny // 2, nz, nx // 2, FINE, LANES),
    ).T


def solution(mesh):
    devices = mesh.devices
    fine = Mesh(devices.reshape(devices.shape[0], 8, 4, 2), AXES)
    tensor = ("y", "x", "c")
    placed = (
        P("z", tensor),
        P("z", tensor),
        P("z"),
        P("z", None),
        P("z", None),
        P("z", None, tensor),
        P("z", None, tensor),
        P("z", tensor, None),
    )
    return jax.shard_map(
        shards, mesh=fine, in_specs=placed, out_specs=P("z", tensor), check_vma=False
    )
```

```python
import functools
import math

import jax
import jax.numpy as jnp
from jax import lax
from jax.experimental import pallas as pl
from jax.experimental.pallas import tpu as pltpu
from jax.sharding import Mesh, PartitionSpec as P

BF16 = jnp.bfloat16
F32 = jnp.float32
LANES = 128
FINE = 16
VMEM_LIMIT = 16 * 1024 * 1024
AXES = ("z", "y", "x", "c")


def backward_tail(gate, upper, back):
    sigmoid_g = jax.nn.sigmoid(gate)
    slope = sigmoid_g * (1.0 + gate * (1.0 - sigmoid_g))
    d_gate = (back * upper * slope).astype(BF16)
    d_upper = (back * gate * sigmoid_g).astype(BF16)
    return d_gate, d_upper


def lane_parts(shape, axis, capacity):
    inner = lax.broadcasted_iota(jnp.int32, shape, axis) % LANES
    return inner // capacity


def lane_slots(tokens, capacity, parts):
    inner = lax.broadcasted_iota(jnp.int32, (LANES, tokens), 0)
    part = inner // capacity
    return jnp.where(part < parts, inner - part * capacity, -1).astype(F32)


def token_slots(ids, experts):
    tokens = ids.shape[1]
    expert = lax.broadcasted_iota(jnp.int32, (experts, tokens), 0).astype(F32)
    first = ids[0:1, :] == expert
    hit = first | (ids[1:2, :] == expert)
    row = lax.broadcasted_iota(jnp.int32, (tokens, tokens), 0)
    col = lax.broadcasted_iota(jnp.int32, (tokens, tokens), 1)
    earlier = jnp.where(row < col, 1.0, 0.0).astype(BF16)
    hit_bf = jnp.where(hit, 1.0, 0.0).astype(BF16)
    before = jnp.dot(hit_bf, earlier, preferred_element_type=F32)
    return jnp.where(hit, before, -2.0), first


def pack_kernel(capacity, ids_hbm, x_hbm, g_hbm, out_hbm, ids_ref, x_ref, g_ref, held, sems):
    copies = [
        pltpu.make_async_copy(src, dst, sems.at[i])
        for i, (src, dst) in enumerate(((ids_hbm, ids_ref), (x_hbm, x_ref), (g_hbm, g_ref)))
    ]
    for copy in copies:
        copy.start()
    nya, nz, nxa = out_hbm.shape[:3]
    feats, tokens = x_ref.shape
    parts = feats // FINE
    lanes = nz * LANES
    part = lane_parts((FINE, lanes), 1, capacity)
    slot_of_lane = lane_slots(tokens, capacity, parts)
    copies[0].wait()
    slots, _ = token_slots(ids_ref[...].astype(F32), nz)
    place = jnp.concatenate(
        [jnp.where(slots[z : z + 1] == slot_of_lane, 1.0, 0.0).astype(BF16) for z in range(nz)],
        axis=0,
    )
    for kind, ref in enumerate((x_ref, g_ref)):
        copies[1 + kind].wait()
        spread = lax.dot_general(
            ref[...],
            place,
            (((1,), (1,)), ((), ())),
            preferred_element_type=F32,
        )
        block = jnp.zeros((FINE, lanes), F32)
        for p in range(parts):
            block = jnp.where(part == p, spread[p * FINE : (p + 1) * FINE], block)
        block = block.astype(BF16)
        here = pl.ds(kind * FINE, FINE)
        for z in range(nz):
            held[z, kind * FINE : (kind + 1) * FINE, :] = block[:, z * LANES : (z + 1) * LANES]
        for ya in range(nya):
            for xa in range(nxa):
                copies.append(
                    pltpu.make_async_copy(
                        held.at[:, here], out_hbm.at[ya, :, xa, here], sems.at[len(copies)]
                    )
                )
                copies[-1].start()
    for copy in copies[3:]:
        copy.wait()


def unpack_kernel(capacity, parts, in_ref, out_ref):
    nx, _, wide = out_ref.shape
    nz = in_ref.shape[1]
    span = wide // parts
    rows = nz * capacity
    for kind in range(2):
        for pair in range(0, nz, 2):
            turned = []
            for z in (pair, pair + 1):
                block = in_ref[:, z, :, kind * FINE : (kind + 1) * FINE, :]
                turned.append(block.reshape(span, LANES).astype(F32).T)
            start = kind * rows + pair * capacity
            for p in range(parts):
                piece = jnp.concatenate(
                    [t[p * capacity : (p + 1) * capacity] for t in turned], axis=0
                ).astype(BF16)
                for i in range(nx):
                    out_ref[i, start : start + 2 * capacity, p * span : (p + 1) * span] = piece


def repack_kernel(capacity, parts, in_ref, out_ref):
    nx, rows, wide = in_ref.shape
    span = wide // parts
    for pair in range(0, rows // capacity, 2):
        here = slice(pair * capacity, (pair + 2) * capacity)
        total = in_ref[0, here, :].astype(F32)
        for i in range(1, nx):
            total += in_ref[i, here, :].astype(F32)
        for half in range(2):
            block = total[half * capacity : (half + 1) * capacity]
            pieces = [block[:, p * span : (p + 1) * span] for p in range(parts)]
            pieces.append(jnp.zeros((LANES - parts * capacity, span), F32))
            turned = jnp.concatenate(pieces, axis=0).T.astype(BF16)
            z = pair + half
            out_ref[:, z] = turned.reshape(out_ref.shape[0], out_ref.shape[2], FINE, LANES)


def gather(src, half, dst, sems, first):
    pieces = (
        (0, pl.ds(0, 1), pl.ds(0, 1)),
        (0, pl.ds(1, 1), pl.ds(3 - 2 * half, 1)),
        (1, pl.ds(0, 2), pl.ds(1 + half, 2)),
    )
    copies = []
    for yb in range(2):
        for column, there, here in pieces:
            for p in range(src.shape[4]):
                copies.append(
                    pltpu.make_async_copy(
                        src.at[:, yb, here, half, p],
                        dst.at[2 * yb + column, p, :, there],
                        sems.at[first + len(copies)],
                    )
                )
    for copy in copies:
        copy.start()
    return copies


def sent_kernel(gate_hbm, up_hbm, down_hbm, gate_ref, up_ref, down_ref, own_hbm, raw, turned, sems):
    core = lax.axis_index("c")
    chunks, _, width = raw.shape
    loads = [
        pltpu.make_async_copy(down_hbm.at[:, pl.ds(k * width, width)], raw.at[k], sems.at[k])
        for k in range(chunks)
    ]
    for copy in loads:
        copy.start()
    each = 6 * gate_hbm.shape[4]
    waits = gather(gate_hbm, 1 - core, gate_ref, sems, chunks)
    waits += gather(up_hbm, 1 - core, up_ref, sems, chunks + each)
    for k, copy in enumerate(loads):
        copy.wait()
        turned[k] = raw[k].T.reshape(turned.shape[1:])
    waits += gather(turned, 1 - core, down_ref, sems, chunks + 2 * each)
    waits += gather(turned, core, own_hbm, sems, chunks + 3 * each)
    for copy in waits:
        copy.wait()


def own_kernel(gate_hbm, up_hbm, own_gate, own_up, held, sems):
    core = lax.axis_index("c")
    each = 6 * gate_hbm.shape[4]
    parts = [
        gather(src, core, held.at[k], sems, k * each) for k, src in enumerate((gate_hbm, up_hbm))
    ]
    waits = []
    for k, out in enumerate((own_gate, own_up)):
        for copy in parts[k]:
            copy.wait()
        waits.append(pltpu.make_async_copy(held.at[k], out, sems.at[2 * each + k]))
        waits[-1].start()
    for copy in waits:
        copy.wait()


def side_by_side(in_ref, rows):
    return jnp.concatenate([in_ref[i, rows, :] for i in range(in_ref.shape[0])], axis=1)


def first_kernel(in_ref, gate_ref, up_ref, down_ref, own_down_ref, own_gate_ref, out_ref):
    rows = out_ref.shape[0]
    hidden = gate_ref.shape[1]
    x, g = side_by_side(in_ref, slice(0, rows)), side_by_side(in_ref, slice(rows, 2 * rows))
    pairs = ((x, gate_ref), (x, up_ref), (g, down_ref), (g, own_down_ref), (x, own_gate_ref))
    for k, (values, w_ref) in enumerate(pairs):
        out_ref[:, k * hidden : (k + 1) * hidden] = jnp.dot(
            values, w_ref[...], preferred_element_type=F32
        )


def second_kernel(in_ref, up_ref, out_ref):
    x = side_by_side(in_ref, slice(0, out_ref.shape[0]))
    out_ref[...] = jnp.dot(x, up_ref[...], preferred_element_type=F32)


def return_part(gate, upper, back, gate_ref, up_ref):
    d_gate, d_upper = backward_tail(gate, upper, back)
    across = (((1,), (1,)), ((), ()))
    part = lax.dot_general(d_gate, gate_ref[...], across, preferred_element_type=F32)
    return part + lax.dot_general(d_upper, up_ref[...], across, preferred_element_type=F32)


def return_kernel(first_ref, second_ref, got_first_ref, gate_ref, up_ref, out_ref):
    hidden = gate_ref.shape[1]
    a, b, c, d, e = (slice(k * hidden, (k + 1) * hidden) for k in range(5))
    out_ref[...] = return_part(
        first_ref[:, e] + got_first_ref[:, a],
        second_ref[...] + got_first_ref[:, b],
        first_ref[:, d] + got_first_ref[:, c],
        gate_ref,
        up_ref,
    )


def return_add_kernel(
    first_ref, got_first_ref, got_second_ref, gate_ref, up_ref, sum_ref, out_ref
):
    members, _, wide = out_ref.shape
    hidden = gate_ref.shape[1]
    a, b, c, d, e = (slice(k * hidden, (k + 1) * hidden) for k in range(5))
    part = return_part(
        first_ref[:, a] + got_first_ref[:, e],
        first_ref[:, b] + got_second_ref[...],
        first_ref[:, c] + got_first_ref[:, d],
        gate_ref,
        up_ref,
    )
    part = (part + sum_ref[...]).astype(out_ref.dtype)
    for i in range(members):
        out_ref[i] = part[:, i * wide : (i + 1) * wide]


def two_parts(values):
    high = values.astype(BF16)
    return high, (values - high.astype(F32)).astype(BF16)


def combine_kernel(capacity, parts, ids_ref, prob_ref, scale_ref, out_ref):
    _, lanes, tokens = out_ref.shape
    experts = lanes // LANES
    slots, first = token_slots(ids_ref[...].astype(F32), experts)
    weights = jnp.where(first, prob_ref[0:1, :], prob_ref[1:2, :]) * scale_ref[...]
    slot_of_lane = lane_slots(tokens, capacity, parts)
    for z in range(experts):
        here = slice(z * LANES, (z + 1) * LANES)
        weight = jnp.where(slots[z : z + 1] == slot_of_lane, weights[z : z + 1], 0.0)
        out_ref[0, here, :], out_ref[1, here, :] = two_parts(weight)


def final_kernel(capacity, parts, combine_ref, in_ref, out_ref):
    nz = combine_ref.shape[1] // LANES
    feats = out_ref.shape[0]
    sums = []
    for z in range(nz):
        total = jnp.zeros((FINE, LANES), F32)
        for ya in range(in_ref.shape[0]):
            for xa in range(in_ref.shape[2]):
                total += in_ref[ya, z, xa].astype(F32)
        sums.append(total)
    sums = jnp.concatenate(sums, axis=1)
    part = lane_parts(sums.shape, 1, capacity)
    spread = jnp.concatenate([jnp.where(part == p, sums, 0.0) for p in range(parts)], axis=0)
    high, low = two_parts(spread)
    first = jnp.dot(
        jnp.concatenate([high, low], axis=0), combine_ref[0], preferred_element_type=F32
    )
    second = jnp.dot(high, combine_ref[1], preferred_element_type=F32)
    out_ref[...] = (first[:feats] + first[feats:] + second).astype(out_ref.dtype)


def call(kernel, shape, dtype, *operands, flops=0):
    moved = sum(o.size * o.dtype.itemsize for o in operands)
    moved += math.prod(shape) * jnp.dtype(dtype).itemsize
    return pl.pallas_call(
        kernel,
        out_shape=jax.ShapeDtypeStruct(shape, dtype),
        in_specs=[pl.BlockSpec(memory_space=pltpu.VMEM)] * len(operands),
        out_specs=pl.BlockSpec(memory_space=pltpu.VMEM),
        compiler_params=pltpu.CompilerParams(vmem_limit_bytes=VMEM_LIMIT),
        cost_estimate=pl.CostEstimate(flops=flops, bytes_accessed=moved, transcendentals=0),
    )(*operands)


def columns(half, nx):
    return (
        [x for a in range(0, nx, 4) for x in (a, a + 3 - 2 * half)],
        [x for a in range(0, nx, 4) for x in (a + 1 + half, a + 2 + half)],
    )


def exchange_groups(nz, ny, nx, nc):
    def index(z, y, x, c):
        return ((z * ny + y % ny) * nx + x % nx) * nc + c

    far = [
        [index(z, y, x, c) for y in range(yb, ny, 2) for z in range(nz) for x in xs]
        for c in range(nc)
        for yb in range(2)
        for xs in columns(c, nx)
    ]
    near = [
        [
            index(z, y + c + (yb + c) % 2, next(v for v in (x + c, x + c + 1) if v % nx in xs), c)
            for yb in range(2)
            for xs in columns(c, nx)
        ]
        for z in range(nz)
        for c in range(nc)
        for y in range(0, ny, 2)
        for x in range(0, nx, 2)
    ]
    return far, near


def swap(blocks, groups):
    return lax.all_to_all(
        blocks, AXES, split_axis=0, concat_axis=0, axis_index_groups=groups, tiled=True
    )


def other_core(values):
    return lax.ppermute(values, "c", [(0, 1), (1, 0)])


def shards(activations, out_grad, token_scale, route_prob, route_ids, w_gate, w_up, w_down):
    nz, ny, nx, nc = (lax.axis_size(a) for a in AXES)
    far, near = exchange_groups(nz, ny, nx, nc)
    spread = ny * nx // 4
    members = 4
    core = lax.axis_index("c")
    tokens, feats = activations.shape
    capacity = min(tokens, 5 * tokens // (2 * nz))
    parts = feats // FINE
    hidden = w_gate.shape[2]
    rows = nz * capacity
    wide = feats * spread

    heads = [route_ids.T, activations.T, out_grad.T]
    send = pl.pallas_call(
        functools.partial(pack_kernel, capacity),
        out_shape=pltpu.HBM((ny // 2, nz, nx // 2, 2 * FINE, LANES), BF16),
        in_specs=[pl.BlockSpec(memory_space=pl.ANY)] * 3,
        out_specs=pl.BlockSpec(memory_space=pltpu.HBM),
        scratch_shapes=[pltpu.VMEM(h.shape, h.dtype) for h in heads]
        + [pltpu.VMEM((nz, 2 * FINE, LANES), BF16), pltpu.SemaphoreType.DMA((3 + 2 * spread,))],
        compiler_params=pltpu.CompilerParams(vmem_limit_bytes=VMEM_LIMIT),
    )(*(pltpu.with_memory_space_constraint(h, pltpu.HBM) for h in heads))
    got = swap(send.reshape(nz * spread, 2 * FINE, LANES), far)

    views = (ny // 2, 2, nx, nc, parts, FINE, hidden)
    ordered = (members, parts, ny // 2, nx // 2, FINE, hidden)
    gate, up = (
        pltpu.with_memory_space_constraint(w.reshape(views), pltpu.HBM) for w in (w_gate, w_up)
    )
    down = pltpu.with_memory_space_constraint(w_down[0], pltpu.HBM)
    chunks, each = ny // 2, 6 * parts

    def order(kernel, spaces, scratch, *sources):
        ordered_weights = pl.pallas_call(
            kernel,
            out_shape=[space(ordered, BF16) for space in spaces],
            in_specs=[pl.BlockSpec(memory_space=pl.ANY)] * len(sources),
            out_specs=[pl.BlockSpec(memory_space=space) for space in spaces],
            scratch_shapes=scratch,
            compiler_params=pltpu.CompilerParams(vmem_limit_bytes=VMEM_LIMIT),
            cost_estimate=pl.CostEstimate(
                flops=0, bytes_accessed=6 * 1024 * 1024, transcendentals=0
            ),
        )(*sources)
        return [w.reshape(members * wide, hidden) for w in ordered_weights]

    *sent, own_down = order(
        sent_kernel,
        [pltpu.VMEM] * 3 + [pltpu.HBM],
        [
            pltpu.VMEM((chunks, hidden, down.shape[1] // chunks), BF16),
            pltpu.VMEM(views, BF16),
            pltpu.SemaphoreType.DMA((chunks + 4 * each,)),
        ],
        gate,
        up,
        down,
    )
    own = order(
        own_kernel,
        [pltpu.HBM] * 2,
        [pltpu.VMEM((2,) + ordered, BF16), pltpu.SemaphoreType.DMA((2 * each + 2,))],
        gate,
        up,
    )
    own = [*own, own_down]
    other = [other_core(w) for w in sent]
    got, own, other = lax.optimization_barrier((got, own, other))

    copies = call(
        functools.partial(unpack_kernel, capacity, parts),
        (members, 2 * rows, wide),
        BF16,
        got.reshape(ny // 2, nz, nx // 2, 2 * FINE, LANES),
    )
    block = swap(copies, near)

    flops = 2 * rows * members * wide * hidden

    first = call(
        first_kernel, (rows, 5 * hidden), F32, block, *other, own[2], own[0], flops=5 * flops
    )
    got_first = other_core(first)
    second = call(second_kernel, (rows, hidden), F32, block, own[1], flops=flops)
    got_second = other_core(second)
    part = call(
        return_kernel,
        (rows, members * wide),
        F32,
        first,
        second,
        got_first,
        *own[:2],
        flops=2 * flops,
    )
    combine = call(
        functools.partial(combine_kernel, capacity, parts),
        (2, nz * LANES, tokens),
        BF16,
        route_ids.T,
        route_prob.T,
        token_scale.reshape(1, tokens),
    )
    part, combine = lax.optimization_barrier((part, combine))
    part = call(
        return_add_kernel,
        (members, rows, wide),
        BF16,
        first,
        got_first,
        got_second,
        *other[:2],
        part,
        flops=2 * flops,
    )
    part = swap(part, near)
    part = call(
        functools.partial(repack_kernel, capacity, parts),
        (ny // 2, nz, nx // 2, FINE, LANES),
        BF16,
        part,
    )
    part = swap(part.reshape(nz * spread, FINE, LANES), far)
    return call(
        functools.partial(final_kernel, capacity, parts),
        (feats, tokens),
        BF16,
        combine,
        part.reshape(ny // 2, nz, nx // 2, FINE, LANES),
    ).T


def solution(mesh):
    devices = mesh.devices
    fine = Mesh(devices.reshape(devices.shape[0], 8, 4, 2), AXES)
    tensor = ("y", "x", "c")
    placed = (
        P("z", tensor),
        P("z", tensor),
        P("z"),
        P("z", None),
        P("z", None),
        P("z", None, tensor),
        P("z", None, tensor),
        P("z", tensor, None),
    )
    return jax.shard_map(
        shards, mesh=fine, in_specs=placed, out_specs=P("z", tensor), check_vma=False
    )
```

```python
import functools
import math

import jax
import jax.numpy as jnp
from jax import lax
from jax.experimental import pallas as pl
from jax.experimental.pallas import tpu as pltpu
from jax.sharding import Mesh, PartitionSpec as P

BF16 = jnp.bfloat16
F32 = jnp.float32
LANES = 128
FINE = 16
VMEM_LIMIT = 16 * 1024 * 1024
AXES = ("z", "y", "x", "c")


def backward_tail(gate, upper, back):
    sigmoid_g = jax.nn.sigmoid(gate)
    slope = sigmoid_g * (1.0 + gate * (1.0 - sigmoid_g))
    d_gate = (back * upper * slope).astype(BF16)
    d_upper = (back * gate * sigmoid_g).astype(BF16)
    return d_gate, d_upper


def lane_parts(shape, axis, capacity):
    inner = lax.broadcasted_iota(jnp.int32, shape, axis) % LANES
    return inner // capacity


def lane_slots(tokens, capacity, parts):
    inner = lax.broadcasted_iota(jnp.int32, (LANES, tokens), 0)
    part = inner // capacity
    return jnp.where(part < parts, inner - part * capacity, -1).astype(F32)


def token_slots(ids, experts):
    tokens = ids.shape[1]
    expert = lax.broadcasted_iota(jnp.int32, (experts, tokens), 0).astype(F32)
    first = ids[0:1, :] == expert
    hit = first | (ids[1:2, :] == expert)
    row = lax.broadcasted_iota(jnp.int32, (tokens, tokens), 0)
    col = lax.broadcasted_iota(jnp.int32, (tokens, tokens), 1)
    earlier = jnp.where(row < col, 1.0, 0.0).astype(BF16)
    hit_bf = jnp.where(hit, 1.0, 0.0).astype(BF16)
    before = jnp.dot(hit_bf, earlier, preferred_element_type=F32)
    return jnp.where(hit, before, -2.0), first


def pack_kernel(capacity, ids_hbm, x_hbm, g_hbm, out_hbm, ids_ref, x_ref, g_ref, held, sems):
    copies = [
        pltpu.make_async_copy(src, dst, sems.at[i])
        for i, (src, dst) in enumerate(((ids_hbm, ids_ref), (x_hbm, x_ref), (g_hbm, g_ref)))
    ]
    for copy in copies:
        copy.start()
    nya, nz, nxa = out_hbm.shape[:3]
    feats, tokens = x_ref.shape
    parts = feats // FINE
    lanes = nz * LANES
    part = lane_parts((FINE, lanes), 1, capacity)
    slot_of_lane = lane_slots(tokens, capacity, parts)
    copies[0].wait()
    slots, _ = token_slots(ids_ref[...].astype(F32), nz)
    place = jnp.concatenate(
        [jnp.where(slots[z : z + 1] == slot_of_lane, 1.0, 0.0).astype(BF16) for z in range(nz)],
        axis=0,
    )
    for kind, ref in enumerate((x_ref, g_ref)):
        copies[1 + kind].wait()
        spread = lax.dot_general(
            ref[...],
            place,
            (((1,), (1,)), ((), ())),
            preferred_element_type=F32,
        )
        block = jnp.zeros((FINE, lanes), F32)
        for p in range(parts):
            block = jnp.where(part == p, spread[p * FINE : (p + 1) * FINE], block)
        block = block.astype(BF16)
        here = pl.ds(kind * FINE, FINE)
        for z in range(nz):
            held[z, kind * FINE : (kind + 1) * FINE, :] = block[:, z * LANES : (z + 1) * LANES]
        for ya in range(nya):
            for xa in range(nxa):
                copies.append(
                    pltpu.make_async_copy(
                        held.at[:, here], out_hbm.at[ya, :, xa, here], sems.at[len(copies)]
                    )
                )
                copies[-1].start()
    for copy in copies[3:]:
        copy.wait()


def unpack_kernel(capacity, parts, in_ref, out_ref):
    nx, _, wide = out_ref.shape
    nz = in_ref.shape[1]
    span = wide // parts
    rows = nz * capacity
    for kind in range(2):
        for pair in range(0, nz, 2):
            turned = []
            for z in (pair, pair + 1):
                block = in_ref[:, z, :, kind * FINE : (kind + 1) * FINE, :]
                turned.append(block.reshape(span, LANES).astype(F32).T)
            start = kind * rows + pair * capacity
            for p in range(parts):
                piece = jnp.concatenate(
                    [t[p * capacity : (p + 1) * capacity] for t in turned], axis=0
                ).astype(BF16)
                for i in range(nx):
                    out_ref[i, start : start + 2 * capacity, p * span : (p + 1) * span] = piece


def repack_kernel(capacity, parts, in_ref, out_ref):
    nx, rows, wide = in_ref.shape
    span = wide // parts
    for pair in range(0, rows // capacity, 2):
        here = slice(pair * capacity, (pair + 2) * capacity)
        total = in_ref[0, here, :].astype(F32)
        for i in range(1, nx):
            total += in_ref[i, here, :].astype(F32)
        for half in range(2):
            block = total[half * capacity : (half + 1) * capacity]
            pieces = [block[:, p * span : (p + 1) * span] for p in range(parts)]
            pieces.append(jnp.zeros((LANES - parts * capacity, span), F32))
            turned = jnp.concatenate(pieces, axis=0).T.astype(BF16)
            z = pair + half
            out_ref[:, z] = turned.reshape(out_ref.shape[0], out_ref.shape[2], FINE, LANES)


def gather(src, half, dst, sems, first):
    pieces = (
        (0, pl.ds(0, 1), pl.ds(0, 1)),
        (0, pl.ds(1, 1), pl.ds(3 - 2 * half, 1)),
        (1, pl.ds(0, 2), pl.ds(1 + half, 2)),
    )
    copies = []
    for yb in range(2):
        for column, there, here in pieces:
            for p in range(src.shape[4]):
                copies.append(
                    pltpu.make_async_copy(
                        src.at[:, yb, here, half, p],
                        dst.at[2 * yb + column, p, :, there],
                        sems.at[first + len(copies)],
                    )
                )
    for copy in copies:
        copy.start()
    return copies


def sent_kernel(
    gate_hbm, up_hbm, down_hbm, gate_ref, up_ref, down_ref, own_down, own_gate, raw, turned, held, sems
):
    core = lax.axis_index("c")
    chunks, _, width = raw.shape
    loads = [
        pltpu.make_async_copy(down_hbm.at[:, pl.ds(k * width, width)], raw.at[k], sems.at[k])
        for k in range(chunks)
    ]
    for copy in loads:
        copy.start()
    each = 6 * gate_hbm.shape[4]
    waits = gather(gate_hbm, 1 - core, gate_ref, sems, chunks)
    waits += gather(up_hbm, 1 - core, up_ref, sems, chunks + each)
    own = gather(gate_hbm, core, held, sems, chunks + 4 * each)
    for k, copy in enumerate(loads):
        copy.wait()
        turned[k] = raw[k].T.reshape(turned.shape[1:])
    waits += gather(turned, 1 - core, down_ref, sems, chunks + 2 * each)
    waits += gather(turned, core, own_down, sems, chunks + 3 * each)
    for copy in own:
        copy.wait()
    waits.append(pltpu.make_async_copy(held, own_gate, sems.at[chunks + 5 * each]))
    waits[-1].start()
    for copy in waits:
        copy.wait()


def own_kernel(up_hbm, own_up, held, sems):
    copies = gather(up_hbm, lax.axis_index("c"), held, sems, 0)
    for copy in copies:
        copy.wait()
    whole = pltpu.make_async_copy(held, own_up, sems.at[len(copies)])
    whole.start()
    whole.wait()


def side_by_side(in_ref, rows):
    return jnp.concatenate([in_ref[i, rows, :] for i in range(in_ref.shape[0])], axis=1)


def first_kernel(in_ref, gate_ref, up_ref, down_ref, own_down_ref, own_gate_ref, out_ref):
    rows = out_ref.shape[0]
    hidden = gate_ref.shape[1]
    x, g = side_by_side(in_ref, slice(0, rows)), side_by_side(in_ref, slice(rows, 2 * rows))
    pairs = ((x, gate_ref), (x, up_ref), (g, down_ref), (g, own_down_ref), (x, own_gate_ref))
    for k, (values, w_ref) in enumerate(pairs):
        out_ref[:, k * hidden : (k + 1) * hidden] = jnp.dot(
            values, w_ref[...], preferred_element_type=F32
        )


def second_kernel(in_ref, up_ref, out_ref):
    x = side_by_side(in_ref, slice(0, out_ref.shape[0]))
    out_ref[...] = jnp.dot(x, up_ref[...], preferred_element_type=F32)


def return_part(gate, upper, back, gate_ref, up_ref):
    d_gate, d_upper = backward_tail(gate, upper, back)
    across = (((1,), (1,)), ((), ()))
    part = lax.dot_general(d_gate, gate_ref[...], across, preferred_element_type=F32)
    return part + lax.dot_general(d_upper, up_ref[...], across, preferred_element_type=F32)


def return_kernel(first_ref, second_ref, got_first_ref, gate_ref, up_ref, out_ref):
    hidden = gate_ref.shape[1]
    a, b, c, d, e = (slice(k * hidden, (k + 1) * hidden) for k in range(5))
    out_ref[...] = return_part(
        first_ref[:, e] + got_first_ref[:, a],
        second_ref[...] + got_first_ref[:, b],
        first_ref[:, d] + got_first_ref[:, c],
        gate_ref,
        up_ref,
    )


def return_add_kernel(
    first_ref, got_first_ref, got_second_ref, gate_ref, up_ref, sum_ref, out_ref
):
    members, _, wide = out_ref.shape
    hidden = gate_ref.shape[1]
    a, b, c, d, e = (slice(k * hidden, (k + 1) * hidden) for k in range(5))
    part = return_part(
        first_ref[:, a] + got_first_ref[:, e],
        first_ref[:, b] + got_second_ref[...],
        first_ref[:, c] + got_first_ref[:, d],
        gate_ref,
        up_ref,
    )
    part = (part + sum_ref[...]).astype(out_ref.dtype)
    for i in range(members):
        out_ref[i] = part[:, i * wide : (i + 1) * wide]


def two_parts(values):
    high = values.astype(BF16)
    return high, (values - high.astype(F32)).astype(BF16)


def combine_kernel(capacity, parts, ids_ref, prob_ref, scale_ref, out_ref):
    _, lanes, tokens = out_ref.shape
    experts = lanes // LANES
    slots, first = token_slots(ids_ref[...].astype(F32), experts)
    weights = jnp.where(first, prob_ref[0:1, :], prob_ref[1:2, :]) * scale_ref[...]
    slot_of_lane = lane_slots(tokens, capacity, parts)
    for z in range(experts):
        here = slice(z * LANES, (z + 1) * LANES)
        weight = jnp.where(slots[z : z + 1] == slot_of_lane, weights[z : z + 1], 0.0)
        out_ref[0, here, :], out_ref[1, here, :] = two_parts(weight)


def final_kernel(capacity, parts, combine_ref, in_ref, out_ref):
    nz = combine_ref.shape[1] // LANES
    feats = out_ref.shape[0]
    sums = []
    for z in range(nz):
        total = jnp.zeros((FINE, LANES), F32)
        for ya in range(in_ref.shape[0]):
            for xa in range(in_ref.shape[2]):
                total += in_ref[ya, z, xa].astype(F32)
        sums.append(total)
    sums = jnp.concatenate(sums, axis=1)
    part = lane_parts(sums.shape, 1, capacity)
    spread = jnp.concatenate([jnp.where(part == p, sums, 0.0) for p in range(parts)], axis=0)
    high, low = two_parts(spread)
    first = jnp.dot(
        jnp.concatenate([high, low], axis=0), combine_ref[0], preferred_element_type=F32
    )
    second = jnp.dot(high, combine_ref[1], preferred_element_type=F32)
    out_ref[...] = (first[:feats] + first[feats:] + second).astype(out_ref.dtype)


def call(kernel, shape, dtype, *operands, flops=0):
    moved = sum(o.size * o.dtype.itemsize for o in operands)
    moved += math.prod(shape) * jnp.dtype(dtype).itemsize
    return pl.pallas_call(
        kernel,
        out_shape=jax.ShapeDtypeStruct(shape, dtype),
        in_specs=[pl.BlockSpec(memory_space=pltpu.VMEM)] * len(operands),
        out_specs=pl.BlockSpec(memory_space=pltpu.VMEM),
        compiler_params=pltpu.CompilerParams(vmem_limit_bytes=VMEM_LIMIT),
        cost_estimate=pl.CostEstimate(flops=flops, bytes_accessed=moved, transcendentals=0),
    )(*operands)


def columns(half, nx):
    return (
        [x for a in range(0, nx, 4) for x in (a, a + 3 - 2 * half)],
        [x for a in range(0, nx, 4) for x in (a + 1 + half, a + 2 + half)],
    )


def exchange_groups(nz, ny, nx, nc):
    def index(z, y, x, c):
        return ((z * ny + y % ny) * nx + x % nx) * nc + c

    far = [
        [index(z, y, x, c) for y in range(yb, ny, 2) for z in range(nz) for x in xs]
        for c in range(nc)
        for yb in range(2)
        for xs in columns(c, nx)
    ]
    near = [
        [
            index(z, y + c + (yb + c) % 2, next(v for v in (x + c, x + c + 1) if v % nx in xs), c)
            for yb in range(2)
            for xs in columns(c, nx)
        ]
        for z in range(nz)
        for c in range(nc)
        for y in range(0, ny, 2)
        for x in range(0, nx, 2)
    ]
    return far, near


def swap(blocks, groups):
    return lax.all_to_all(
        blocks, AXES, split_axis=0, concat_axis=0, axis_index_groups=groups, tiled=True
    )


def other_core(values):
    return lax.ppermute(values, "c", [(0, 1), (1, 0)])


def shards(activations, out_grad, token_scale, route_prob, route_ids, w_gate, w_up, w_down):
    nz, ny, nx, nc = (lax.axis_size(a) for a in AXES)
    far, near = exchange_groups(nz, ny, nx, nc)
    spread = ny * nx // 4
    members = 4
    core = lax.axis_index("c")
    tokens, feats = activations.shape
    capacity = min(tokens, 5 * tokens // (2 * nz))
    parts = feats // FINE
    hidden = w_gate.shape[2]
    rows = nz * capacity
    wide = feats * spread

    heads = [route_ids.T, activations.T, out_grad.T]
    send = pl.pallas_call(
        functools.partial(pack_kernel, capacity),
        out_shape=pltpu.HBM((ny // 2, nz, nx // 2, 2 * FINE, LANES), BF16),
        in_specs=[pl.BlockSpec(memory_space=pl.ANY)] * 3,
        out_specs=pl.BlockSpec(memory_space=pltpu.HBM),
        scratch_shapes=[pltpu.VMEM(h.shape, h.dtype) for h in heads]
        + [pltpu.VMEM((nz, 2 * FINE, LANES), BF16), pltpu.SemaphoreType.DMA((3 + 2 * spread,))],
        compiler_params=pltpu.CompilerParams(vmem_limit_bytes=VMEM_LIMIT),
    )(*(pltpu.with_memory_space_constraint(h, pltpu.HBM) for h in heads))
    got = swap(send.reshape(nz * spread, 2 * FINE, LANES), far)

    views = (ny // 2, 2, nx, nc, parts, FINE, hidden)
    ordered = (members, parts, ny // 2, nx // 2, FINE, hidden)
    gate, up = (
        pltpu.with_memory_space_constraint(w.reshape(views), pltpu.HBM) for w in (w_gate, w_up)
    )
    down = pltpu.with_memory_space_constraint(w_down[0], pltpu.HBM)
    chunks, each = ny // 2, 6 * parts

    def order(kernel, spaces, scratch, *sources):
        ordered_weights = pl.pallas_call(
            kernel,
            out_shape=[space(ordered, BF16) for space in spaces],
            in_specs=[pl.BlockSpec(memory_space=pl.ANY)] * len(sources),
            out_specs=[pl.BlockSpec(memory_space=space) for space in spaces],
            scratch_shapes=scratch,
            compiler_params=pltpu.CompilerParams(vmem_limit_bytes=VMEM_LIMIT),
            cost_estimate=pl.CostEstimate(
                flops=0, bytes_accessed=6 * 1024 * 1024, transcendentals=0
            ),
        )(*sources)
        return [w.reshape(members * wide, hidden) for w in ordered_weights]

    *sent, own_down, own_gate = order(
        sent_kernel,
        [pltpu.VMEM] * 3 + [pltpu.HBM] * 2,
        [
            pltpu.VMEM((chunks, hidden, down.shape[1] // chunks), BF16),
            pltpu.VMEM(views, BF16),
            pltpu.VMEM(ordered, BF16),
            pltpu.SemaphoreType.DMA((chunks + 5 * each + 1,)),
        ],
        gate,
        up,
        down,
    )
    (own_up,) = order(
        own_kernel,
        [pltpu.HBM],
        [pltpu.VMEM(ordered, BF16), pltpu.SemaphoreType.DMA((each + 1,))],
        up,
    )
    own = [own_gate, own_up, own_down]
    other = [other_core(w) for w in sent]
    got, own, other = lax.optimization_barrier((got, own, other))

    copies = call(
        functools.partial(unpack_kernel, capacity, parts),
        (members, 2 * rows, wide),
        BF16,
        got.reshape(ny // 2, nz, nx // 2, 2 * FINE, LANES),
    )
    block = swap(copies, near)

    flops = 2 * rows * members * wide * hidden

    first = call(
        first_kernel, (rows, 5 * hidden), F32, block, *other, own[2], own[0], flops=5 * flops
    )
    got_first = other_core(first)
    second = call(second_kernel, (rows, hidden), F32, block, own[1], flops=flops)
    got_second = other_core(second)
    part = call(
        return_kernel,
        (rows, members * wide),
        F32,
        first,
        second,
        got_first,
        *own[:2],
        flops=2 * flops,
    )
    combine = call(
        functools.partial(combine_kernel, capacity, parts),
        (2, nz * LANES, tokens),
        BF16,
        route_ids.T,
        route_prob.T,
        token_scale.reshape(1, tokens),
    )
    part, combine = lax.optimization_barrier((part, combine))
    part = call(
        return_add_kernel,
        (members, rows, wide),
        BF16,
        first,
        got_first,
        got_second,
        *other[:2],
        part,
        flops=2 * flops,
    )
    part = swap(part, near)
    part = call(
        functools.partial(repack_kernel, capacity, parts),
        (ny // 2, nz, nx // 2, FINE, LANES),
        BF16,
        part,
    )
    part = swap(part.reshape(nz * spread, FINE, LANES), far)
    return call(
        functools.partial(final_kernel, capacity, parts),
        (feats, tokens),
        BF16,
        combine,
        part.reshape(ny // 2, nz, nx // 2, FINE, LANES),
    ).T


def solution(mesh):
    devices = mesh.devices
    fine = Mesh(devices.reshape(devices.shape[0], 8, 4, 2), AXES)
    tensor = ("y", "x", "c")
    placed = (
        P("z", tensor),
        P("z", tensor),
        P("z"),
        P("z", None),
        P("z", None),
        P("z", None, tensor),
        P("z", None, tensor),
        P("z", tensor, None),
    )
    return jax.shard_map(
        shards, mesh=fine, in_specs=placed, out_specs=P("z", tensor), check_vma=False
    )
```
